32 devices in a mesh: groups: 2 (over y), row: 4 (over x, core), col: 4 (over z).
Axes of the slice: x: 2, y: 2, z: 4, core: 2. Of those that a mesh axis runs over, the one named last changes fastest.
Arguments:
- pair_act: bfloat16 [768, 384, 128], P(('groups', 'row'), 'col'), parts along dimension 0, may hold values from -6 to 6
- pair_mask: int32 [768, 384], P(('groups', 'row'), 'col'), parts along dimension 0, may hold values 0 or 1
- input_gain: float32 [2, 128], replicated, may hold values from 0.5 to 1.5
- input_bias: float32 [2, 128], replicated, may hold values from -3 to 3
- project_weight: bfloat16 [2, 128, 512], replicated, may hold values from -0.5 to 0.5
- gate_weight: bfloat16 [2, 128, 128], replicated, may hold values from -0.5 to 0.5
- output_gain: float32 [2, 128], replicated, may hold values from 0.5 to 1.5
- output_bias: float32 [2, 128], replicated, may hold values from -3 to 3
- output_weight: bfloat16 [2, 128, 128], replicated, may hold values from -0.5 to 0.5
Outputs:
- updated_pair: bfloat16 [768, 384, 128], P(('groups', 'row'), 'col'), parts along dimension 0
The draws below stay inside these ranges and needn't reach their ends.
There are 2 independent parts, one for each index of `groups`. The reference program is written for one: setup_inputs(seed, part) draws one part's arguments, and reference() takes and returns one part's arrays. A program takes and returns all parts, laid end to end along the dimension named above; an argument that names none is the same for every part. Nothing has to cross between parts.
Inputs may be any that keep to these rules, and one draw needn't show every extreme that they name: `pair_mask`: 1 marks a valid residue pair.
All inputs are finite; a program needn't handle non-finite values. No bound on the sum of `pair_mask` on one device may be relied on, other than what follows from the above.
Results may differ from the reference program's by a relative error of at most 0.0075.
Values may be sent and summed in bfloat16 or wider, within the bound.
No kernel may reach another device: no remote copies, remote signals or barrier semaphores. Data moves between devices by JAX's collectives and lax.ppermute only.
A program may use at most 128 MiB of HBM per device.

```python
import jax
import jax.numpy as jnp
from jax import lax

RESIDUES = 384
CHANNELS = 128
HIDDEN_SIZE = 128


def place_ends(values, rng, least, largest):
    dims = values.shape
    spot = [jax.random.randint(jax.random.fold_in(rng, axis), (), 0, dims[axis]) for axis in range(len(dims))]
    values = values.at[tuple(spot)].set(least)
    longest = dims.index(max(dims))
    spot[longest] = (spot[longest] + 1) % dims[longest]
    return values.at[tuple(spot)].set(largest)


def level_of(stream_key, extent, shards, smallest, top_value):
    level = 1.0
    for dim, shards_of in shards:
        steps = jax.random.uniform(jax.random.fold_in(jax.random.fold_in(stream_key, 6), dim), (shards_of,), jnp.float32, smallest / len(shards), top_value / len(shards))
        level = level * jnp.repeat(jnp.exp(steps), extent[dim] // shards_of).reshape((-1,) + (1,) * (len(extent) - 1 - dim))
    return level


def normal_values(own_key, dims, width, limit, cuts=(), dtype=jnp.bfloat16):
    entries = width * jax.random.normal(own_key, dims, jnp.float32)
    if cuts:
        entries = entries * level_of(own_key, dims, cuts, -0.22, 0.18)
    return jnp.clip(entries, -limit, limit).astype(dtype)


def setup_inputs(seed: int = 0, part: int = 0) -> dict:
    keys = jax.random.split(jax.random.key(seed), 10)
    part_splits = jax.random.split(jax.random.fold_in(keys[9], part), 10)
    pair_act = normal_values(part_splits[0], (RESIDUES, RESIDUES, CHANNELS), 1.0, 6.0, ((0, 4), (1, 4)))
    pair_mask = place_ends((jax.random.randint(part_splits[1], (RESIDUES, RESIDUES), 0, 8) < 7).astype(jnp.int32), jax.random.fold_in(part_splits[1], 1), 0, 1)
    input_gain = jnp.clip(1.0 + 0.1 * jax.random.normal(keys[2], (2, CHANNELS), jnp.float32), 0.5, 1.5)
    input_bias = normal_values(keys[3], (2, CHANNELS), 0.5, 3.0, (), jnp.float32)
    project_weight = normal_values(keys[4], (2, CHANNELS, 4 * HIDDEN_SIZE), CHANNELS ** -0.5, 0.5)
    gate_weight = normal_values(keys[5], (2, CHANNELS, CHANNELS), CHANNELS ** -0.5, 0.5)
    output_gain = jnp.clip(1.0 + 0.1 * jax.random.normal(keys[6], (2, HIDDEN_SIZE), jnp.float32), 0.5, 1.5)
    output_bias = normal_values(keys[7], (2, HIDDEN_SIZE), 0.5, 3.0, (), jnp.float32)
    output_weight = normal_values(keys[8], (2, HIDDEN_SIZE, CHANNELS), HIDDEN_SIZE ** -0.5, 0.5)
    return dict(pair_act=pair_act, pair_mask=pair_mask, input_gain=input_gain, input_bias=input_bias, project_weight=project_weight, gate_weight=gate_weight, output_gain=output_gain, output_bias=output_bias, output_weight=output_weight)


def layer_norm(values, gain, bias):
    average = lax.optimization_barrier(jnp.mean(values, axis=-1, keepdims=True))
    centred = values - average
    spread_sq = lax.optimization_barrier(jnp.mean(centred * centred, axis=-1, keepdims=True))
    return centred * lax.rsqrt(spread_sq + 1e-05) * gain + bias

def triangle_update(pair_act, mask_float, layer_index, input_gain, input_bias, project_weight, gate_weight, output_gain, output_bias, output_weight, incoming):
    pair_float = pair_act.astype(jnp.float32)
    normed = layer_norm(pair_float, input_gain[layer_index], input_bias[layer_index]).astype(jnp.bfloat16)
    flattened = normed.reshape(-1, CHANNELS)
    projected = jnp.dot(flattened, project_weight[layer_index], preferred_element_type=jnp.float32)
    projected = projected.reshape(RESIDUES, RESIDUES, 4 * HIDDEN_SIZE)
    left_proj = jax.nn.sigmoid(projected[..., :HIDDEN_SIZE]) * projected[..., HIDDEN_SIZE:2 * HIDDEN_SIZE] * mask_float
    right_proj = jax.nn.sigmoid(projected[..., 2 * HIDDEN_SIZE:3 * HIDDEN_SIZE]) * projected[..., 3 * HIDDEN_SIZE:] * mask_float
    left_proj = left_proj.astype(jnp.bfloat16).astype(jnp.float32)
    right_proj = right_proj.astype(jnp.bfloat16).astype(jnp.float32)
    gate_value = jax.nn.sigmoid(jnp.dot(flattened, gate_weight[layer_index], preferred_element_type=jnp.float32))
    gate_value = gate_value.reshape(RESIDUES, RESIDUES, CHANNELS)
    if incoming:
        triangle = jnp.einsum('kic,kjc->ijc', left_proj, right_proj)
    else:
        triangle = jnp.einsum('ikc,jkc->ijc', left_proj, right_proj)
    normed_sum = layer_norm(triangle, output_gain[layer_index], output_bias[layer_index]).astype(jnp.bfloat16)
    mapped = jnp.dot(normed_sum.reshape(-1, HIDDEN_SIZE), output_weight[layer_index], preferred_element_type=jnp.float32)
    mapped = mapped.reshape(RESIDUES, RESIDUES, CHANNELS)
    return (pair_float + gate_value * mapped).astype(jnp.bfloat16)

def reference(pair_act, pair_mask, input_gain, input_bias, project_weight, gate_weight, output_gain, output_bias, output_weight):
    mask_float = pair_mask.astype(jnp.float32)[..., None]
    after_outgoing = triangle_update(pair_act, mask_float, 0, input_gain, input_bias, project_weight, gate_weight, output_gain, output_bias, output_weight, False)
    return triangle_update(after_outgoing, mask_float, 1, input_gain, input_bias, project_weight, gate_weight, output_gain, output_bias, output_weight, True)
```

```python
import jax
import jax.numpy as jnp
from jax import lax
from jax.sharding import PartitionSpec as P

GRID = ("row", "col")


def layer_norm(values, gain, bias, axis):
    average = jnp.mean(values, axis=axis, keepdims=True)
    centred = values - average
    spread_sq = jnp.mean(centred * centred, axis=axis, keepdims=True)
    return centred * lax.rsqrt(spread_sq + 1e-05) * gain + bias


def triangle_update(
    pair_act,
    mask_float,
    layer_index,
    input_gain,
    input_bias,
    project_weight,
    gate_weight,
    output_gain,
    output_bias,
    output_weight,
    incoming,
):
    rows, cols = lax.axis_size("row"), lax.axis_size("col")
    peers = rows * cols
    rows_here, cols_here, channels_here = pair_act.shape
    width = output_weight.shape[1]
    own = width // peers
    pixels = rows_here * cols_here
    pair_float = pair_act.astype(jnp.float32).reshape(pixels, channels_here)
    normed = layer_norm(
        pair_float, input_gain[layer_index], input_bias[layer_index], -1
    ).astype(jnp.bfloat16)
    projected = lax.dot_general(
        project_weight[layer_index],
        normed,
        (((0,), (1,)), ((), ())),
        preferred_element_type=jnp.float32,
    ).reshape(4, peers, own, pixels)
    mask_row = mask_float.reshape(1, 1, pixels)
    left_proj = (jax.nn.sigmoid(projected[0]) * projected[1] * mask_row).astype(jnp.bfloat16)
    right_proj = (jax.nn.sigmoid(projected[2]) * projected[3] * mask_row).astype(jnp.bfloat16)
    both = jnp.concatenate([left_proj, right_proj], axis=1)
    both = lax.all_to_all(both, GRID, 0, 0)
    both = both.reshape(rows, cols, 2, own, rows_here, cols_here)
    both = both.transpose(2, 3, 0, 4, 1, 5).reshape(2, own, rows * rows_here, cols * cols_here)
    spec = "cki,ckj->cij" if incoming else "cik,cjk->cij"
    triangle = jnp.einsum(spec, both[0], both[1], preferred_element_type=jnp.float32)
    triangle = triangle.astype(jnp.bfloat16).reshape(own, rows, rows_here, cols, cols_here)
    triangle = triangle.transpose(1, 3, 0, 2, 4).reshape(peers, own, pixels)
    triangle = lax.all_to_all(triangle, GRID, 0, 0).reshape(width, pixels)
    normed_sum = layer_norm(
        triangle.astype(jnp.float32),
        output_gain[layer_index][:, None],
        output_bias[layer_index][:, None],
        0,
    ).astype(jnp.bfloat16)
    gate_value = jax.nn.sigmoid(
        jnp.dot(normed, gate_weight[layer_index], preferred_element_type=jnp.float32)
    )
    mapped = lax.dot_general(
        normed_sum,
        output_weight[layer_index],
        (((0,), (0,)), ((), ())),
        preferred_element_type=jnp.float32,
    )
    return (
        (pair_float + gate_value * mapped)
        .astype(jnp.bfloat16)
        .reshape(rows_here, cols_here, channels_here)
    )


def shards(pair_act, pair_mask, *params):
    mask_float = pair_mask.astype(jnp.float32)
    for index in range(2):
        pair_act = triangle_update(pair_act, mask_float, index, *params, index == 1)
    return pair_act


def solution(mesh):
    return jax.shard_map(
        shards,
        mesh=mesh,
        in_specs=(P(("groups", "row"), "col", None), P(("groups", "row"), "col"))
        + (P(),) * 7,
        out_specs=P(("groups", "row"), "col", None),
        check_vma=False,
    )
```

```python
import functools

import jax
import jax.numpy as jnp
from jax import lax
from jax.experimental import pallas as pl
from jax.experimental.pallas import tpu as pltpu
from jax.sharding import PartitionSpec as P

GRID = ("row", "col")
LANES = 128


def logistic(values):
    return 0.5 * jnp.tanh(0.5 * values) + 0.5


def channel_norm(values, gain, bias):
    average = jnp.mean(values, axis=0, keepdims=True)
    centred = values - average
    spread_sq = jnp.mean(centred * centred, axis=0, keepdims=True)
    return centred * lax.rsqrt(spread_sq + 1e-05) * gain + bias


def dot(left, right):
    return jnp.dot(left, right, preferred_element_type=jnp.float32)


def emit_projections(peers, zt, mask, gain, bias, weight_t, lr_ref):
    width = weight_t.shape[0] // 4
    own = width // peers
    normed = channel_norm(zt, gain, bias).astype(jnp.bfloat16)
    projected = dot(weight_t, normed)
    tile = projected.shape[1]
    left = logistic(projected[:width]) * projected[width : 2 * width] * mask
    right = logistic(projected[2 * width : 3 * width]) * projected[3 * width :] * mask
    both = jnp.concatenate(
        [left.reshape(peers, own, tile), right.reshape(peers, own, tile)], axis=1
    )
    lr_ref[...] = both.reshape(2 * width, tile).astype(jnp.bfloat16)


def first_kernel(peers, z_ref, mask_ref, gain_ref, bias_ref, weight_ref, lr_ref, zt_ref):
    zt = z_ref[...].astype(jnp.float32).T
    zt_ref[...] = zt.astype(jnp.bfloat16)
    emit_projections(
        peers, zt, mask_ref[...], gain_ref[...], bias_ref[...], weight_ref[...], lr_ref
    )


def gate_kernel(zt_ref, gain_ref, bias_ref, weight_ref, gate_ref):
    normed = channel_norm(
        zt_ref[...].astype(jnp.float32), gain_ref[...], bias_ref[...]
    ).astype(jnp.bfloat16)
    gate_ref[...] = logistic(dot(weight_ref[...], normed)).astype(jnp.bfloat16)


def updated(t_ref, zt_ref, gate_ref, ogain_ref, obias_ref, oweight_ref):
    normed_sum = channel_norm(
        t_ref[...].astype(jnp.float32), ogain_ref[...], obias_ref[...]
    ).astype(jnp.bfloat16)
    mapped = dot(oweight_ref[...], normed_sum)
    return zt_ref[...].astype(jnp.float32) + gate_ref[...].astype(jnp.float32) * mapped


def middle_kernel(
    peers, t_ref, zt_ref, gate_ref, ogain_ref, obias_ref, oweight_ref,
    mask_ref, gain_ref, bias_ref, weight_ref, lr_ref, out_ref,
):
    fresh = updated(t_ref, zt_ref, gate_ref, ogain_ref, obias_ref, oweight_ref).astype(jnp.bfloat16)
    out_ref[...] = fresh
    emit_projections(
        peers, fresh.astype(jnp.float32), mask_ref[...], gain_ref[...], bias_ref[...],
        weight_ref[...], lr_ref,
    )


def last_kernel(t_ref, zt_ref, gate_ref, ogain_ref, obias_ref, oweight_ref, out_ref):
    fresh = updated(t_ref, zt_ref, gate_ref, ogain_ref, obias_ref, oweight_ref)
    out_ref[...] = fresh.T.astype(jnp.bfloat16)


def triangle_kernel(
    blocks, side, own, incoming, x_ref, y_ref, left_ref, right_ref, rows_ref, tiles_ref
):
    step = pl.program_id(0)
    pair = 2 * own
    span = 4 * side
    lane = lax.broadcasted_iota(jnp.int32, (pair, LANES), 1)
    inside = lane < side

    @pl.when(step < blocks)
    def _unpack():
        for col in range(blocks):

            def split(group, carry, col=col):
                x = x_ref[
                    pl.ds(col * pair, pair), pl.ds(pl.multiple_of(group * span, LANES), span)
                ].astype(jnp.float32)
                a, b, c = x[:, :LANES], x[:, LANES : 2 * LANES], x[:, 2 * LANES :]
                picked = (
                    a,
                    pltpu.roll(jnp.where(lane >= 96, a, b), 32, 1),
                    pltpu.roll(jnp.where(lane >= 64, b, c), 64, 1),
                    pltpu.roll(c, 96, 1),
                )
                for k, row in enumerate(picked):
                    rows_ref[
                        pl.ds(pl.multiple_of((group * 4 + k) * pair, pair), pair), :
                    ] = jnp.where(inside, row, 0.0)
                return carry

            lax.fori_loop(0, side // 4, split, 0, unroll=4)
            at = pl.multiple_of(step * side, 16)
            at_right = at if incoming else pl.multiple_of(step * LANES, 16)
            for ch in range(own):
                left_ref[ch, pl.ds(at, side), col * LANES : (col + 1) * LANES] = rows_ref[
                    pl.ds(ch, side, stride=pair), :
                ].astype(jnp.bfloat16)
                right_ref[ch, pl.ds(at_right, side), col * LANES : (col + 1) * LANES] = rows_ref[
                    pl.ds(own + ch, side, stride=pair), :
                ].astype(jnp.bfloat16)

    @pl.when(step >= blocks)
    def _multiply():
        block = step - blocks
        for ch in range(own):
            if incoming:
                left = left_ref[ch, :, pl.ds(pl.multiple_of(block * LANES, LANES), LANES)]
                product = lax.dot_general(
                    left, right_ref[ch], (((0,), (0,)), ((), ())), preferred_element_type=jnp.float32
                )[:side]
            else:
                left = left_ref[ch, pl.ds(pl.multiple_of(block * side, 16), side), :]
                product = lax.dot_general(
                    left, right_ref[ch], (((1,), (1,)), ((), ())), preferred_element_type=jnp.float32
                )
            for col in range(blocks):
                tiles_ref[
                    pl.ds((col // 2) * side * pair + (col % 2) * own + ch, side, stride=pair), :
                ] = product[:, col * LANES : (col + 1) * LANES]
        for half in range(blocks // 2):

            def join(group, carry, half=half):
                p, q, r, s = (
                    tiles_ref[
                        pl.ds(
                            pl.multiple_of(half * side * pair + (group * 4 + k) * pair, pair), pair
                        ),
                        :,
                    ]
                    for k in range(4)
                )
                q, r, s = pltpu.roll(q, 96, 1), pltpu.roll(r, 64, 1), pltpu.roll(s, 32, 1)
                flat = jnp.concatenate(
                    [
                        jnp.where(inside, p, q),
                        jnp.where(lane < 64, q, r),
                        jnp.where(lane < 32, r, s),
                    ],
                    axis=1,
                )
                y_ref[
                    pl.ds(half * pair, pair), pl.ds(pl.multiple_of(group * span, LANES), span)
                ] = flat.astype(jnp.bfloat16)
                return carry

            lax.fori_loop(0, side // 4, join, 0, unroll=4)


def fits(rows, cols, rows_here, cols_here, width):
    return (
        rows == cols
        and rows % 2 == 0
        and rows_here == cols_here
        and 4 * cols_here == 3 * LANES
        and 16 * rows * cols == 2 * width
    )


def whole_spec(array):
    return pl.BlockSpec(array.shape, lambda i: (0,) * array.ndim)


def triangle_call(received, blocks, side, own, incoming):
    pair = 2 * own
    pixels = side * side
    padded = blocks * LANES
    left_rows = blocks * side
    right_rows = left_rows if incoming else padded
    return pl.pallas_call(
        functools.partial(triangle_kernel, blocks, side, own, incoming),
        grid=(2 * blocks,),
        in_specs=[
            pl.BlockSpec((blocks * pair, pixels), lambda i: (jnp.minimum(i, blocks - 1), 0))
        ],
        out_specs=pl.BlockSpec((blocks * own, pixels), lambda i: (jnp.maximum(i - blocks, 0), 0)),
        out_shape=jax.ShapeDtypeStruct((blocks * blocks * own, pixels), jnp.bfloat16),
        scratch_shapes=[
            pltpu.VMEM((own, left_rows, padded), jnp.bfloat16),
            pltpu.VMEM((own, right_rows, padded), jnp.bfloat16),
            pltpu.VMEM((side * pair, LANES), jnp.float32),
            pltpu.VMEM((blocks // 2 * side * pair, LANES), jnp.float32),
        ],
        compiler_params=pltpu.CompilerParams(vmem_limit_bytes=48 * 1024 * 1024),
        cost_estimate=pl.CostEstimate(
            flops=2 * own * (blocks * side) ** 3, bytes_accessed=6 * received.size, transcendentals=0
        ),
    )(received)


def pixel_call(body, tiled, fixed, outs, pixels, tile, flops, row_major_in=(), row_major_out=()):
    def spec(channels, row_major):
        if row_major:
            return pl.BlockSpec((tile, channels), lambda i: (i, 0))
        return pl.BlockSpec((channels, tile), lambda i: (0, i))

    in_specs = [
        spec(a.shape[1] if k in row_major_in else a.shape[0], k in row_major_in)
        for k, a in enumerate(tiled)
    ] + [whole_spec(a) for a in fixed]
    out_specs = [spec(ch, k in row_major_out) for k, ch in enumerate(outs)]
    out_shape = [
        jax.ShapeDtypeStruct((pixels, ch) if k in row_major_out else (ch, pixels), jnp.bfloat16)
        for k, ch in enumerate(outs)
    ]
    return pl.pallas_call(
        body,
        grid=(pixels // tile,),
        in_specs=in_specs,
        out_specs=out_specs,
        out_shape=out_shape,
        compiler_params=pltpu.CompilerParams(vmem_limit_bytes=48 * 1024 * 1024),
        cost_estimate=pl.CostEstimate(
            flops=flops, bytes_accessed=2 * pixels * (sum(outs) + 256), transcendentals=0
        ),
    )(*tiled, *fixed)


def by_kernels(
    pair_act,
    mask_float,
    input_gain,
    input_bias,
    project_weight,
    gate_weight,
    output_gain,
    output_bias,
    output_weight,
):
    rows, cols = lax.axis_size("row"), lax.axis_size("col")
    peers = rows * cols
    side, _, channels = pair_act.shape
    width = output_weight.shape[1]
    own = width // peers
    pixels = side * side
    tile = 9 * LANES
    mask = mask_float.reshape(1, pixels)
    column = [a[:, :, None] for a in (input_gain, input_bias, output_gain, output_bias)]
    project_t, gate_t, output_t = (
        a.transpose(0, 2, 1) for a in (project_weight, gate_weight, output_weight)
    )
    arriving = lambda u: (column[0][u], column[1][u], project_t[u])
    leaving = lambda u: (column[2][u], column[3][u], output_t[u])
    mult = 2 * pixels * channels

    def gate_of(zt, u):
        return pixel_call(
            gate_kernel, (zt,), (column[0][u], column[1][u], gate_t[u]), (channels,),
            pixels, tile, mult * channels,
        )[0]

    def triangle_of(sent, incoming):
        received = lax.all_to_all(sent.reshape(peers, 2 * own, pixels), GRID, 0, 0)
        product = triangle_call(
            received.reshape(2 * width, pixels), rows, side, own, incoming
        )
        return lax.all_to_all(product.reshape(peers, own, pixels), GRID, 0, 0).reshape(width, pixels)

    sent, zt = pixel_call(
        functools.partial(first_kernel, peers),
        (pair_act.reshape(pixels, channels), mask), arriving(0), (2 * width, channels),
        pixels, tile, mult * 4 * width, row_major_in=(0,),
    )
    gate = gate_of(zt, 0)
    triangle = triangle_of(sent, False)

    def middle(t, z, g, m, og, ob, ow, ig, ib, pw, lr, out):
        middle_kernel(peers, t, z, g, og, ob, ow, m, ig, ib, pw, lr, out)

    sent, zt = pixel_call(
        middle, (triangle, zt, gate, mask), leaving(0) + arriving(1), (2 * width, channels),
        pixels, tile, mult * 5 * width,
    )
    gate = gate_of(zt, 1)
    triangle = triangle_of(sent, True)
    return pixel_call(
        last_kernel, (triangle, zt, gate), leaving(1), (channels,),
        pixels, tile, mult * channels, row_major_out=(0,),
    )[0].reshape(side, side, channels)


def layer_norm(values, gain, bias, axis):
    average = jnp.mean(values, axis=axis, keepdims=True)
    centred = values - average
    spread_sq = jnp.mean(centred * centred, axis=axis, keepdims=True)
    return centred * lax.rsqrt(spread_sq + 1e-05) * gain + bias


def triangle_update(
    pair_act,
    mask_float,
    layer_index,
    input_gain,
    input_bias,
    project_weight,
    gate_weight,
    output_gain,
    output_bias,
    output_weight,
    incoming,
):
    rows, cols = lax.axis_size("row"), lax.axis_size("col")
    peers = rows * cols
    rows_here, cols_here, channels_here = pair_act.shape
    width = output_weight.shape[1]
    own = width // peers
    pixels = rows_here * cols_here
    pair_float = pair_act.astype(jnp.float32).reshape(pixels, channels_here)
    normed = layer_norm(
        pair_float, input_gain[layer_index], input_bias[layer_index], -1
    ).astype(jnp.bfloat16)
    projected = lax.dot_general(
        project_weight[layer_index],
        normed,
        (((0,), (1,)), ((), ())),
        preferred_element_type=jnp.float32,
    ).reshape(4, peers, own, pixels)
    mask_row = mask_float.reshape(1, 1, pixels)
    left_proj = (jax.nn.sigmoid(projected[0]) * projected[1] * mask_row).astype(jnp.bfloat16)
    right_proj = (jax.nn.sigmoid(projected[2]) * projected[3] * mask_row).astype(jnp.bfloat16)
    both = jnp.concatenate([left_proj, right_proj], axis=1)
    both = lax.all_to_all(both, GRID, 0, 0)
    both = both.reshape(rows, cols, 2, own, rows_here, cols_here)
    both = both.transpose(2, 3, 0, 4, 1, 5).reshape(2, own, rows * rows_here, cols * cols_here)
    spec = "cki,ckj->cij" if incoming else "cik,cjk->cij"
    triangle = jnp.einsum(spec, both[0], both[1], preferred_element_type=jnp.float32)
    triangle = triangle.astype(jnp.bfloat16).reshape(own, rows, rows_here, cols, cols_here)
    triangle = triangle.transpose(1, 3, 0, 2, 4).reshape(peers, own, pixels)
    triangle = lax.all_to_all(triangle, GRID, 0, 0).reshape(width, pixels)
    normed_sum = layer_norm(
        triangle.astype(jnp.float32),
        output_gain[layer_index][:, None],
        output_bias[layer_index][:, None],
        0,
    ).astype(jnp.bfloat16)
    gate_value = jax.nn.sigmoid(
        jnp.dot(normed, gate_weight[layer_index], preferred_element_type=jnp.float32)
    )
    mapped = lax.dot_general(
        normed_sum,
        output_weight[layer_index],
        (((0,), (0,)), ((), ())),
        preferred_element_type=jnp.float32,
    )
    return (
        (pair_float + gate_value * mapped)
        .astype(jnp.bfloat16)
        .reshape(rows_here, cols_here, channels_here)
    )


def shards(pair_act, pair_mask, *params):
    mask_float = pair_mask.astype(jnp.float32)
    rows, cols = lax.axis_size("row"), lax.axis_size("col")
    if fits(rows, cols, *pair_act.shape[:2], params[-1].shape[1]):
        return by_kernels(pair_act, mask_float, *params)
    for index in range(2):
        pair_act = triangle_update(pair_act, mask_float, index, *params, index == 1)
    return pair_act


def solution(mesh):
    return jax.shard_map(
        shards,
        mesh=mesh,
        in_specs=(P(("groups", "row"), "col", None), P(("groups", "row"), "col"))
        + (P(),) * 7,
        out_specs=P(("groups", "row"), "col", None),
        check_vma=False,
    )
```

```python
import functools

import jax
import jax.numpy as jnp
from jax import lax
from jax.experimental import pallas as pl
from jax.experimental.pallas import tpu as pltpu
from jax.sharding import PartitionSpec as P

GRID = ("row", "col")
LANES = 128


def logistic(values):
    return 0.5 * jnp.tanh(0.5 * values) + 0.5


def channel_norm(values, gain, bias):
    average = jnp.mean(values, axis=0, keepdims=True)
    centred = values - average
    spread_sq = jnp.mean(centred * centred, axis=0, keepdims=True)
    return centred * lax.rsqrt(spread_sq + 1e-05) * gain + bias


def dot(left, right):
    return jnp.dot(left, right, preferred_element_type=jnp.float32)


def emit_projections(peers, zt, mask, gain, bias, weight_t, lr_ref):
    width = weight_t.shape[0] // 4
    own = width // peers
    normed = channel_norm(zt, gain, bias).astype(jnp.bfloat16)
    projected = dot(weight_t, normed)
    tile = projected.shape[1]
    left = logistic(projected[:width]) * projected[width : 2 * width] * mask
    right = logistic(projected[2 * width : 3 * width]) * projected[3 * width :] * mask
    both = jnp.concatenate(
        [left.reshape(peers, own, tile), right.reshape(peers, own, tile)], axis=1
    )
    lr_ref[...] = both.reshape(2 * width, tile).astype(jnp.bfloat16)


def first_kernel(peers, z_ref, mask_ref, gain_ref, bias_ref, weight_ref, lr_ref, zt_ref):
    zt = z_ref[...].astype(jnp.float32).T
    zt_ref[...] = zt.astype(jnp.bfloat16)
    emit_projections(
        peers, zt, mask_ref[...], gain_ref[...], bias_ref[...], weight_ref[...], lr_ref
    )


def gate_kernel(zt_ref, gain_ref, bias_ref, weight_ref, gate_ref):
    normed = channel_norm(
        zt_ref[...].astype(jnp.float32), gain_ref[...], bias_ref[...]
    ).astype(jnp.bfloat16)
    gate_ref[...] = logistic(dot(weight_ref[...], normed)).astype(jnp.bfloat16)


def updated(t_ref, zt_ref, gate_ref, ogain_ref, obias_ref, oweight_ref):
    normed_sum = channel_norm(
        t_ref[...].astype(jnp.float32), ogain_ref[...], obias_ref[...]
    ).astype(jnp.bfloat16)
    mapped = dot(oweight_ref[...], normed_sum)
    return zt_ref[...].astype(jnp.float32) + gate_ref[...].astype(jnp.float32) * mapped


def middle_kernel(
    peers, t_ref, zt_ref, gate_ref, ogain_ref, obias_ref, oweight_ref,
    mask_ref, gain_ref, bias_ref, weight_ref, lr_ref, out_ref,
):
    fresh = updated(t_ref, zt_ref, gate_ref, ogain_ref, obias_ref, oweight_ref).astype(jnp.bfloat16)
    out_ref[...] = fresh
    emit_projections(
        peers, fresh.astype(jnp.float32), mask_ref[...], gain_ref[...], bias_ref[...],
        weight_ref[...], lr_ref,
    )


def last_kernel(t_ref, zt_ref, gate_ref, ogain_ref, obias_ref, oweight_ref, out_ref):
    fresh = updated(t_ref, zt_ref, gate_ref, ogain_ref, obias_ref, oweight_ref)
    out_ref[...] = fresh.T.astype(jnp.bfloat16)


def triangle_kernel(
    blocks, side, own, incoming, x_ref, y_ref, left_ref, right_ref, rows_ref, tiles_ref
):
    step = pl.program_id(0)
    pair = 2 * own
    span = 4 * side
    pitch_rows = pair + 1
    lane = lax.broadcasted_iota(jnp.int32, (pair, LANES), 1)
    inside = lane < side

    @pl.when(step < blocks)
    def _unpack():
        for col in range(blocks):

            def split(group, carry, col=col):
                x = x_ref[
                    pl.ds(col * pair, pair), pl.ds(pl.multiple_of(group * span, LANES), span)
                ].astype(jnp.float32)
                a, b, c = x[:, :LANES], x[:, LANES : 2 * LANES], x[:, 2 * LANES :]
                picked = (
                    a,
                    pltpu.roll(jnp.where(lane >= 96, a, b), 32, 1),
                    pltpu.roll(jnp.where(lane >= 64, b, c), 64, 1),
                    pltpu.roll(c, 96, 1),
                )
                for k, row in enumerate(picked):
                    rows_ref[
                        pl.ds((group * 4 + k) * pitch_rows, pair), :
                    ] = jnp.where(inside, row, 0.0)
                return carry

            lax.fori_loop(0, side // 4, split, 0, unroll=24)
            at = pl.multiple_of(step * side, 16)
            at_right = at if incoming else pl.multiple_of(step * LANES, 16)
            for ch in range(own):
                left_ref[ch, pl.ds(at, side), col * LANES : (col + 1) * LANES] = rows_ref[
                    pl.ds(ch, side, stride=pitch_rows), :
                ].astype(jnp.bfloat16)
                right_ref[ch, pl.ds(at_right, side), col * LANES : (col + 1) * LANES] = rows_ref[
                    pl.ds(own + ch, side, stride=pitch_rows), :
                ].astype(jnp.bfloat16)

    @pl.when(step == blocks - 1)
    def _multiply():
        contract = ((0,), (0,)) if incoming else ((1,), (1,))
        for ch in range(own):
            product = lax.dot_general(
                left_ref[ch], right_ref[ch], (contract, ((), ())), preferred_element_type=jnp.float32
            )
            pitch = LANES if incoming else side
            for row in range(blocks):
                for col in range(blocks):
                    tiles_ref[
                        row,
                        pl.ds((col // 2) * side * pitch_rows + (col % 2) * own + ch, side, stride=pitch_rows),
                        :,
                    ] = product[
                        row * pitch : row * pitch + side, col * LANES : (col + 1) * LANES
                    ]

    @pl.when(step >= blocks)
    def _repack():
        block = step - blocks
        for half in range(blocks // 2):

            def join(group, carry, half=half):
                p, q, r, s = (
                    tiles_ref[
                        block,
                        pl.ds(
                            half * side * pitch_rows + (group * 4 + k) * pitch_rows, pair
                        ),
                        :,
                    ]
                    for k in range(4)
                )
                q, r, s = pltpu.roll(q, 96, 1), pltpu.roll(r, 64, 1), pltpu.roll(s, 32, 1)
                flat = jnp.concatenate(
                    [
                        jnp.where(inside, p, q),
                        jnp.where(lane < 64, q, r),
                        jnp.where(lane < 32, r, s),
                    ],
                    axis=1,
                )
                y_ref[
                    pl.ds(half * pair, pair), pl.ds(pl.multiple_of(group * span, LANES), span)
                ] = flat.astype(jnp.bfloat16)
                return carry

            lax.fori_loop(0, side // 4, join, 0, unroll=24)


def fits(rows, cols, rows_here, cols_here, width):
    return (
        rows == cols
        and rows % 2 == 0
        and rows_here == cols_here
        and 4 * cols_here == 3 * LANES
        and 16 * rows * cols == 2 * width
    )


def whole_spec(array):
    return pl.BlockSpec(array.shape, lambda i: (0,) * array.ndim)


def triangle_call(received, blocks, side, own, incoming):
    pair = 2 * own
    pixels = side * side
    padded = blocks * LANES
    left_rows = blocks * side
    right_rows = left_rows if incoming else padded
    return pl.pallas_call(
        functools.partial(triangle_kernel, blocks, side, own, incoming),
        grid=(2 * blocks,),
        in_specs=[
            pl.BlockSpec((blocks * pair, pixels), lambda i: (jnp.minimum(i, blocks - 1), 0))
        ],
        out_specs=pl.BlockSpec((blocks * own, pixels), lambda i: (jnp.maximum(i - blocks, 0), 0)),
        out_shape=jax.ShapeDtypeStruct((blocks * blocks * own, pixels), jnp.bfloat16),
        scratch_shapes=[
            pltpu.VMEM((own, left_rows, padded), jnp.bfloat16),
            pltpu.VMEM((own, right_rows, padded), jnp.bfloat16),
            pltpu.VMEM((side * (pair + 1), LANES), jnp.float32),
            pltpu.VMEM((blocks, blocks // 2 * side * (pair + 1), LANES), jnp.float32),
        ],
        compiler_params=pltpu.CompilerParams(vmem_limit_bytes=48 * 1024 * 1024),
        cost_estimate=pl.CostEstimate(
            flops=2 * own * (blocks * side) ** 3, bytes_accessed=6 * received.size, transcendentals=0
        ),
    )(received)


def pixel_call(body, tiled, fixed, outs, pixels, tile, flops, row_major_in=(), row_major_out=()):
    def spec(channels, row_major):
        if row_major:
            return pl.BlockSpec((tile, channels), lambda i: (i, 0))
        return pl.BlockSpec((channels, tile), lambda i: (0, i))

    in_specs = [
        spec(a.shape[1] if k in row_major_in else a.shape[0], k in row_major_in)
        for k, a in enumerate(tiled)
    ] + [whole_spec(a) for a in fixed]
    out_specs = [spec(ch, k in row_major_out) for k, ch in enumerate(outs)]
    out_shape = [
        jax.ShapeDtypeStruct((pixels, ch) if k in row_major_out else (ch, pixels), jnp.bfloat16)
        for k, ch in enumerate(outs)
    ]
    return pl.pallas_call(
        body,
        grid=(pixels // tile,),
        in_specs=in_specs,
        out_specs=out_specs,
        out_shape=out_shape,
        compiler_params=pltpu.CompilerParams(vmem_limit_bytes=48 * 1024 * 1024),
        cost_estimate=pl.CostEstimate(
            flops=flops, bytes_accessed=2 * pixels * (sum(outs) + 256), transcendentals=0
        ),
    )(*tiled, *fixed)


def by_kernels(
    pair_act,
    mask_float,
    input_gain,
    input_bias,
    project_weight,
    gate_weight,
    output_gain,
    output_bias,
    output_weight,
):
    rows, cols = lax.axis_size("row"), lax.axis_size("col")
    peers = rows * cols
    side, _, channels = pair_act.shape
    width = output_weight.shape[1]
    own = width // peers
    pixels = side * side
    tile = 9 * LANES
    mask = mask_float.reshape(1, pixels)
    column = [a[:, :, None] for a in (input_gain, input_bias, output_gain, output_bias)]
    project_t, gate_t, output_t = (
        a.transpose(0, 2, 1) for a in (project_weight, gate_weight, output_weight)
    )
    arriving = lambda u: (column[0][u], column[1][u], project_t[u])
    leaving = lambda u: (column[2][u], column[3][u], output_t[u])
    mult = 2 * pixels * channels

    def gate_of(zt, u):
        return pixel_call(
            gate_kernel, (zt,), (column[0][u], column[1][u], gate_t[u]), (channels,),
            pixels, tile, mult * channels,
        )[0]

    def triangle_of(sent, incoming):
        received = lax.all_to_all(sent.reshape(peers, 2 * own, pixels), GRID, 0, 0)
        product = triangle_call(
            received.reshape(2 * width, pixels), rows, side, own, incoming
        )
        return lax.all_to_all(product.reshape(peers, own, pixels), GRID, 0, 0).reshape(width, pixels)

    sent, zt = pixel_call(
        functools.partial(first_kernel, peers),
        (pair_act.reshape(pixels, channels), mask), arriving(0), (2 * width, channels),
        pixels, tile, mult * 4 * width, row_major_in=(0,),
    )
    gate = gate_of(zt, 0)
    triangle = triangle_of(sent, False)

    def middle(t, z, g, m, og, ob, ow, ig, ib, pw, lr, out):
        middle_kernel(peers, t, z, g, og, ob, ow, m, ig, ib, pw, lr, out)

    sent, zt = pixel_call(
        middle, (triangle, zt, gate, mask), leaving(0) + arriving(1), (2 * width, channels),
        pixels, tile, mult * 5 * width,
    )
    gate = gate_of(zt, 1)
    triangle = triangle_of(sent, True)
    return pixel_call(
        last_kernel, (triangle, zt, gate), leaving(1), (channels,),
        pixels, tile, mult * channels, row_major_out=(0,),
    )[0].reshape(side, side, channels)


def layer_norm(values, gain, bias, axis):
    average = jnp.mean(values, axis=axis, keepdims=True)
    centred = values - average
    spread_sq = jnp.mean(centred * centred, axis=axis, keepdims=True)
    return centred * lax.rsqrt(spread_sq + 1e-05) * gain + bias


def triangle_update(
    pair_act,
    mask_float,
    layer_index,
    input_gain,
    input_bias,
    project_weight,
    gate_weight,
    output_gain,
    output_bias,
    output_weight,
    incoming,
):
    rows, cols = lax.axis_size("row"), lax.axis_size("col")
    peers = rows * cols
    rows_here, cols_here, channels_here = pair_act.shape
    width = output_weight.shape[1]
    own = width // peers
    pixels = rows_here * cols_here
    pair_float = pair_act.astype(jnp.float32).reshape(pixels, channels_here)
    normed = layer_norm(
        pair_float, input_gain[layer_index], input_bias[layer_index], -1
    ).astype(jnp.bfloat16)
    projected = lax.dot_general(
        project_weight[layer_index],
        normed,
        (((0,), (1,)), ((), ())),
        preferred_element_type=jnp.float32,
    ).reshape(4, peers, own, pixels)
    mask_row = mask_float.reshape(1, 1, pixels)
    left_proj = (jax.nn.sigmoid(projected[0]) * projected[1] * mask_row).astype(jnp.bfloat16)
    right_proj = (jax.nn.sigmoid(projected[2]) * projected[3] * mask_row).astype(jnp.bfloat16)
    both = jnp.concatenate([left_proj, right_proj], axis=1)
    both = lax.all_to_all(both, GRID, 0, 0)
    both = both.reshape(rows, cols, 2, own, rows_here, cols_here)
    both = both.transpose(2, 3, 0, 4, 1, 5).reshape(2, own, rows * rows_here, cols * cols_here)
    spec = "cki,ckj->cij" if incoming else "cik,cjk->cij"
    triangle = jnp.einsum(spec, both[0], both[1], preferred_element_type=jnp.float32)
    triangle = triangle.astype(jnp.bfloat16).reshape(own, rows, rows_here, cols, cols_here)
    triangle = triangle.transpose(1, 3, 0, 2, 4).reshape(peers, own, pixels)
    triangle = lax.all_to_all(triangle, GRID, 0, 0).reshape(width, pixels)
    normed_sum = layer_norm(
        triangle.astype(jnp.float32),
        output_gain[layer_index][:, None],
        output_bias[layer_index][:, None],
        0,
    ).astype(jnp.bfloat16)
    gate_value = jax.nn.sigmoid(
        jnp.dot(normed, gate_weight[layer_index], preferred_element_type=jnp.float32)
    )
    mapped = lax.dot_general(
        normed_sum,
        output_weight[layer_index],
        (((0,), (0,)), ((), ())),
        preferred_element_type=jnp.float32,
    )
    return (
        (pair_float + gate_value * mapped)
        .astype(jnp.bfloat16)
        .reshape(rows_here, cols_here, channels_here)
    )


def shards(pair_act, pair_mask, *params):
    mask_float = pair_mask.astype(jnp.float32)
    rows, cols = lax.axis_size("row"), lax.axis_size("col")
    if fits(rows, cols, *pair_act.shape[:2], params[-1].shape[1]):
        return by_kernels(pair_act, mask_float, *params)
    for index in range(2):
        pair_act = triangle_update(pair_act, mask_float, index, *params, index == 1)
    return pair_act


def solution(mesh):
    return jax.shard_map(
        shards,
        mesh=mesh,
        in_specs=(P(("groups", "row"), "col", None), P(("groups", "row"), "col"))
        + (P(),) * 7,
        out_specs=P(("groups", "row"), "col", None),
        check_vma=False,
    )
```

```python
import functools

import jax
import jax.numpy as jnp
from jax import lax
from jax.experimental import pallas as pl
from jax.experimental.pallas import tpu as pltpu
from jax.sharding import PartitionSpec as P

GRID = ("row", "col")
LANES = 128


def logistic(values):
    return 0.5 * jnp.tanh(0.5 * values) + 0.5


def channel_norm(values, gain, bias):
    average = jnp.mean(values, axis=0, keepdims=True)
    centred = values - average
    spread_sq = jnp.mean(centred * centred, axis=0, keepdims=True)
    return centred * lax.rsqrt(spread_sq + 1e-05) * gain + bias


def dot(left, right):
    return jnp.dot(left, right, preferred_element_type=jnp.float32)


def emit_projections(peers, zt, mask, gain, bias, weight_t, lr_ref):
    width = weight_t.shape[0] // 4
    own = width // peers
    normed = channel_norm(zt, gain, bias).astype(jnp.bfloat16)
    projected = dot(weight_t, normed)
    tile = projected.shape[1]
    left = logistic(projected[:width]) * projected[width : 2 * width] * mask
    right = logistic(projected[2 * width : 3 * width]) * projected[3 * width :] * mask
    both = jnp.concatenate(
        [left.reshape(peers, own, tile), right.reshape(peers, own, tile)], axis=1
    )
    lr_ref[...] = both.reshape(2 * width, tile).astype(jnp.bfloat16)


def first_kernel(peers, z_ref, mask_ref, gain_ref, bias_ref, weight_ref, lr_ref, zt_ref):
    zt = z_ref[...].astype(jnp.float32).T
    zt_ref[...] = zt.astype(jnp.bfloat16)
    emit_projections(
        peers, zt, mask_ref[...], gain_ref[...], bias_ref[...], weight_ref[...], lr_ref
    )


def gate_kernel(zt_ref, gain_ref, bias_ref, weight_ref, gate_ref):
    normed = channel_norm(
        zt_ref[...].astype(jnp.float32), gain_ref[...], bias_ref[...]
    ).astype(jnp.bfloat16)
    gate_ref[...] = logistic(dot(weight_ref[...], normed)).astype(jnp.bfloat16)


def updated(t_ref, zt_ref, gate_ref, ogain_ref, obias_ref, oweight_ref):
    normed_sum = channel_norm(
        t_ref[...].astype(jnp.float32), ogain_ref[...], obias_ref[...]
    ).astype(jnp.bfloat16)
    mapped = dot(oweight_ref[...], normed_sum)
    return zt_ref[...].astype(jnp.float32) + gate_ref[...].astype(jnp.float32) * mapped


def middle_kernel(
    peers, t_ref, zt_ref, gate_ref, ogain_ref, obias_ref, oweight_ref,
    mask_ref, gain_ref, bias_ref, weight_ref, lr_ref, out_ref,
):
    fresh = updated(t_ref, zt_ref, gate_ref, ogain_ref, obias_ref, oweight_ref).astype(jnp.bfloat16)
    out_ref[...] = fresh
    emit_projections(
        peers, fresh.astype(jnp.float32), mask_ref[...], gain_ref[...], bias_ref[...],
        weight_ref[...], lr_ref,
    )


def last_kernel(t_ref, zt_ref, gate_ref, ogain_ref, obias_ref, oweight_ref, out_ref):
    fresh = updated(t_ref, zt_ref, gate_ref, ogain_ref, obias_ref, oweight_ref)
    out_ref[...] = fresh.T.astype(jnp.bfloat16)


def triangle_kernel(blocks, side, own, incoming, n_in, *refs):
    x_refs, y_refs, (left_ref, right_ref, rows_ref, tiles_ref) = refs[:n_in], refs[n_in:-4], refs[-4:]
    step = pl.program_id(0)
    zh = lax.axis_index("zh")
    pair = 2 * own
    span = 4 * side
    strip = side // 2
    half = blocks // 2
    pitch_rows = pair + 1
    lane = lax.broadcasted_iota(jnp.int32, (pair, LANES), 1)
    inside = lane < side

    def piece_of(piece_refs, piece):
        if len(piece_refs) == 1:
            return piece_refs[0], piece * strip * side
        return piece_refs[piece], 0

    @pl.when(step < blocks)
    def _unpack():
        upper, row_pair = step // half, lax.rem(step, half)
        mirror = lax.rem(row_pair + zh, 2)
        for r in range(2):
            at = pl.multiple_of((row_pair * 2 + r) * side + upper * strip, 16)
            if incoming:
                at_right = at
            else:
                at_right = pl.multiple_of((mirror * 2 + r) * LANES + upper * strip, 16)
            for zl in range(half):
                for piece in range(2):
                    x_ref, first = piece_of(x_refs, piece)
                    for group in range(strip // 4):
                        x = x_ref[
                            (r * half + zl) * pair : (r * half + zl + 1) * pair,
                            first + group * span : first + (group + 1) * span,
                        ].astype(jnp.float32)
                        a, b, c = x[:, :LANES], x[:, LANES : 2 * LANES], x[:, 2 * LANES :]
                        picked = (
                            a,
                            pltpu.roll(jnp.where(lane >= 96, a, b), 32, 1),
                            pltpu.roll(jnp.where(lane >= 64, b, c), 64, 1),
                            pltpu.roll(c, 96, 1),
                        )
                        for k, row in enumerate(picked):
                            rows_ref[pl.ds((group * 4 + k) * pitch_rows, pair), :] = jnp.where(
                                inside, row, 0.0
                            )
                    lanes = slice((piece * half + zl) * LANES, (piece * half + zl + 1) * LANES)
                    for ch in range(own):
                        left_ref[ch, pl.ds(at, strip), lanes] = rows_ref[
                            pl.ds(ch, strip, stride=pitch_rows), :
                        ].astype(jnp.bfloat16)
                        right_ref[ch, pl.ds(at_right, strip), lanes] = rows_ref[
                            pl.ds(own + ch, strip, stride=pitch_rows), :
                        ].astype(jnp.bfloat16)

    @pl.when(step == blocks - 1)
    def _multiply():
        contract = ((0,), (0,)) if incoming else ((1,), (1,))
        for ch in range(own):
            product = lax.dot_general(
                left_ref[ch], right_ref[ch], (contract, ((), ())), preferred_element_type=jnp.float32
            )
            for place in range(blocks):
                if incoming:
                    row, pitch = lax.rem(place // 2 + zh, 2) * 2 + place % 2, LANES
                else:
                    row, pitch = place, side
                for upper in range(2):
                    for col in range(blocks):
                        tiles_ref[
                            col // half,
                            upper * blocks + row,
                            pl.ds((col % half) * own + ch, strip, stride=pitch_rows),
                            :,
                        ] = product[
                            place * pitch + upper * strip : place * pitch + (upper + 1) * strip,
                            col * LANES : (col + 1) * LANES,
                        ]

    @pl.when(step >= blocks)
    def _repack():
        for r in range(2):
            place = (step - blocks) * 2 + r
            for piece in range(2):
                y_ref, first = piece_of(y_refs, piece)
                for group in range(strip // 4):
                    p, q, t, s = (
                        tiles_ref[piece, place, pl.ds((group * 4 + k) * pitch_rows, pair), :]
                        for k in range(4)
                    )
                    q, t, s = pltpu.roll(q, 96, 1), pltpu.roll(t, 64, 1), pltpu.roll(s, 32, 1)
                    flat = jnp.concatenate(
                        [
                            jnp.where(inside, p, q),
                            jnp.where(lane < 64, q, t),
                            jnp.where(lane < 32, t, s),
                        ],
                        axis=1,
                    )
                    y_ref[
                        r * pair : (r + 1) * pair, first + group * span : first + (group + 1) * span
                    ] = flat.astype(jnp.bfloat16)


def fits(mesh, residues, width):
    rows, cols = mesh.shape["row"], mesh.shape["col"]
    return (
        mesh.shape["groups"] == 2
        and rows == 4
        and cols == 4
        and 4 * residues == 3 * LANES * cols
        and width == 8 * rows * cols
    )


def whole_spec(array):
    return pl.BlockSpec(array.shape, lambda i: (0,) * array.ndim)


def triangle_call(received, n_out, blocks, side, own, incoming):
    pair = 2 * own
    pixels = side * side
    padded = blocks * LANES
    strip = side // 2
    left_rows = blocks * side
    right_rows = left_rows if incoming else padded
    return pl.pallas_call(
        functools.partial(triangle_kernel, blocks, side, own, incoming, len(received)),
        grid=(2 * blocks,),
        in_specs=[
            pl.BlockSpec((blocks * pair, a.shape[1]), lambda i: (jnp.minimum(i, blocks - 1), 0))
            for a in received
        ],
        out_specs=[
            pl.BlockSpec((2 * pair, pixels // n_out), lambda i: (jnp.maximum(i - blocks, 0), 0))
        ] * n_out,
        out_shape=[
            jax.ShapeDtypeStruct((blocks * blocks * own, pixels // n_out), jnp.bfloat16)
        ] * n_out,
        scratch_shapes=[
            pltpu.VMEM((own, left_rows, padded), jnp.bfloat16),
            pltpu.VMEM((own, right_rows, padded), jnp.bfloat16),
            pltpu.VMEM((strip * (pair + 1), LANES), jnp.float32),
            pltpu.VMEM((2, 2 * blocks, strip * (pair + 1), LANES), jnp.float32),
        ],
        compiler_params=pltpu.CompilerParams(vmem_limit_bytes=48 * 1024 * 1024),
        cost_estimate=pl.CostEstimate(
            flops=2 * own * (blocks * side) ** 3,
            bytes_accessed=12 * blocks * blocks * pair * pixels // 2,
            transcendentals=0,
        ),
    )(*received)


def pixel_call(body, tiled, fixed, outs, pixels, tile, flops, row_major_in=(), row_major_out=()):
    def spec(channels, row_major):
        if row_major:
            return pl.BlockSpec((tile, channels), lambda i: (i, 0))
        return pl.BlockSpec((channels, tile), lambda i: (0, i))

    in_specs = [
        spec(a.shape[1] if k in row_major_in else a.shape[0], k in row_major_in)
        for k, a in enumerate(tiled)
    ] + [whole_spec(a) for a in fixed]
    out_specs = [spec(ch, k in row_major_out) for k, ch in enumerate(outs)]
    out_shape = [
        jax.ShapeDtypeStruct((pixels, ch) if k in row_major_out else (ch, pixels), jnp.bfloat16)
        for k, ch in enumerate(outs)
    ]
    return pl.pallas_call(
        body,
        grid=(pixels // tile,),
        in_specs=in_specs,
        out_specs=out_specs,
        out_shape=out_shape,
        compiler_params=pltpu.CompilerParams(vmem_limit_bytes=48 * 1024 * 1024),
        cost_estimate=pl.CostEstimate(
            flops=flops, bytes_accessed=2 * pixels * (sum(outs) + 256), transcendentals=0
        ),
    )(*tiled, *fixed)


SWAP = ((0, 1), (1, 0))
LINE = ("groups", "zh")
CUBE = ("groups", "row", "zl")


def gather_group(own_half, other_half, home, chunks):
    early = lax.ppermute(own_half, LINE, ((1, 0), (2, 3)))
    size = own_half.shape[0] // chunks
    over, late = [], []
    for k in range(chunks):
        part = lax.ppermute(other_half[k * size : (k + 1) * size], "groups", SWAP)
        over.append(part)
        late.append(lax.ppermute(part, LINE, ((0, 1), (3, 2))))
    over, late = (jnp.concatenate(parts) if chunks > 1 else parts[0] for parts in (over, late))
    return jnp.where(home, own_half, over), jnp.where(home, early, late)


def by_kernels(
    pair_act,
    pair_mask,
    input_gain,
    input_bias,
    project_weight,
    gate_weight,
    output_gain,
    output_bias,
    output_weight,
):
    blocks = lax.axis_size("row")
    peers = blocks * blocks
    side, _, channels = pair_act.shape
    width = output_weight.shape[1]
    own = width // peers
    pixels = side * side
    strip = side // 2
    tile = 9 * LANES
    upper = lax.axis_index("groups")
    home = upper == lax.axis_index("zh")
    column = [a[:, :, None] for a in (input_gain, input_bias, output_gain, output_bias)]
    project_t, gate_t, output_t = (
        a.transpose(0, 2, 1) for a in (project_weight, gate_weight, output_weight)
    )
    arriving = lambda u: (column[0][u], column[1][u], project_t[u])
    leaving = lambda u: (column[2][u], column[3][u], output_t[u])
    mult = 2 * channels

    def halves(array):
        return (
            lax.dynamic_slice_in_dim(array, upper * strip, strip),
            lax.dynamic_slice_in_dim(array, (1 - upper) * strip, strip),
        )

    z_pieces = gather_group(*halves(pair_act), home, 2)
    m_pieces = gather_group(
        *(h.reshape(-1, LANES) for h in halves(pair_mask.astype(jnp.bfloat16))), home, 1
    )
    m_pieces = [m.reshape(1, -1) for m in m_pieces]

    def gate_of(zt, u):
        return pixel_call(
            gate_kernel, (zt,), (column[0][u], column[1][u], gate_t[u]), (channels,),
            zt.shape[1], tile, zt.shape[1] * mult * channels,
        )[0]

    def exchange(array):
        there = lax.all_to_all(array.reshape(peers, -1, array.shape[1]), CUBE, 0, 0)
        return there.reshape(array.shape)

    received, zts = [], []
    for z, m in zip(z_pieces, m_pieces):
        sent, zt = pixel_call(
            functools.partial(first_kernel, peers),
            (z.reshape(-1, channels), m), arriving(0), (2 * width, channels),
            pixels // 2, tile, pixels // 2 * mult * 4 * width, row_major_in=(0,),
        )
        received.append(exchange(sent))
        zts.append(zt)
    zt = jnp.concatenate(zts, axis=1)
    mask = jnp.concatenate(m_pieces, axis=1)
    gate = gate_of(zt, 0)
    triangle = exchange(*triangle_call(received, 1, blocks, side, own, False))

    def middle(t, z, g, m, og, ob, ow, ig, ib, pw, lr, out):
        middle_kernel(peers, t, z, g, og, ob, ow, m, ig, ib, pw, lr, out)

    sent, zt = pixel_call(
        middle, (triangle, zt, gate, mask), leaving(0) + arriving(1), (2 * width, channels),
        pixels, tile, pixels * mult * 5 * width,
    )
    gate = gate_of(zt, 1)
    products = triangle_call([exchange(sent)], 2, blocks, side, own, True)

    def finish(piece, triangle):
        part = slice(piece * strip * side, (piece + 1) * strip * side)
        return pixel_call(
            last_kernel, (triangle, zt[:, part], gate[:, part]), leaving(1), (channels,),
            pixels // 2, tile, pixels // 2 * mult * channels, row_major_out=(0,),
        )[0]

    there = finish(1, exchange(products[1]))
    beside, across = (
        lax.ppermute(there, LINE, pairs) for pairs in (((0, 1), (3, 2)), ((1, 2), (2, 1)))
    )
    there, waiting = lax.optimization_barrier((there, products[0]))
    here = finish(0, exchange(waiting))
    back = lax.ppermute(here, LINE, ((1, 3), (2, 0)))
    mine, others = jnp.where(home, here, beside), jnp.where(home, back, across)
    first = upper == 0
    return jnp.concatenate(
        [jnp.where(first, mine, others), jnp.where(first, others, mine)]
    ).reshape(side, side, channels)


def layer_norm(values, gain, bias, axis):
    average = jnp.mean(values, axis=axis, keepdims=True)
    centred = values - average
    spread_sq = jnp.mean(centred * centred, axis=axis, keepdims=True)
    return centred * lax.rsqrt(spread_sq + 1e-05) * gain + bias


def triangle_update(
    pair_act,
    mask_float,
    layer_index,
    input_gain,
    input_bias,
    project_weight,
    gate_weight,
    output_gain,
    output_bias,
    output_weight,
    incoming,
):
    rows, cols = lax.axis_size("row"), lax.axis_size("col")
    peers = rows * cols
    rows_here, cols_here, channels_here = pair_act.shape
    width = output_weight.shape[1]
    own = width // peers
    pixels = rows_here * cols_here
    pair_float = pair_act.astype(jnp.float32).reshape(pixels, channels_here)
    normed = layer_norm(
        pair_float, input_gain[layer_index], input_bias[layer_index], -1
    ).astype(jnp.bfloat16)
    projected = lax.dot_general(
        project_weight[layer_index],
        normed,
        (((0,), (1,)), ((), ())),
        preferred_element_type=jnp.float32,
    ).reshape(4, peers, own, pixels)
    mask_row = mask_float.reshape(1, 1, pixels)
    left_proj = (jax.nn.sigmoid(projected[0]) * projected[1] * mask_row).astype(jnp.bfloat16)
    right_proj = (jax.nn.sigmoid(projected[2]) * projected[3] * mask_row).astype(jnp.bfloat16)
    both = jnp.concatenate([left_proj, right_proj], axis=1)
    both = lax.all_to_all(both, GRID, 0, 0)
    both = both.reshape(rows, cols, 2, own, rows_here, cols_here)
    both = both.transpose(2, 3, 0, 4, 1, 5).reshape(2, own, rows * rows_here, cols * cols_here)
    spec = "cki,ckj->cij" if incoming else "cik,cjk->cij"
    triangle = jnp.einsum(spec, both[0], both[1], preferred_element_type=jnp.float32)
    triangle = triangle.astype(jnp.bfloat16).reshape(own, rows, rows_here, cols, cols_here)
    triangle = triangle.transpose(1, 3, 0, 2, 4).reshape(peers, own, pixels)
    triangle = lax.all_to_all(triangle, GRID, 0, 0).reshape(width, pixels)
    normed_sum = layer_norm(
        triangle.astype(jnp.float32),
        output_gain[layer_index][:, None],
        output_bias[layer_index][:, None],
        0,
    ).astype(jnp.bfloat16)
    gate_value = jax.nn.sigmoid(
        jnp.dot(normed, gate_weight[layer_index], preferred_element_type=jnp.float32)
    )
    mapped = lax.dot_general(
        normed_sum,
        output_weight[layer_index],
        (((0,), (0,)), ((), ())),
        preferred_element_type=jnp.float32,
    )
    return (
        (pair_float + gate_value * mapped)
        .astype(jnp.bfloat16)
        .reshape(rows_here, cols_here, channels_here)
    )


def shards(pair_act, pair_mask, *params):
    mask_float = pair_mask.astype(jnp.float32)
    for index in range(2):
        pair_act = triangle_update(pair_act, mask_float, index, *params, index == 1)
    return pair_act


def solution(mesh):
    def updates(pair_act, pair_mask, *params):
        body, grid, cols = shards, mesh, "col"
        if fits(mesh, pair_act.shape[1], params[-1].shape[1]):
            sizes = mesh.devices.shape
            grid = jax.sharding.Mesh(
                mesh.devices.reshape(*sizes[:2], 2, sizes[2] // 2), ("groups", "row", "zh", "zl")
            )
            body, cols = by_kernels, ("zh", "zl")
        pixels = (("groups", "row"), cols)
        return jax.shard_map(
            body,
            mesh=grid,
            in_specs=(P(*pixels, None), P(*pixels)) + (P(),) * 7,
            out_specs=P(*pixels, None),
            check_vma=False,
        )(pair_act, pair_mask, *params)

    return updates
```

```python
import functools

import jax
import jax.numpy as jnp
from jax import lax
from jax.experimental import pallas as pl
from jax.experimental.pallas import tpu as pltpu
from jax.sharding import PartitionSpec as P

GRID = ("row", "col")
LANES = 128


IN_GAIN, IN_BIAS, OUT_GAIN, OUT_BIAS = range(4)


def channel_norm(values, gain, bias):
    average = jnp.mean(values, axis=0, keepdims=True)
    centred = values - average
    spread_sq = jnp.mean(centred * centred, axis=0, keepdims=True)
    return centred * lax.rsqrt(spread_sq + 1e-05) * gain + bias


def dot(left, right):
    return jnp.dot(left, right, preferred_element_type=jnp.float32)


def norm_of(values, small_ref, update, which):
    at = 4 * update + which
    return channel_norm(values, small_ref[:, at : at + 1], small_ref[:, at + 1 : at + 2])


def emit_projections(peers, update, zt, mask_ref, small_ref, weight_ref, lr_ref):
    width = lr_ref.shape[0] // 2
    own = width // peers
    tile = zt.shape[1]
    normed = norm_of(zt, small_ref, update, IN_GAIN) * mask_ref[...].astype(jnp.float32)
    projected = dot(weight_ref[update, : 4 * width], normed.astype(jnp.bfloat16))
    left = (jnp.tanh(projected[:width]) + 1.0) * projected[width : 2 * width]
    right = (jnp.tanh(projected[2 * width : 3 * width]) + 1.0) * projected[3 * width :]
    both = jnp.concatenate(
        [left.reshape(peers, own, tile), right.reshape(peers, own, tile)], axis=1
    )
    lr_ref[...] = both.reshape(2 * width, tile).astype(jnp.bfloat16)


def first_kernel(peers, n_far, own_ref, *refs):
    far_refs, (mask_ref, small_ref, weight_ref), (lr_ref, zt_ref, z_ref) = (
        refs[:n_far], refs[n_far : n_far + 3], refs[-3:],
    )
    home = lax.axis_index("groups") == lax.axis_index("zh")
    per_part = pl.num_programs(0) // n_far

    @pl.when(home)
    def _own():
        z_ref[...] = own_ref[...].astype(jnp.float32)

    for k, far_ref in enumerate(far_refs):

        @pl.when(jnp.logical_and(jnp.logical_not(home), pl.program_id(0) // per_part == k))
        def _far(far_ref=far_ref):
            z_ref[...] = far_ref[...].astype(jnp.float32)

    zt = z_ref[...].T
    zt_ref[...] = zt.astype(jnp.bfloat16)
    emit_projections(peers, 0, zt, mask_ref, small_ref, weight_ref, lr_ref)


def gate_kernel(update, zt_ref, small_ref, weight_ref, gate_ref):
    channels = gate_ref.shape[0]
    normed = norm_of(zt_ref[...].astype(jnp.float32), small_ref, update, IN_GAIN)
    at = weight_ref.shape[1] - 2 * channels
    gates = dot(weight_ref[update, at : at + channels], normed.astype(jnp.bfloat16))
    gate_ref[...] = (0.5 * jnp.tanh(gates) + 0.5).astype(jnp.bfloat16)


def updated(update, t_ref, zt_ref, gate_ref, small_ref, weight_ref):
    normed_sum = norm_of(t_ref[...].astype(jnp.float32), small_ref, update, OUT_GAIN)
    at = weight_ref.shape[1] - zt_ref.shape[0]
    mapped = dot(weight_ref[update, at:], normed_sum.astype(jnp.bfloat16))
    return zt_ref[...].astype(jnp.float32) + gate_ref[...].astype(jnp.float32) * mapped


def middle_kernel(
    peers, t_ref, zt_ref, gate_ref, mask_ref, small_ref, weight_ref, lr_ref, out_ref
):
    fresh = updated(0, t_ref, zt_ref, gate_ref, small_ref, weight_ref).astype(jnp.bfloat16)
    out_ref[...] = fresh
    emit_projections(peers, 1, fresh.astype(jnp.float32), mask_ref, small_ref, weight_ref, lr_ref)


def last_kernel(t_ref, zt_ref, gate_ref, small_ref, weight_ref, out_ref):
    fresh = updated(1, t_ref, zt_ref, gate_ref, small_ref, weight_ref)
    out_ref[...] = fresh.T.astype(jnp.bfloat16)


def assemble_kernel(here_ref, beside_ref, back_ref, across_ref, out_ref, sems):
    upper = lax.axis_index("groups")
    home = upper == lax.axis_index("zh")

    def put(mine_ref, others_ref):
        copies = (
            pltpu.make_async_copy(mine_ref, out_ref.at[upper], sems.at[0]),
            pltpu.make_async_copy(others_ref, out_ref.at[1 - upper], sems.at[1]),
        )
        for copy in copies:
            copy.start()
        for copy in copies:
            copy.wait()

    @pl.when(home)
    def _home():
        put(here_ref, back_ref)

    @pl.when(jnp.logical_not(home))
    def _away():
        put(beside_ref, across_ref)


def triangle_kernel(blocks, side, own, incoming, n_in, *refs):
    x_refs, y_refs, (left_ref, right_ref, rows_ref, tiles_ref) = refs[:n_in], refs[n_in:-4], refs[-4:]
    step = pl.program_id(0)
    zh = lax.axis_index("zh")
    pair = 2 * own
    span = 4 * side
    strip = side // 2
    half = blocks // 2
    pitch_rows = pair + 1
    lane = lax.broadcasted_iota(jnp.int32, (pair, LANES), 1)
    inside = lane < side

    def piece_of(piece_refs, piece):
        if len(piece_refs) == 1:
            return piece_refs[0], piece * strip * side
        return piece_refs[piece], 0

    @pl.when(step < blocks)
    def _unpack():
        upper, row_pair = step // half, lax.rem(step, half)
        mirror = lax.rem(row_pair + zh, 2)
        for r in range(2):
            at = pl.multiple_of((row_pair * 2 + r) * side + upper * strip, 16)
            if incoming:
                at_right = at
            else:
                at_right = pl.multiple_of((mirror * 2 + r) * LANES + upper * strip, 16)
            for zl in range(half):
                for piece in range(2):
                    x_ref, first = piece_of(x_refs, piece)
                    for group in range(strip // 4):
                        x = x_ref[
                            (r * half + zl) * pair : (r * half + zl + 1) * pair,
                            first + group * span : first + (group + 1) * span,
                        ].astype(jnp.float32)
                        a, b, c = x[:, :LANES], x[:, LANES : 2 * LANES], x[:, 2 * LANES :]
                        picked = (
                            a,
                            pltpu.roll(jnp.where(lane >= 96, a, b), 32, 1),
                            pltpu.roll(jnp.where(lane >= 64, b, c), 64, 1),
                            pltpu.roll(c, 96, 1),
                        )
                        for k, row in enumerate(picked):
                            rows_ref[pl.ds((group * 4 + k) * pitch_rows, pair), :] = jnp.where(
                                inside, row, 0.0
                            )
                    lanes = slice((piece * half + zl) * LANES, (piece * half + zl + 1) * LANES)
                    for ch in range(own):
                        left_ref[ch, pl.ds(at, strip), lanes] = rows_ref[
                            pl.ds(ch, strip, stride=pitch_rows), :
                        ].astype(jnp.bfloat16)
                        right_ref[ch, pl.ds(at_right, strip), lanes] = rows_ref[
                            pl.ds(own + ch, strip, stride=pitch_rows), :
                        ].astype(jnp.bfloat16)

    @pl.when(step == blocks - 1)
    def _multiply():
        contract = ((0,), (0,)) if incoming else ((1,), (1,))
        for ch in range(own):
            product = lax.dot_general(
                left_ref[ch], right_ref[ch], (contract, ((), ())), preferred_element_type=jnp.float32
            )
            for place in range(blocks):
                if incoming:
                    row, pitch = lax.rem(place // 2 + zh, 2) * 2 + place % 2, LANES
                else:
                    row, pitch = place, side
                for upper in range(2):
                    for col in range(blocks):
                        tiles_ref[
                            col // half,
                            upper * blocks + row,
                            pl.ds((col % half) * own + ch, strip, stride=pitch_rows),
                            :,
                        ] = product[
                            place * pitch + upper * strip : place * pitch + (upper + 1) * strip,
                            col * LANES : (col + 1) * LANES,
                        ]

    @pl.when(step >= blocks)
    def _repack():
        for r in range(2):
            place = (step - blocks) * 2 + r
            for piece in range(2):
                y_ref, first = piece_of(y_refs, piece)
                for group in range(strip // 4):
                    p, q, t, s = (
                        tiles_ref[piece, place, pl.ds((group * 4 + k) * pitch_rows, pair), :]
                        for k in range(4)
                    )
                    q, t, s = pltpu.roll(q, 96, 1), pltpu.roll(t, 64, 1), pltpu.roll(s, 32, 1)
                    flat = jnp.concatenate(
                        [
                            jnp.where(inside, p, q),
                            jnp.where(lane < 64, q, t),
                            jnp.where(lane < 32, t, s),
                        ],
                        axis=1,
                    )
                    y_ref[
                        r * pair : (r + 1) * pair, first + group * span : first + (group + 1) * span
                    ] = flat.astype(jnp.bfloat16)


def fits(mesh, residues, width):
    rows, cols = mesh.shape["row"], mesh.shape["col"]
    return (
        mesh.shape["groups"] == 2
        and rows == 4
        and cols == 4
        and 4 * residues == 3 * LANES * cols
        and width == 8 * rows * cols
    )


def whole_spec(array):
    return pl.BlockSpec(array.shape, lambda i: (0,) * array.ndim)


def triangle_call(received, n_out, blocks, side, own, incoming):
    pair = 2 * own
    pixels = side * side
    padded = blocks * LANES
    strip = side // 2
    left_rows = blocks * side
    right_rows = left_rows if incoming else padded
    return pl.pallas_call(
        functools.partial(triangle_kernel, blocks, side, own, incoming, len(received)),
        grid=(2 * blocks,),
        in_specs=[
            pl.BlockSpec((blocks * pair, a.shape[1]), lambda i: (jnp.minimum(i, blocks - 1), 0))
            for a in received
        ],
        out_specs=[
            pl.BlockSpec((2 * pair, pixels // n_out), lambda i: (jnp.maximum(i - blocks, 0), 0))
        ] * n_out,
        out_shape=[
            jax.ShapeDtypeStruct((blocks * blocks * own, pixels // n_out), jnp.bfloat16)
        ] * n_out,
        scratch_shapes=[
            pltpu.VMEM((own, left_rows, padded), jnp.bfloat16),
            pltpu.VMEM((own, right_rows, padded), jnp.bfloat16),
            pltpu.VMEM((strip * (pair + 1), LANES), jnp.float32),
            pltpu.VMEM((2, 2 * blocks, strip * (pair + 1), LANES), jnp.float32),
        ],
        compiler_params=pltpu.CompilerParams(vmem_limit_bytes=48 * 1024 * 1024),
        cost_estimate=pl.CostEstimate(
            flops=2 * own * (blocks * side) ** 3,
            bytes_accessed=12 * blocks * blocks * pair * pixels // 2,
            transcendentals=0,
        ),
    )(*received)


def pixel_call(body, tiled, fixed, outs, steps, tile, flops, start=0, pixels=None, kept=(), scratch=(), row_major_out=False):
    pixels = pixels or steps * tile

    def spec(channels, first, count, row_major):
        if row_major:
            return pl.BlockSpec(
                (tile, channels), lambda i: (jnp.clip(i + first, 0, count - 1), 0)
            )
        return pl.BlockSpec((channels, tile), lambda i: (0, jnp.clip(i + first, 0, count - 1)))

    in_specs = [
        spec(a.shape[1] if row_major else a.shape[0], first, count, row_major)
        for a, first, count, row_major in tiled
    ]
    in_specs += [whole_spec(a) for a in fixed]
    in_specs += [pl.BlockSpec(memory_space=pl.ANY)] * len(kept)
    n_in, n_kept = len(in_specs), len(kept)

    def kernel(*refs):
        body(*refs[: n_in - n_kept], *refs[n_in:])

    return pl.pallas_call(
        kernel,
        grid=(steps,),
        in_specs=in_specs,
        out_specs=[spec(ch, start, pixels // tile, row_major_out) for ch in outs],
        out_shape=[
            jax.ShapeDtypeStruct((pixels, ch) if row_major_out else (ch, pixels), jnp.bfloat16)
            for ch in outs
        ],
        input_output_aliases={n_in - n_kept + k: k for k in range(n_kept)},
        scratch_shapes=list(scratch),
        compiler_params=pltpu.CompilerParams(vmem_limit_bytes=48 * 1024 * 1024),
        cost_estimate=pl.CostEstimate(
            flops=flops, bytes_accessed=2 * steps * tile * (sum(outs) + 256), transcendentals=0
        ),
    )(*(a for a, *_ in tiled), *fixed, *kept)


SWAP = ((0, 1), (1, 0))
LINE = ("groups", "zh")
CUBE = ("groups", "row", "zl")


def gather_group(own_half, other_half, chunks):
    early = lax.ppermute(own_half, LINE, ((1, 0), (2, 3)))
    size = own_half.shape[0] // chunks
    over, late = [], []
    for k in range(chunks):
        part = lax.ppermute(other_half[k * size : (k + 1) * size], "groups", SWAP)
        over.append(part)
        late.append(lax.ppermute(part, LINE, ((0, 1), (3, 2))))
    return early, over, late


def by_kernels(
    pair_act,
    pair_mask,
    input_gain,
    input_bias,
    project_weight,
    gate_weight,
    output_gain,
    output_bias,
    output_weight,
):
    blocks = lax.axis_size("row")
    peers = blocks * blocks
    side, _, channels = pair_act.shape
    width = output_weight.shape[1]
    own = width // peers
    pixels = side * side
    strip = side // 2
    tile = 9 * LANES
    steps = pixels // tile
    upper = lax.axis_index("groups")
    home = upper == lax.axis_index("zh")
    mult = 2 * channels * tile

    def halves(array):
        return (
            lax.dynamic_slice_in_dim(array, upper * strip, strip),
            lax.dynamic_slice_in_dim(array, (1 - upper) * strip, strip),
        )

    z_own, z_other = (h.reshape(-1, channels) for h in halves(pair_act))
    z_early, z_over, z_late = gather_group(z_own, z_other, 2)
    m_own, m_other = (
        h.reshape(-1, LANES) for h in halves(pair_mask.astype(jnp.bfloat16))
    )
    m_early, (m_over,), (m_late,) = gather_group(m_own, m_other, 1)
    m_pieces = [
        jnp.where(home, a, b).reshape(1, -1) for a, b in ((m_own, m_over), (m_early, m_late))
    ]
    small = jnp.stack([input_gain, input_bias, output_gain, output_bias], axis=1)
    small = small.reshape(-1, channels).T
    weights = jnp.concatenate(
        [project_weight * 0.5, gate_weight * 0.5, output_weight], axis=2
    ).transpose(0, 2, 1)
    fixed = (small, weights)

    def first(piece, ours, far, mask, kept):
        per_part = steps // 2 // len(far)
        tiled = [(ours, 0, steps // 2, True)]
        tiled += [(part, -k * per_part, per_part, True) for k, part in enumerate(far)]
        tiled += [(mask, 0, steps // 2, False)]
        return pixel_call(
            functools.partial(first_kernel, peers, len(far)),
            tiled, fixed, (2 * width, channels), steps // 2, tile, steps // 2 * mult * 4 * width,
            start=piece * steps // 2, pixels=pixels, kept=kept,
            scratch=(pltpu.VMEM((tile, channels), jnp.float32),),
        )

    def gate_of(zt, u):
        return pixel_call(
            functools.partial(gate_kernel, u), [(zt, 0, steps, False)], fixed, (channels,),
            steps, tile, steps * mult * channels,
        )[0]

    def exchange(array):
        there = lax.all_to_all(array.reshape(peers, -1, array.shape[1]), CUBE, 0, 0)
        return there.reshape(array.shape)

    begun = first(0, z_own, z_over, m_pieces[0], ())
    sent, zt = first(1, z_early, z_late, m_pieces[1], begun)
    gate = gate_of(zt, 0)
    triangle = exchange(*triangle_call([exchange(sent)], 1, blocks, side, own, False))
    mask = jnp.concatenate(m_pieces, axis=1)
    sent, zt = pixel_call(
        functools.partial(middle_kernel, peers),
        [(a, 0, steps, False) for a in (triangle, zt, gate, mask)], fixed, (2 * width, channels),
        steps, tile, steps * mult * 5 * width,
    )
    gate = gate_of(zt, 1)
    products = triangle_call([exchange(sent)], 2, blocks, side, own, True)

    def finish(piece, triangle):
        at = piece * steps // 2
        return pixel_call(
            last_kernel,
            [(triangle, 0, steps // 2, False), (zt, at, steps, False), (gate, at, steps, False)],
            fixed, (channels,), steps // 2, tile, steps // 2 * mult * channels, row_major_out=True,
        )[0]

    there = finish(1, exchange(products[1]))
    beside, across = (
        lax.ppermute(there, LINE, pairs) for pairs in (((0, 1), (3, 2)), ((1, 2), (2, 1)))
    )
    there, waiting = lax.optimization_barrier((there, products[0]))
    here = finish(0, exchange(waiting))
    back = lax.ppermute(here, LINE, ((1, 3), (2, 0)))
    return pl.pallas_call(
        assemble_kernel,
        in_specs=[pl.BlockSpec(memory_space=pl.ANY)] * 4,
        out_specs=pl.BlockSpec(memory_space=pl.ANY),
        out_shape=jax.ShapeDtypeStruct((2, *here.shape), here.dtype),
        scratch_shapes=[pltpu.SemaphoreType.DMA((2,))],
    )(here, beside, back, across).reshape(side, side, channels)


def layer_norm(values, gain, bias, axis):
    average = jnp.mean(values, axis=axis, keepdims=True)
    centred = values - average
    spread_sq = jnp.mean(centred * centred, axis=axis, keepdims=True)
    return centred * lax.rsqrt(spread_sq + 1e-05) * gain + bias


def triangle_update(
    pair_act,
    mask_float,
    layer_index,
    input_gain,
    input_bias,
    project_weight,
    gate_weight,
    output_gain,
    output_bias,
    output_weight,
    incoming,
):
    rows, cols = lax.axis_size("row"), lax.axis_size("col")
    peers = rows * cols
    rows_here, cols_here, channels_here = pair_act.shape
    width = output_weight.shape[1]
    own = width // peers
    pixels = rows_here * cols_here
    pair_float = pair_act.astype(jnp.float32).reshape(pixels, channels_here)
    normed = layer_norm(
        pair_float, input_gain[layer_index], input_bias[layer_index], -1
    ).astype(jnp.bfloat16)
    projected = lax.dot_general(
        project_weight[layer_index],
        normed,
        (((0,), (1,)), ((), ())),
        preferred_element_type=jnp.float32,
    ).reshape(4, peers, own, pixels)
    mask_row = mask_float.reshape(1, 1, pixels)
    left_proj = (jax.nn.sigmoid(projected[0]) * projected[1] * mask_row).astype(jnp.bfloat16)
    right_proj = (jax.nn.sigmoid(projected[2]) * projected[3] * mask_row).astype(jnp.bfloat16)
    both = jnp.concatenate([left_proj, right_proj], axis=1)
    both = lax.all_to_all(both, GRID, 0, 0)
    both = both.reshape(rows, cols, 2, own, rows_here, cols_here)
    both = both.transpose(2, 3, 0, 4, 1, 5).reshape(2, own, rows * rows_here, cols * cols_here)
    spec = "cki,ckj->cij" if incoming else "cik,cjk->cij"
    triangle = jnp.einsum(spec, both[0], both[1], preferred_element_type=jnp.float32)
    triangle = triangle.astype(jnp.bfloat16).reshape(own, rows, rows_here, cols, cols_here)
    triangle = triangle.transpose(1, 3, 0, 2, 4).reshape(peers, own, pixels)
    triangle = lax.all_to_all(triangle, GRID, 0, 0).reshape(width, pixels)
    normed_sum = layer_norm(
        triangle.astype(jnp.float32),
        output_gain[layer_index][:, None],
        output_bias[layer_index][:, None],
        0,
    ).astype(jnp.bfloat16)
    gate_value = jax.nn.sigmoid(
        jnp.dot(normed, gate_weight[layer_index], preferred_element_type=jnp.float32)
    )
    mapped = lax.dot_general(
        normed_sum,
        output_weight[layer_index],
        (((0,), (0,)), ((), ())),
        preferred_element_type=jnp.float32,
    )
    return (
        (pair_float + gate_value * mapped)
        .astype(jnp.bfloat16)
        .reshape(rows_here, cols_here, channels_here)
    )


def shards(pair_act, pair_mask, *params):
    mask_float = pair_mask.astype(jnp.float32)
    for index in range(2):
        pair_act = triangle_update(pair_act, mask_float, index, *params, index == 1)
    return pair_act


def solution(mesh):
    def updates(pair_act, pair_mask, *params):
        body, grid, cols = shards, mesh, "col"
        if fits(mesh, pair_act.shape[1], params[-1].shape[1]):
            sizes = mesh.devices.shape
            grid = jax.sharding.Mesh(
                mesh.devices.reshape(*sizes[:2], 2, sizes[2] // 2), ("groups", "row", "zh", "zl")
            )
            body, cols = by_kernels, ("zh", "zl")
        pixels = (("groups", "row"), cols)
        return jax.shard_map(
            body,
            mesh=grid,
            in_specs=(P(*pixels, None), P(*pixels)) + (P(),) * 7,
            out_specs=P(*pixels, None),
            check_vma=False,
        )(pair_act, pair_mask, *params)

    return updates
```

```python
import functools

import jax
import jax.numpy as jnp
from jax import lax
from jax.experimental import pallas as pl
from jax.experimental.pallas import tpu as pltpu
from jax.sharding import PartitionSpec as P

GRID = ("row", "col")
LANES = 128


IN_GAIN, IN_BIAS, OUT_GAIN, OUT_BIAS = range(4)


def channel_norm(values, gain, bias):
    average = jnp.mean(values, axis=0, keepdims=True)
    centred = values - average
    spread_sq = jnp.mean(centred * centred, axis=0, keepdims=True)
    return centred * lax.rsqrt(spread_sq + 1e-05) * gain + bias


def dot(left, right):
    return jnp.dot(left, right, preferred_element_type=jnp.float32)


def norm_of(values, small_ref, update, which):
    at = 4 * update + which
    return channel_norm(values, small_ref[:, at : at + 1], small_ref[:, at + 1 : at + 2])


def emit_projections(peers, update, zt, mask_ref, small_ref, weight_ref, lr_ref):
    width = lr_ref.shape[0] // 2
    own = width // peers
    tile = zt.shape[1]
    normed = norm_of(zt, small_ref, update, IN_GAIN) * mask_ref[...].astype(jnp.float32)
    projected = dot(weight_ref[update, : 4 * width], normed.astype(jnp.bfloat16))
    left = (jnp.tanh(projected[:width]) + 1.0) * projected[width : 2 * width]
    right = (jnp.tanh(projected[2 * width : 3 * width]) + 1.0) * projected[3 * width :]
    both = jnp.concatenate(
        [left.reshape(peers, own, tile), right.reshape(peers, own, tile)], axis=1
    )
    lr_ref[...] = both.reshape(2 * width, tile).astype(jnp.bfloat16)


def first_kernel(peers, parts, own_ref, *refs):
    far_refs, (mask_ref, small_ref, weight_ref), (lr_ref, zt_ref) = (
        refs[: len(parts)], refs[len(parts) : -2], refs[-2:],
    )
    home = lax.axis_index("groups") == lax.axis_index("zh")
    step = pl.program_id(0)

    def put(z_ref):
        zt_ref[...] = z_ref[...].astype(jnp.float32).T.astype(jnp.bfloat16)

    pl.when(home)(lambda: put(own_ref))
    for (begin, end), far_ref in zip(parts, far_refs):
        here = jnp.logical_and(step >= begin, step < end)
        pl.when(jnp.logical_and(jnp.logical_not(home), here))(functools.partial(put, far_ref))
    zt = zt_ref[...].astype(jnp.float32)
    emit_projections(peers, 0, zt, mask_ref, small_ref, weight_ref, lr_ref)


def gate_kernel(update, zt_ref, small_ref, weight_ref, gate_ref):
    channels = gate_ref.shape[0]
    normed = norm_of(zt_ref[...].astype(jnp.float32), small_ref, update, IN_GAIN)
    at = weight_ref.shape[1] - 2 * channels
    gates = dot(weight_ref[update, at : at + channels], normed.astype(jnp.bfloat16))
    gate_ref[...] = (0.5 * jnp.tanh(gates) + 0.5).astype(jnp.bfloat16)


def updated(update, t_ref, zt_ref, gate_ref, small_ref, weight_ref):
    normed_sum = norm_of(t_ref[...].astype(jnp.float32), small_ref, update, OUT_GAIN)
    at = weight_ref.shape[1] - zt_ref.shape[0]
    mapped = dot(weight_ref[update, at:], normed_sum.astype(jnp.bfloat16))
    return zt_ref[...].astype(jnp.float32) + gate_ref[...].astype(jnp.float32) * mapped


def middle_kernel(
    peers, t_ref, zt_ref, gate_ref, mask_ref, small_ref, weight_ref, lr_ref, out_ref
):
    fresh = updated(0, t_ref, zt_ref, gate_ref, small_ref, weight_ref).astype(jnp.bfloat16)
    out_ref[...] = fresh
    emit_projections(peers, 1, fresh.astype(jnp.float32), mask_ref, small_ref, weight_ref, lr_ref)


def last_kernel(t_ref, zt_ref, gate_ref, small_ref, weight_ref, out_ref):
    fresh = updated(1, t_ref, zt_ref, gate_ref, small_ref, weight_ref)
    out_ref[...] = fresh.T.astype(jnp.bfloat16)


def assemble_kernel(per_half, place_ref, here_ref, beside_ref, back_ref, across_ref, out_ref):
    mine = pl.program_id(0) // per_half == place_ref[0]
    home = place_ref[1] == 1
    for side_of, whose, ref in (
        (home, mine, here_ref),
        (jnp.logical_not(home), mine, beside_ref),
        (home, jnp.logical_not(mine), back_ref),
        (jnp.logical_not(home), jnp.logical_not(mine), across_ref),
    ):

        @pl.when(jnp.logical_and(side_of, whose))
        def _put(ref=ref):
            out_ref[...] = ref[...]


def triangle_kernel(blocks, side, own, incoming, n_in, *refs):
    x_refs, y_refs, (left_ref, right_ref, rows_ref, tiles_ref) = refs[:n_in], refs[n_in:-4], refs[-4:]
    step = pl.program_id(0)
    zh = lax.axis_index("zh")
    pair = 2 * own
    span = 4 * side
    strip = side // 2
    half = blocks // 2
    pitch_rows = pair + 1
    lane = lax.broadcasted_iota(jnp.int32, (pair, LANES), 1)
    inside = lane < side

    def piece_of(piece_refs, piece):
        if len(piece_refs) == 1:
            return piece_refs[0], piece * strip * side
        return piece_refs[piece], 0

    @pl.when(step < blocks)
    def _unpack():
        upper, row_pair = step // half, lax.rem(step, half)
        mirror = lax.rem(row_pair + zh, 2)
        for r in range(2):
            at = pl.multiple_of((row_pair * 2 + r) * side + upper * strip, 16)
            if incoming:
                at_right = at
            else:
                at_right = pl.multiple_of((mirror * 2 + r) * LANES + upper * strip, 16)
            for zl in range(half):
                for piece in range(2):
                    x_ref, first = piece_of(x_refs, piece)
                    for group in range(strip // 4):
                        x = x_ref[
                            (r * half + zl) * pair : (r * half + zl + 1) * pair,
                            first + group * span : first + (group + 1) * span,
                        ].astype(jnp.float32)
                        a, b, c = x[:, :LANES], x[:, LANES : 2 * LANES], x[:, 2 * LANES :]
                        picked = (
                            a,
                            pltpu.roll(jnp.where(lane >= 96, a, b), 32, 1),
                            pltpu.roll(jnp.where(lane >= 64, b, c), 64, 1),
                            pltpu.roll(c, 96, 1),
                        )
                        for k, row in enumerate(picked):
                            rows_ref[pl.ds((group * 4 + k) * pitch_rows, pair), :] = jnp.where(
                                inside, row, 0.0
                            )
                    lanes = slice((piece * half + zl) * LANES, (piece * half + zl + 1) * LANES)
                    for ch in range(own):
                        left_ref[ch, pl.ds(at, strip), lanes] = rows_ref[
                            pl.ds(ch, strip, stride=pitch_rows), :
                        ].astype(jnp.bfloat16)
                        right_ref[ch, pl.ds(at_right, strip), lanes] = rows_ref[
                            pl.ds(own + ch, strip, stride=pitch_rows), :
                        ].astype(jnp.bfloat16)

    @pl.when(step == blocks - 1)
    def _multiply():
        contract = ((0,), (0,)) if incoming else ((1,), (1,))
        for ch in range(own):
            product = lax.dot_general(
                left_ref[ch], right_ref[ch], (contract, ((), ())), preferred_element_type=jnp.float32
            )
            for place in range(blocks):
                if incoming:
                    row, pitch = lax.rem(place // 2 + zh, 2) * 2 + place % 2, LANES
                else:
                    row, pitch = place, side
                for upper in range(2):
                    for col in range(blocks):
                        tiles_ref[
                            col // half,
                            upper * blocks + row,
                            pl.ds((col % half) * own + ch, strip, stride=pitch_rows),
                            :,
                        ] = product[
                            place * pitch + upper * strip : place * pitch + (upper + 1) * strip,
                            col * LANES : (col + 1) * LANES,
                        ]

    @pl.when(step >= blocks)
    def _repack():
        for r in range(2):
            place = (step - blocks) * 2 + r
            for piece in range(2):
                y_ref, first = piece_of(y_refs, piece)
                for group in range(strip // 4):
                    p, q, t, s = (
                        tiles_ref[piece, place, pl.ds((group * 4 + k) * pitch_rows, pair), :]
                        for k in range(4)
                    )
                    q, t, s = pltpu.roll(q, 96, 1), pltpu.roll(t, 64, 1), pltpu.roll(s, 32, 1)
                    flat = jnp.concatenate(
                        [
                            jnp.where(inside, p, q),
                            jnp.where(lane < 64, q, t),
                            jnp.where(lane < 32, t, s),
                        ],
                        axis=1,
                    )
                    y_ref[
                        r * pair : (r + 1) * pair, first + group * span : first + (group + 1) * span
                    ] = flat.astype(jnp.bfloat16)


def fits(mesh, residues, width):
    rows, cols = mesh.shape["row"], mesh.shape["col"]
    return (
        mesh.shape["groups"] == 2
        and rows == 4
        and cols == 4
        and 4 * residues == 3 * LANES * cols
        and width == 8 * rows * cols
    )


def whole_spec(array):
    return pl.BlockSpec(array.shape, lambda i: (0,) * array.ndim)


def triangle_call(received, n_out, blocks, side, own, incoming):
    pair = 2 * own
    pixels = side * side
    padded = blocks * LANES
    strip = side // 2
    left_rows = blocks * side
    right_rows = left_rows if incoming else padded
    return pl.pallas_call(
        functools.partial(triangle_kernel, blocks, side, own, incoming, len(received)),
        grid=(2 * blocks,),
        in_specs=[
            pl.BlockSpec((blocks * pair, a.shape[1]), lambda i: (jnp.minimum(i, blocks - 1), 0))
            for a in received
        ],
        out_specs=[
            pl.BlockSpec((2 * pair, pixels // n_out), lambda i: (jnp.maximum(i - blocks, 0), 0))
        ] * n_out,
        out_shape=[
            jax.ShapeDtypeStruct((blocks * blocks * own, pixels // n_out), jnp.bfloat16)
        ] * n_out,
        scratch_shapes=[
            pltpu.VMEM((own, left_rows, padded), jnp.bfloat16),
            pltpu.VMEM((own, right_rows, padded), jnp.bfloat16),
            pltpu.VMEM((strip * (pair + 1), LANES), jnp.float32),
            pltpu.VMEM((2, 2 * blocks, strip * (pair + 1), LANES), jnp.float32),
        ],
        compiler_params=pltpu.CompilerParams(vmem_limit_bytes=48 * 1024 * 1024),
        cost_estimate=pl.CostEstimate(
            flops=2 * own * (blocks * side) ** 3,
            bytes_accessed=12 * blocks * blocks * pair * pixels // 2,
            transcendentals=0,
        ),
    )(*received)


def pixel_call(body, tiled, fixed, outs, steps, tile, flops, start=0, pixels=None, kept=(), scratch=(), row_major_out=False):
    pixels = pixels or steps * tile

    def spec(channels, first, count, row_major):
        if row_major:
            return pl.BlockSpec(
                (tile, channels), lambda i: (jnp.clip(i + first, 0, count - 1), 0)
            )
        return pl.BlockSpec((channels, tile), lambda i: (0, jnp.clip(i + first, 0, count - 1)))

    in_specs = [
        spec(a.shape[1] if row_major else a.shape[0], first, count, row_major)
        for a, first, count, row_major in tiled
    ]
    in_specs += [whole_spec(a) for a in fixed]
    in_specs += [pl.BlockSpec(memory_space=pl.ANY)] * len(kept)
    n_in, n_kept = len(in_specs), len(kept)

    def kernel(*refs):
        body(*refs[: n_in - n_kept], *refs[n_in:])

    return pl.pallas_call(
        kernel,
        grid=(steps,),
        in_specs=in_specs,
        out_specs=[spec(ch, start, pixels // tile, row_major_out) for ch in outs],
        out_shape=[
            jax.ShapeDtypeStruct((pixels, ch) if row_major_out else (ch, pixels), jnp.bfloat16)
            for ch in outs
        ],
        input_output_aliases={n_in - n_kept + k: k for k in range(n_kept)},
        scratch_shapes=list(scratch),
        compiler_params=pltpu.CompilerParams(vmem_limit_bytes=48 * 1024 * 1024),
        cost_estimate=pl.CostEstimate(
            flops=flops, bytes_accessed=2 * steps * tile * (sum(outs) + 256), transcendentals=0
        ),
    )(*(a for a, *_ in tiled), *fixed, *kept)


SWAP = ((0, 1), (1, 0))
LINE = ("groups", "zh")
CUBE = ("groups", "row", "zl")


def gather_group(own_half, other_half, cuts):
    early = lax.ppermute(own_half, LINE, ((1, 0), (2, 3)))
    over, late = [], []
    for begin, end in zip((0, *cuts[:-2]), cuts[:-1]):
        part = lax.ppermute(other_half[begin:end], "groups", SWAP)
        over.append(part)
        late.append(lax.ppermute(part, LINE, ((0, 1), (3, 2))))
    rest = other_half[cuts[-2] :]
    late.append(lax.ppermute(rest, LINE, ((1, 2), (2, 1))))
    over.append(lax.ppermute(rest, LINE, ((0, 2), (3, 1))))
    return early, over, late


def by_kernels(
    pair_act,
    pair_mask,
    input_gain,
    input_bias,
    project_weight,
    gate_weight,
    output_gain,
    output_bias,
    output_weight,
):
    blocks = lax.axis_size("row")
    peers = blocks * blocks
    side, _, channels = pair_act.shape
    width = output_weight.shape[1]
    own = width // peers
    pixels = side * side
    strip = side // 2
    upper = lax.axis_index("groups")
    home = upper == lax.axis_index("zh")
    mult = 2 * channels

    def halves(array):
        return (
            lax.dynamic_slice_in_dim(array, upper * strip, strip),
            lax.dynamic_slice_in_dim(array, (1 - upper) * strip, strip),
        )

    m_own, m_other = (
        h.reshape(-1, LANES) for h in halves(pair_mask.astype(jnp.bfloat16))
    )
    m_next = lax.ppermute(
        jnp.where(home, m_other, m_own), LINE, ((1, 0), (2, 3), (0, 2), (3, 1))
    )
    m_across = lax.ppermute(m_other, LINE, ((1, 2), (2, 1)))
    m_pieces = [
        jnp.where(home, a, b).reshape(1, -1) for a, b in ((m_own, m_next), (m_next, m_across))
    ]
    z_own, z_other = (h.reshape(-1, channels) for h in halves(pair_act))
    tile = 9 * LANES
    per_piece = pixels // 2 // tile
    tiles = (1, per_piece - 1, per_piece)
    z_early, z_over, z_late = gather_group(z_own, z_other, [n * tile for n in tiles])
    small = jnp.stack([input_gain, input_bias, output_gain, output_bias], axis=1)
    small = small.reshape(-1, channels).T
    weights = jnp.concatenate(
        [project_weight * 0.5, gate_weight * 0.5, output_weight], axis=2
    ).transpose(0, 2, 1)
    fixed = (small, weights)

    def first(piece, ours, far, mask, kept):
        parts = list(zip((0, *tiles), tiles))
        tiled = [(ours, 0, per_piece, True)]
        tiled += [
            (part, -begin, end - begin, True) for part, (begin, end) in zip(far, parts)
        ]
        tiled += [(mask, 0, per_piece, False)]
        return pixel_call(
            functools.partial(first_kernel, peers, parts),
            tiled, fixed, (2 * width, channels), per_piece, tile, pixels // 2 * mult * 4 * width,
            start=piece * per_piece, pixels=pixels, kept=kept,
        )

    begun = first(0, z_own, z_over, m_pieces[0], ())
    sent, zt = first(1, z_early, z_late, m_pieces[1], begun)
    wide = 2 * tile
    steps = pixels // wide

    def gate_of(zt, u):
        return pixel_call(
            functools.partial(gate_kernel, u), [(zt, 0, steps, False)], fixed, (channels,),
            steps, wide, pixels * mult * channels,
        )[0]

    def exchange(array):
        there = lax.all_to_all(array.reshape(peers, -1, array.shape[1]), CUBE, 0, 0)
        return there.reshape(array.shape)

    gate = gate_of(zt, 0)
    triangle = exchange(*triangle_call([exchange(sent)], 1, blocks, side, own, False))
    mask = jnp.concatenate(m_pieces, axis=1)
    sent, zt = pixel_call(
        functools.partial(middle_kernel, peers),
        [(a, 0, steps, False) for a in (triangle, zt, gate, mask)], fixed, (2 * width, channels),
        steps, wide, pixels * mult * 5 * width,
    )
    gate = gate_of(zt, 1)
    products = triangle_call([exchange(sent)], 2, blocks, side, own, True)

    def finish(piece, triangle):
        at = piece * steps // 2
        return pixel_call(
            last_kernel,
            [(triangle, 0, steps // 2, False), (zt, at, steps, False), (gate, at, steps, False)],
            fixed, (channels,), steps // 2, wide, pixels // 2 * mult * channels, row_major_out=True,
        )[0]

    there = finish(1, exchange(products[1]))
    beside, across = (
        lax.ppermute(there, LINE, pairs) for pairs in (((0, 1), (3, 2)), ((1, 2), (2, 1)))
    )
    there, waiting = lax.optimization_barrier((there, products[0]))
    here = finish(0, exchange(waiting))
    back = lax.ppermute(here, LINE, ((1, 3), (2, 0)))
    place = jnp.stack([upper, home.astype(upper.dtype)])
    per_half = steps // 2

    def source(of_mine, at_home):
        def index(i, place_ref):
            wanted = jnp.logical_and(
                (i // per_half == place_ref[0]) == of_mine, (place_ref[1] == 1) == at_home
            )
            return jnp.where(wanted, lax.rem(i, per_half), 0), 0

        return pl.BlockSpec((wide, channels), index)

    return pl.pallas_call(
        functools.partial(assemble_kernel, per_half),
        grid_spec=pltpu.PrefetchScalarGridSpec(
            num_scalar_prefetch=1,
            grid=(steps,),
            in_specs=[source(*w) for w in ((True, True), (True, False), (False, True), (False, False))],
            out_specs=pl.BlockSpec((wide, channels), lambda i, place_ref: (i, 0)),
        ),
        out_shape=jax.ShapeDtypeStruct((pixels, channels), jnp.bfloat16),
    )(place, here, beside, back, across).reshape(side, side, channels)


def layer_norm(values, gain, bias, axis):
    average = jnp.mean(values, axis=axis, keepdims=True)
    centred = values - average
    spread_sq = jnp.mean(centred * centred, axis=axis, keepdims=True)
    return centred * lax.rsqrt(spread_sq + 1e-05) * gain + bias


def triangle_update(
    pair_act,
    mask_float,
    layer_index,
    input_gain,
    input_bias,
    project_weight,
    gate_weight,
    output_gain,
    output_bias,
    output_weight,
    incoming,
):
    rows, cols = lax.axis_size("row"), lax.axis_size("col")
    peers = rows * cols
    rows_here, cols_here, channels_here = pair_act.shape
    width = output_weight.shape[1]
    own = width // peers
    pixels = rows_here * cols_here
    pair_float = pair_act.astype(jnp.float32).reshape(pixels, channels_here)
    normed = layer_norm(
        pair_float, input_gain[layer_index], input_bias[layer_index], -1
    ).astype(jnp.bfloat16)
    projected = lax.dot_general(
        project_weight[layer_index],
        normed,
        (((0,), (1,)), ((), ())),
        preferred_element_type=jnp.float32,
    ).reshape(4, peers, own, pixels)
    mask_row = mask_float.reshape(1, 1, pixels)
    left_proj = (jax.nn.sigmoid(projected[0]) * projected[1] * mask_row).astype(jnp.bfloat16)
    right_proj = (jax.nn.sigmoid(projected[2]) * projected[3] * mask_row).astype(jnp.bfloat16)
    both = jnp.concatenate([left_proj, right_proj], axis=1)
    both = lax.all_to_all(both, GRID, 0, 0)
    both = both.reshape(rows, cols, 2, own, rows_here, cols_here)
    both = both.transpose(2, 3, 0, 4, 1, 5).reshape(2, own, rows * rows_here, cols * cols_here)
    spec = "cki,ckj->cij" if incoming else "cik,cjk->cij"
    triangle = jnp.einsum(spec, both[0], both[1], preferred_element_type=jnp.float32)
    triangle = triangle.astype(jnp.bfloat16).reshape(own, rows, rows_here, cols, cols_here)
    triangle = triangle.transpose(1, 3, 0, 2, 4).reshape(peers, own, pixels)
    triangle = lax.all_to_all(triangle, GRID, 0, 0).reshape(width, pixels)
    normed_sum = layer_norm(
        triangle.astype(jnp.float32),
        output_gain[layer_index][:, None],
        output_bias[layer_index][:, None],
        0,
    ).astype(jnp.bfloat16)
    gate_value = jax.nn.sigmoid(
        jnp.dot(normed, gate_weight[layer_index], preferred_element_type=jnp.float32)
    )
    mapped = lax.dot_general(
        normed_sum,
        output_weight[layer_index],
        (((0,), (0,)), ((), ())),
        preferred_element_type=jnp.float32,
    )
    return (
        (pair_float + gate_value * mapped)
        .astype(jnp.bfloat16)
        .reshape(rows_here, cols_here, channels_here)
    )


def shards(pair_act, pair_mask, *params):
    mask_float = pair_mask.astype(jnp.float32)
    for index in range(2):
        pair_act = triangle_update(pair_act, mask_float, index, *params, index == 1)
    return pair_act


def solution(mesh):
    def updates(pair_act, pair_mask, *params):
        body, grid, cols = shards, mesh, "col"
        if fits(mesh, pair_act.shape[1], params[-1].shape[1]):
            sizes = mesh.devices.shape
            grid = jax.sharding.Mesh(
                mesh.devices.reshape(*sizes[:2], 2, sizes[2] // 2), ("groups", "row", "zh", "zl")
            )
            body, cols = by_kernels, ("zh", "zl")
        pixels = (("groups", "row"), cols)
        return jax.shard_map(
            body,
            mesh=grid,
            in_specs=(P(*pixels, None), P(*pixels)) + (P(),) * 7,
            out_specs=P(*pixels, None),
            check_vma=False,
        )(pair_act, pair_mask, *params)

    return updates
```

```python
import functools

import jax
import jax.numpy as jnp
from jax import lax
from jax.experimental import pallas as pl
from jax.experimental.pallas import tpu as pltpu
from jax.sharding import PartitionSpec as P

GRID = ("row", "col")
LANES = 128


IN_GAIN, IN_BIAS, OUT_GAIN, OUT_BIAS = range(4)


def channel_norm(values, gain, bias):
    average = jnp.mean(values, axis=0, keepdims=True)
    centred = values - average
    spread_sq = jnp.mean(centred * centred, axis=0, keepdims=True)
    return centred * lax.rsqrt(spread_sq + 1e-05) * gain + bias


def dot(left, right):
    return jnp.dot(left, right, preferred_element_type=jnp.float32)


def norm_of(values, small_ref, update, which):
    at = 4 * update + which
    return channel_norm(values, small_ref[:, at : at + 1], small_ref[:, at + 1 : at + 2])


def emit_projections(peers, update, zt, mask, small_ref, weight_ref, lr_ref):
    width = lr_ref.shape[0] // 2
    own = width // peers
    tile = zt.shape[1]
    normed = norm_of(zt, small_ref, update, IN_GAIN) * mask
    projected = dot(weight_ref[update, : 4 * width], normed.astype(jnp.bfloat16))
    left = (jnp.tanh(projected[:width]) + 1.0) * projected[width : 2 * width]
    right = (jnp.tanh(projected[2 * width : 3 * width]) + 1.0) * projected[3 * width :]
    both = jnp.concatenate(
        [left.reshape(peers, own, tile), right.reshape(peers, own, tile)], axis=1
    )
    lr_ref[...] = both.reshape(2 * width, tile).astype(jnp.bfloat16)


def pack_kernel(cuts, place_ref, own_ref, own_mask_ref, other_ref, other_mask_ref, *out_refs):
    part_refs, (own_out_ref, next_ref) = out_refs[:-2], out_refs[-2:]
    step = pl.program_id(0)
    size = own_ref.shape[0]

    def put(out_ref, ref, mask_ref):
        out_ref[0, :size] = ref[...]
        out_ref[0, size:] = mask_ref[0]

    put(own_out_ref, own_ref, own_mask_ref)
    pl.when(place_ref[1] == 1)(lambda: put(next_ref, other_ref, other_mask_ref))
    pl.when(place_ref[1] != 1)(lambda: put(next_ref, own_ref, own_mask_ref))
    for begin, end, part_ref in zip((0, *cuts), cuts, part_refs):
        pl.when(jnp.logical_and(step >= begin, step < end))(
            functools.partial(put, part_ref, other_ref, other_mask_ref)
        )


def first_kernel(peers, parts, own_ref, *refs):
    far_refs, (small_ref, weight_ref), (lr_ref, zt_ref, mask_ref) = (
        refs[: len(parts)], refs[len(parts) : -3], refs[-3:],
    )
    home = lax.axis_index("groups") == lax.axis_index("zh")
    step = pl.program_id(0)
    tile = zt_ref.shape[1]

    def put(z_ref):
        zt_ref[...] = z_ref[0, :tile].astype(jnp.float32).T.astype(jnp.bfloat16)
        marks = z_ref[0, tile:].astype(jnp.float32)
        flat = jnp.concatenate([marks[k : k + 1] for k in range(tile // LANES)], axis=1)
        mask_ref[...] = jnp.broadcast_to(flat, mask_ref.shape).astype(jnp.bfloat16)

    pl.when(home)(lambda: put(own_ref))
    for (begin, end), far_ref in zip(parts, far_refs):
        here = jnp.logical_and(step >= begin, step < end)
        pl.when(jnp.logical_and(jnp.logical_not(home), here))(functools.partial(put, far_ref))
    zt = zt_ref[...].astype(jnp.float32)
    mask = mask_ref[...].astype(jnp.float32)[:1]
    emit_projections(peers, 0, zt, mask, small_ref, weight_ref, lr_ref)


def gate_kernel(update, zt_ref, small_ref, weight_ref, gate_ref):
    channels = gate_ref.shape[0]
    normed = norm_of(zt_ref[...].astype(jnp.float32), small_ref, update, IN_GAIN)
    at = weight_ref.shape[1] - 2 * channels
    gates = dot(weight_ref[update, at : at + channels], normed.astype(jnp.bfloat16))
    gate_ref[...] = (0.5 * jnp.tanh(gates) + 0.5).astype(jnp.bfloat16)


def updated(update, t_ref, zt_ref, gate_ref, small_ref, weight_ref):
    normed_sum = norm_of(t_ref[...].astype(jnp.float32), small_ref, update, OUT_GAIN)
    at = weight_ref.shape[1] - zt_ref.shape[0]
    mapped = dot(weight_ref[update, at:], normed_sum.astype(jnp.bfloat16))
    return zt_ref[...].astype(jnp.float32) + gate_ref[...].astype(jnp.float32) * mapped


def middle_kernel(
    peers, t_ref, zt_ref, gate_ref, mask_ref, small_ref, weight_ref, lr_ref, out_ref
):
    fresh = updated(0, t_ref, zt_ref, gate_ref, small_ref, weight_ref).astype(jnp.bfloat16)
    out_ref[...] = fresh
    mask = mask_ref[...].astype(jnp.float32)[:1]
    emit_projections(peers, 1, fresh.astype(jnp.float32), mask, small_ref, weight_ref, lr_ref)


def last_kernel(t_ref, zt_ref, gate_ref, small_ref, weight_ref, out_ref):
    fresh = updated(1, t_ref, zt_ref, gate_ref, small_ref, weight_ref)
    out_ref[...] = fresh.T.astype(jnp.bfloat16)


def assemble_kernel(per_half, place_ref, here_ref, beside_ref, back_ref, across_ref, out_ref):
    mine = pl.program_id(0) // per_half == place_ref[0]
    home = place_ref[1] == 1
    for side_of, whose, ref in (
        (home, mine, here_ref),
        (jnp.logical_not(home), mine, beside_ref),
        (home, jnp.logical_not(mine), back_ref),
        (jnp.logical_not(home), jnp.logical_not(mine), across_ref),
    ):

        @pl.when(jnp.logical_and(side_of, whose))
        def _put(ref=ref):
            out_ref[...] = ref[...]


def triangle_kernel(blocks, side, own, incoming, n_in, *refs):
    x_refs, y_refs, (left_ref, right_ref, rows_ref, tiles_ref) = refs[:n_in], refs[n_in:-4], refs[-4:]
    step = pl.program_id(0)
    zh = lax.axis_index("zh")
    pair = 2 * own
    span = 4 * side
    strip = side // 2
    half = blocks // 2
    pitch_rows = pair + 1
    lane = lax.broadcasted_iota(jnp.int32, (pair, LANES), 1)
    inside = lane < side

    def piece_of(piece_refs, piece):
        if len(piece_refs) == 1:
            return piece_refs[0], piece * strip * side
        return piece_refs[piece], 0

    @pl.when(step < blocks)
    def _unpack():
        upper, row_pair = step // half, lax.rem(step, half)
        mirror = lax.rem(row_pair + zh, 2)
        for r in range(2):
            at = pl.multiple_of((row_pair * 2 + r) * side + upper * strip, 16)
            if incoming:
                at_right = at
            else:
                at_right = pl.multiple_of((mirror * 2 + r) * LANES + upper * strip, 16)
            for zl in range(half):
                for piece in range(2):
                    x_ref, first = piece_of(x_refs, piece)
                    for group in range(strip // 4):
                        x = x_ref[
                            (r * half + zl) * pair : (r * half + zl + 1) * pair,
                            first + group * span : first + (group + 1) * span,
                        ].astype(jnp.float32)
                        a, b, c = x[:, :LANES], x[:, LANES : 2 * LANES], x[:, 2 * LANES :]
                        picked = (
                            a,
                            pltpu.roll(jnp.where(lane >= 96, a, b), 32, 1),
                            pltpu.roll(jnp.where(lane >= 64, b, c), 64, 1),
                            pltpu.roll(c, 96, 1),
                        )
                        for k, row in enumerate(picked):
                            rows_ref[pl.ds((group * 4 + k) * pitch_rows, pair), :] = jnp.where(
                                inside, row, 0.0
                            )
                    lanes = slice((piece * half + zl) * LANES, (piece * half + zl + 1) * LANES)
                    for ch in range(own):
                        left_ref[ch, pl.ds(at, strip), lanes] = rows_ref[
                            pl.ds(ch, strip, stride=pitch_rows), :
                        ].astype(jnp.bfloat16)
                        right_ref[ch, pl.ds(at_right, strip), lanes] = rows_ref[
                            pl.ds(own + ch, strip, stride=pitch_rows), :
                        ].astype(jnp.bfloat16)

    @pl.when(step == blocks - 1)
    def _multiply():
        contract = ((0,), (0,)) if incoming else ((1,), (1,))
        for ch in range(own):
            product = lax.dot_general(
                left_ref[ch], right_ref[ch], (contract, ((), ())), preferred_element_type=jnp.float32
            )
            for place in range(blocks):
                if incoming:
                    row, pitch = lax.rem(place // 2 + zh, 2) * 2 + place % 2, LANES
                else:
                    row, pitch = place, side
                for upper in range(2):
                    for col in range(blocks):
                        tiles_ref[
                            col // half,
                            upper * blocks + row,
                            pl.ds((col % half) * own + ch, strip, stride=pitch_rows),
                            :,
                        ] = product[
                            place * pitch + upper * strip : place * pitch + (upper + 1) * strip,
                            col * LANES : (col + 1) * LANES,
                        ]

    @pl.when(step >= blocks)
    def _repack():
        for r in range(2):
            place = (step - blocks) * 2 + r
            for piece in range(2):
                y_ref, first = piece_of(y_refs, piece)
                for group in range(strip // 4):
                    p, q, t, s = (
                        tiles_ref[piece, place, pl.ds((group * 4 + k) * pitch_rows, pair), :]
                        for k in range(4)
                    )
                    q, t, s = pltpu.roll(q, 96, 1), pltpu.roll(t, 64, 1), pltpu.roll(s, 32, 1)
                    flat = jnp.concatenate(
                        [
                            jnp.where(inside, p, q),
                            jnp.where(lane < 64, q, t),
                            jnp.where(lane < 32, t, s),
                        ],
                        axis=1,
                    )
                    y_ref[
                        r * pair : (r + 1) * pair, first + group * span : first + (group + 1) * span
                    ] = flat.astype(jnp.bfloat16)


def fits(mesh, residues, width):
    rows, cols = mesh.shape["row"], mesh.shape["col"]
    return (
        mesh.shape["groups"] == 2
        and rows == 4
        and cols == 4
        and 4 * residues == 3 * LANES * cols
        and width == 8 * rows * cols
    )


def whole_spec(array):
    return pl.BlockSpec(array.shape, lambda i: (0,) * array.ndim)


def triangle_call(received, n_out, blocks, side, own, incoming):
    pair = 2 * own
    pixels = side * side
    padded = blocks * LANES
    strip = side // 2
    left_rows = blocks * side
    right_rows = left_rows if incoming else padded
    return pl.pallas_call(
        functools.partial(triangle_kernel, blocks, side, own, incoming, len(received)),
        grid=(2 * blocks,),
        in_specs=[
            pl.BlockSpec((blocks * pair, a.shape[1]), lambda i: (jnp.minimum(i, blocks - 1), 0))
            for a in received
        ],
        out_specs=[
            pl.BlockSpec((2 * pair, pixels // n_out), lambda i: (jnp.maximum(i - blocks, 0), 0))
        ] * n_out,
        out_shape=[
            pltpu.HBM((blocks * blocks * own, pixels // n_out), jnp.bfloat16)
        ] * n_out,
        scratch_shapes=[
            pltpu.VMEM((own, left_rows, padded), jnp.bfloat16),
            pltpu.VMEM((own, right_rows, padded), jnp.bfloat16),
            pltpu.VMEM((strip * (pair + 1), LANES), jnp.float32),
            pltpu.VMEM((2, 2 * blocks, strip * (pair + 1), LANES), jnp.float32),
        ],
        compiler_params=pltpu.CompilerParams(vmem_limit_bytes=48 * 1024 * 1024),
        cost_estimate=pl.CostEstimate(
            flops=2 * own * (blocks * side) ** 3,
            bytes_accessed=12 * blocks * blocks * pair * pixels // 2,
            transcendentals=0,
        ),
    )(*received)


def pixel_call(body, tiled, fixed, outs, steps, tile, flops, start=0, pixels=None, kept=(), scratch=(), row_major_out=False):
    pixels = pixels or steps * tile

    def spec(channels, first, count, row_major):
        if row_major:
            return pl.BlockSpec(
                (tile, channels), lambda i: (jnp.clip(i + first, 0, count - 1), 0)
            )
        return pl.BlockSpec((channels, tile), lambda i: (0, jnp.clip(i + first, 0, count - 1)))

    def packed(a, first, count):
        return pl.BlockSpec(
            (1, *a.shape[1:]), lambda i: (jnp.clip(i + first, 0, count - 1), 0, 0)
        )

    in_specs = [
        packed(a, first, count) if a.ndim == 3 else spec(a.shape[0], first, count, False)
        for a, first, count in tiled
    ]
    in_specs += [whole_spec(a) for a in fixed]
    in_specs += [pl.BlockSpec(memory_space=pl.ANY)] * len(kept)
    n_in, n_kept = len(in_specs), len(kept)

    def kernel(*refs):
        body(*refs[: n_in - n_kept], *refs[n_in:])

    return pl.pallas_call(
        kernel,
        grid=(steps,),
        in_specs=in_specs,
        out_specs=[spec(ch, start, pixels // tile, row_major_out) for ch in outs],
        out_shape=[
            pltpu.HBM((pixels, ch) if row_major_out else (ch, pixels), jnp.bfloat16)
            for ch in outs
        ],
        input_output_aliases={n_in - n_kept + k: k for k in range(n_kept)},
        scratch_shapes=list(scratch),
        compiler_params=pltpu.CompilerParams(vmem_limit_bytes=48 * 1024 * 1024),
        cost_estimate=pl.CostEstimate(
            flops=flops, bytes_accessed=2 * steps * tile * (sum(outs) + 256), transcendentals=0
        ),
    )(*(a for a, *_ in tiled), *fixed, *kept)


LINE = ("groups", "zh")
CUBE = ("groups", "row", "zl")


def pack(pair_act, mask, place, cuts, tile):
    per_strip = cuts[-1]
    channels = pair_act.shape[1]
    rows = tile + mask.shape[1]

    def strip(other, blocks):
        index = lambda i, place_ref: jnp.abs(other - place_ref[0]) * per_strip + i
        if blocks:
            return pl.BlockSpec((1, *mask.shape[1:]), lambda i, p: (index(i, p), 0, 0))
        return pl.BlockSpec((tile, channels), lambda i, p: (index(i, p), 0))

    def part(begin, end):
        return pl.BlockSpec(
            (1, rows, channels), lambda i, p: (jnp.clip(i - begin, 0, end - begin - 1), 0, 0)
        )

    outs = [*zip((0, *cuts), cuts), (0, per_strip), (0, per_strip)]
    return pl.pallas_call(
        functools.partial(pack_kernel, cuts),
        grid_spec=pltpu.PrefetchScalarGridSpec(
            num_scalar_prefetch=1,
            grid=(per_strip,),
            in_specs=[strip(0, False), strip(0, True), strip(1, False), strip(1, True)],
            out_specs=[part(*o) for o in outs],
        ),
        out_shape=[pltpu.HBM((end - begin, rows, channels), jnp.bfloat16) for begin, end in outs],
    )(place, pair_act, mask, pair_act, mask)


def by_kernels(
    pair_act,
    pair_mask,
    input_gain,
    input_bias,
    project_weight,
    gate_weight,
    output_gain,
    output_bias,
    output_weight,
):
    blocks = lax.axis_size("row")
    peers = blocks * blocks
    side, _, channels = pair_act.shape
    width = output_weight.shape[1]
    own = width // peers
    pixels = side * side
    strip = side // 2
    upper = lax.axis_index("groups")
    home = upper == lax.axis_index("zh")
    mult = 2 * channels

    place = jnp.stack([upper, home.astype(upper.dtype)])
    tile = 9 * LANES
    per_piece = pixels // 2 // tile
    cuts = (1, per_piece - 1, per_piece)
    marks = pair_mask.astype(jnp.bfloat16).reshape(2 * per_piece, tile // LANES, LANES)
    marks = jnp.pad(marks, ((0, 0), (0, 16 - tile // LANES), (0, 0)))
    *z_parts, z_own, z_next = pack(pair_act.reshape(pixels, channels), marks, place, cuts, tile)
    z_far = []
    for part in z_parts[:-1]:
        over = lax.ppermute(part, LINE, ((1, 3), (2, 0)))
        z_far.append(lax.ppermute(over, LINE, ((0, 1), (3, 2))))
    z_near = lax.ppermute(z_next, LINE, ((1, 0), (2, 3), (0, 2), (3, 1)))
    z_far.append(lax.ppermute(z_parts[-1], LINE, ((1, 2), (2, 1))))
    small = jnp.stack([input_gain, input_bias, output_gain, output_bias], axis=1)
    small = small.reshape(-1, channels).T
    weights = jnp.concatenate(
        [project_weight * 0.5, gate_weight * 0.5, output_weight], axis=2
    ).transpose(0, 2, 1)
    fixed = (small, weights)

    def first(piece, ours, far, parts, kept):
        tiled = [(ours, 0, per_piece)]
        tiled += [(part, -begin, end - begin) for part, (begin, end) in zip(far, parts)]
        return pixel_call(
            functools.partial(first_kernel, peers, parts),
            tiled, fixed, (2 * width, channels, 16), per_piece, tile, pixels // 2 * mult * 4 * width,
            start=piece * per_piece, pixels=pixels, kept=kept,
        )

    begun = first(0, z_own, [z_near], [(0, per_piece)], ())
    sent, zt, mask = first(1, z_near, z_far, list(zip((0, *cuts), cuts)), begun)
    wide = 2 * tile
    steps = pixels // wide

    def gate_of(zt, u):
        return pixel_call(
            functools.partial(gate_kernel, u), [(zt, 0, steps)], fixed, (channels,),
            steps, wide, pixels * mult * channels,
        )[0]

    def exchange(array):
        there = lax.all_to_all(array.reshape(peers, -1, array.shape[1]), CUBE, 0, 0)
        return there.reshape(array.shape)

    gate = gate_of(zt, 0)
    triangle = exchange(*triangle_call([exchange(sent)], 1, blocks, side, own, False))
    sent, zt = pixel_call(
        functools.partial(middle_kernel, peers),
        [(a, 0, steps) for a in (triangle, zt, gate, mask)], fixed, (2 * width, channels),
        steps, wide, pixels * mult * 5 * width,
    )
    gate = gate_of(zt, 1)
    products = triangle_call([exchange(sent)], 2, blocks, side, own, True)

    def finish(piece, triangle):
        at = piece * steps // 2
        return pixel_call(
            last_kernel,
            [(triangle, 0, steps // 2), (zt, at, steps), (gate, at, steps)],
            fixed, (channels,), steps // 2, wide, pixels // 2 * mult * channels, row_major_out=True,
        )[0]

    there = finish(1, exchange(products[1]))
    beside, across = (
        lax.ppermute(there, LINE, pairs) for pairs in (((0, 1), (3, 2)), ((1, 2), (2, 1)))
    )
    there, waiting = lax.optimization_barrier((there, products[0]))
    here = finish(0, exchange(waiting))
    back = lax.ppermute(here, LINE, ((1, 3), (2, 0)))
    per_half = steps // 2

    def source(of_mine, at_home):
        def index(i, place_ref):
            wanted = jnp.logical_and(
                (i // per_half == place_ref[0]) == of_mine, (place_ref[1] == 1) == at_home
            )
            return jnp.where(wanted, lax.rem(i, per_half), 0), 0

        return pl.BlockSpec((wide, channels), index)

    return pl.pallas_call(
        functools.partial(assemble_kernel, per_half),
        grid_spec=pltpu.PrefetchScalarGridSpec(
            num_scalar_prefetch=1,
            grid=(steps,),
            in_specs=[source(*w) for w in ((True, True), (True, False), (False, True), (False, False))],
            out_specs=pl.BlockSpec((wide, channels), lambda i, place_ref: (i, 0)),
        ),
        out_shape=jax.ShapeDtypeStruct((pixels, channels), jnp.bfloat16),
    )(place, here, beside, back, across).reshape(side, side, channels)


def layer_norm(values, gain, bias, axis):
    average = jnp.mean(values, axis=axis, keepdims=True)
    centred = values - average
    spread_sq = jnp.mean(centred * centred, axis=axis, keepdims=True)
    return centred * lax.rsqrt(spread_sq + 1e-05) * gain + bias


def triangle_update(
    pair_act,
    mask_float,
    layer_index,
    input_gain,
    input_bias,
    project_weight,
    gate_weight,
    output_gain,
    output_bias,
    output_weight,
    incoming,
):
    rows, cols = lax.axis_size("row"), lax.axis_size("col")
    peers = rows * cols
    rows_here, cols_here, channels_here = pair_act.shape
    width = output_weight.shape[1]
    own = width // peers
    pixels = rows_here * cols_here
    pair_float = pair_act.astype(jnp.float32).reshape(pixels, channels_here)
    normed = layer_norm(
        pair_float, input_gain[layer_index], input_bias[layer_index], -1
    ).astype(jnp.bfloat16)
    projected = lax.dot_general(
        project_weight[layer_index],
        normed,
        (((0,), (1,)), ((), ())),
        preferred_element_type=jnp.float32,
    ).reshape(4, peers, own, pixels)
    mask_row = mask_float.reshape(1, 1, pixels)
    left_proj = (jax.nn.sigmoid(projected[0]) * projected[1] * mask_row).astype(jnp.bfloat16)
    right_proj = (jax.nn.sigmoid(projected[2]) * projected[3] * mask_row).astype(jnp.bfloat16)
    both = jnp.concatenate([left_proj, right_proj], axis=1)
    both = lax.all_to_all(both, GRID, 0, 0)
    both = both.reshape(rows, cols, 2, own, rows_here, cols_here)
    both = both.transpose(2, 3, 0, 4, 1, 5).reshape(2, own, rows * rows_here, cols * cols_here)
    spec = "cki,ckj->cij" if incoming else "cik,cjk->cij"
    triangle = jnp.einsum(spec, both[0], both[1], preferred_element_type=jnp.float32)
    triangle = triangle.astype(jnp.bfloat16).reshape(own, rows, rows_here, cols, cols_here)
    triangle = triangle.transpose(1, 3, 0, 2, 4).reshape(peers, own, pixels)
    triangle = lax.all_to_all(triangle, GRID, 0, 0).reshape(width, pixels)
    normed_sum = layer_norm(
        triangle.astype(jnp.float32),
        output_gain[layer_index][:, None],
        output_bias[layer_index][:, None],
        0,
    ).astype(jnp.bfloat16)
    gate_value = jax.nn.sigmoid(
        jnp.dot(normed, gate_weight[layer_index], preferred_element_type=jnp.float32)
    )
    mapped = lax.dot_general(
        normed_sum,
        output_weight[layer_index],
        (((0,), (0,)), ((), ())),
        preferred_element_type=jnp.float32,
    )
    return (
        (pair_float + gate_value * mapped)
        .astype(jnp.bfloat16)
        .reshape(rows_here, cols_here, channels_here)
    )


def shards(pair_act, pair_mask, *params):
    mask_float = pair_mask.astype(jnp.float32)
    for index in range(2):
        pair_act = triangle_update(pair_act, mask_float, index, *params, index == 1)
    return pair_act


def solution(mesh):
    def updates(pair_act, pair_mask, *params):
        body, grid, cols = shards, mesh, "col"
        if fits(mesh, pair_act.shape[1], params[-1].shape[1]):
            sizes = mesh.devices.shape
            grid = jax.sharding.Mesh(
                mesh.devices.reshape(*sizes[:2], 2, sizes[2] // 2), ("groups", "row", "zh", "zl")
            )
            body, cols = by_kernels, ("zh", "zl")
        pixels = (("groups", "row"), cols)
        return jax.shard_map(
            body,
            mesh=grid,
            in_specs=(P(*pixels, None), P(*pixels)) + (P(),) * 7,
            out_specs=P(*pixels, None),
            check_vma=False,
        )(pair_act, pair_mask, *params)

    return updates
```

```python
import functools

import jax
import jax.numpy as jnp
from jax import lax
from jax.experimental import pallas as pl
from jax.experimental.pallas import tpu as pltpu
from jax.sharding import PartitionSpec as P

GRID = ("row", "col")
LANES = 128


IN_GAIN, IN_BIAS, OUT_GAIN, OUT_BIAS = range(4)


def channel_norm(values, gain, bias):
    average = jnp.mean(values, axis=0, keepdims=True)
    centred = values - average
    spread_sq = jnp.mean(centred * centred, axis=0, keepdims=True)
    return centred * lax.rsqrt(spread_sq + 1e-05) * gain + bias


def dot(left, right):
    return jnp.dot(left, right, preferred_element_type=jnp.float32)


def norm_of(values, small_ref, update, which):
    at = 4 * update + which
    return channel_norm(values, small_ref[:, at : at + 1], small_ref[:, at + 1 : at + 2])


def emit_projections(peers, update, zt, mask, small_ref, weight_ref, lr_ref):
    width = lr_ref.shape[0] // 2
    own = width // peers
    tile = zt.shape[1]
    normed = norm_of(zt, small_ref, update, IN_GAIN) * mask
    projected = dot(weight_ref[update, : 4 * width], normed.astype(jnp.bfloat16))
    left = (jnp.tanh(projected[:width]) + 1.0) * projected[width : 2 * width]
    right = (jnp.tanh(projected[2 * width : 3 * width]) + 1.0) * projected[3 * width :]
    both = jnp.concatenate(
        [left.reshape(peers, own, tile), right.reshape(peers, own, tile)], axis=1
    )
    lr_ref[...] = both.reshape(2 * width, tile).astype(jnp.bfloat16)


def pack_kernel(cuts, tile, z_ref, mask_ref, *refs):
    out_refs, (held_ref, z_sems, mask_sems, out_sems) = refs[:-4], refs[-4:]
    part_refs, (own_ref, next_ref) = out_refs[:-2], out_refs[-2:]
    upper = lax.axis_index("groups")
    home = upper == lax.axis_index("zh")
    per_strip = cuts[-1]
    rows = held_ref.shape[2]
    fetches = []
    for which in range(2):
        strip = lax.rem(upper + 1 - which, 2)
        for t in range(per_strip):
            at = pl.multiple_of((strip * per_strip + t) * tile, tile)
            fetches.append(
                pltpu.make_async_copy(
                    z_ref.at[pl.ds(at, tile)], held_ref.at[which, t, 0:tile], z_sems.at[which, t]
                )
            )
            fetches.append(
                pltpu.make_async_copy(
                    mask_ref.at[strip * per_strip + t], held_ref.at[which, t, tile:rows],
                    mask_sems.at[which, t],
                )
            )
    stores = [
        pltpu.make_async_copy(held_ref.at[0, begin:end], part_ref, out_sems.at[k])
        for k, (begin, end, part_ref) in enumerate(zip((0, *cuts), cuts, part_refs))
    ]
    stores += [
        pltpu.make_async_copy(held_ref.at[1], own_ref, out_sems.at[len(cuts)]),
        pltpu.make_async_copy(
            held_ref.at[1 - home.astype(jnp.int32)], next_ref, out_sems.at[len(cuts) + 1]
        ),
    ]
    for fetch in fetches:
        fetch.start()
    for fetch in fetches[: 2 * per_strip]:
        fetch.wait()
    for store in stores[: len(cuts)]:
        store.start()
    for fetch in fetches[2 * per_strip :]:
        fetch.wait()
    for store in stores[len(cuts) :]:
        store.start()
    for store in stores:
        store.wait()


def first_kernel(peers, parts, own_ref, *refs):
    far_refs, (small_ref, weight_ref), (lr_ref, zt_ref, mask_ref) = (
        refs[: len(parts)], refs[len(parts) : -3], refs[-3:],
    )
    home = lax.axis_index("groups") == lax.axis_index("zh")
    step = pl.program_id(0)
    tile = zt_ref.shape[1]

    def put(z_ref):
        zt_ref[...] = z_ref[0, :tile].astype(jnp.float32).T.astype(jnp.bfloat16)
        marks = z_ref[0, tile:].astype(jnp.float32)
        flat = jnp.concatenate([marks[k : k + 1] for k in range(tile // LANES)], axis=1)
        mask_ref[...] = jnp.broadcast_to(flat, mask_ref.shape).astype(jnp.bfloat16)

    pl.when(home)(lambda: put(own_ref))
    for (begin, end), far_ref in zip(parts, far_refs):
        here = jnp.logical_and(step >= begin, step < end)
        pl.when(jnp.logical_and(jnp.logical_not(home), here))(functools.partial(put, far_ref))
    zt = zt_ref[...].astype(jnp.float32)
    mask = mask_ref[...].astype(jnp.float32)[:1]
    emit_projections(peers, 0, zt, mask, small_ref, weight_ref, lr_ref)


def gate_kernel(update, zt_ref, small_ref, weight_ref, gate_ref):
    channels = gate_ref.shape[0]
    normed = norm_of(zt_ref[...].astype(jnp.float32), small_ref, update, IN_GAIN)
    at = weight_ref.shape[1] - 2 * channels
    gates = dot(weight_ref[update, at : at + channels], normed.astype(jnp.bfloat16))
    gate_ref[...] = (0.5 * jnp.tanh(gates) + 0.5).astype(jnp.bfloat16)


def updated(update, t_ref, zt_ref, gate_ref, small_ref, weight_ref):
    normed_sum = norm_of(t_ref[...].astype(jnp.float32), small_ref, update, OUT_GAIN)
    at = weight_ref.shape[1] - zt_ref.shape[0]
    mapped = dot(weight_ref[update, at:], normed_sum.astype(jnp.bfloat16))
    return zt_ref[...].astype(jnp.float32) + gate_ref[...].astype(jnp.float32) * mapped


def middle_kernel(
    peers, t_ref, zt_ref, gate_ref, mask_ref, small_ref, weight_ref, lr_ref, out_ref
):
    fresh = updated(0, t_ref, zt_ref, gate_ref, small_ref, weight_ref).astype(jnp.bfloat16)
    out_ref[...] = fresh
    mask = mask_ref[...].astype(jnp.float32)[:1]
    emit_projections(peers, 1, fresh.astype(jnp.float32), mask, small_ref, weight_ref, lr_ref)


def last_kernel(t_ref, zt_ref, gate_ref, small_ref, weight_ref, out_ref):
    fresh = updated(1, t_ref, zt_ref, gate_ref, small_ref, weight_ref)
    out_ref[...] = fresh.T.astype(jnp.bfloat16)


def assemble_kernel(here_ref, beside_ref, back_ref, across_ref, out_ref, held_ref, in_sems, out_sems):
    upper = lax.axis_index("groups")
    home = upper == lax.axis_index("zh")
    parts = in_sems.shape[1]
    size = here_ref.shape[0] // parts

    def move(*sources):
        pieces = [(which, k, slice(k * size, (k + 1) * size)) for k in range(parts) for which in range(2)]
        fetches = [
            pltpu.make_async_copy(
                sources[which].at[rows], held_ref.at[which, rows], in_sems.at[which, k]
            )
            for which, k, rows in pieces
        ]
        stores = [
            pltpu.make_async_copy(
                held_ref.at[which, rows], out_ref.at[lax.rem(upper + which, 2), rows],
                out_sems.at[which, k],
            )
            for which, k, rows in pieces
        ]
        for fetch in fetches:
            fetch.start()
        for fetch, store in zip(fetches, stores):
            fetch.wait()
            store.start()
        for store in stores:
            store.wait()

    pl.when(home)(lambda: move(here_ref, back_ref))
    pl.when(jnp.logical_not(home))(lambda: move(beside_ref, across_ref))


def triangle_kernel(blocks, side, own, incoming, n_in, *refs):
    x_refs, y_refs, (left_ref, right_ref, rows_ref, tiles_ref) = refs[:n_in], refs[n_in:-4], refs[-4:]
    step = pl.program_id(0)
    zh = lax.axis_index("zh")
    pair = 2 * own
    span = 4 * side
    strip = side // 2
    half = blocks // 2
    pitch_rows = pair + 1
    lane = lax.broadcasted_iota(jnp.int32, (pair, LANES), 1)
    inside = lane < side

    def piece_of(piece_refs, piece):
        if len(piece_refs) == 1:
            return piece_refs[0], piece * strip * side
        return piece_refs[piece], 0

    @pl.when(step < blocks)
    def _unpack():
        upper, row_pair = step // half, lax.rem(step, half)
        mirror = lax.rem(row_pair + zh, 2)
        for r in range(2):
            at = pl.multiple_of((row_pair * 2 + r) * side + upper * strip, 16)
            if incoming:
                at_right = at
            else:
                at_right = pl.multiple_of((mirror * 2 + r) * LANES + upper * strip, 16)
            for zl in range(half):
                for piece in range(2):
                    x_ref, first = piece_of(x_refs, piece)
                    for group in range(strip // 4):
                        x = x_ref[
                            (r * half + zl) * pair : (r * half + zl + 1) * pair,
                            first + group * span : first + (group + 1) * span,
                        ].astype(jnp.float32)
                        a, b, c = x[:, :LANES], x[:, LANES : 2 * LANES], x[:, 2 * LANES :]
                        picked = (
                            a,
                            pltpu.roll(jnp.where(lane >= 96, a, b), 32, 1),
                            pltpu.roll(jnp.where(lane >= 64, b, c), 64, 1),
                            pltpu.roll(c, 96, 1),
                        )
                        for k, row in enumerate(picked):
                            rows_ref[pl.ds((group * 4 + k) * pitch_rows, pair), :] = jnp.where(
                                inside, row, 0.0
                            )
                    lanes = slice((piece * half + zl) * LANES, (piece * half + zl + 1) * LANES)
                    for ch in range(own):
                        left_ref[ch, pl.ds(at, strip), lanes] = rows_ref[
                            pl.ds(ch, strip, stride=pitch_rows), :
                        ].astype(jnp.bfloat16)
                        right_ref[ch, pl.ds(at_right, strip), lanes] = rows_ref[
                            pl.ds(own + ch, strip, stride=pitch_rows), :
                        ].astype(jnp.bfloat16)

    @pl.when(step == blocks - 1)
    def _multiply():
        contract = ((0,), (0,)) if incoming else ((1,), (1,))
        for ch in range(own):
            product = lax.dot_general(
                left_ref[ch], right_ref[ch], (contract, ((), ())), preferred_element_type=jnp.float32
            )
            for place in range(blocks):
                if incoming:
                    row, pitch = lax.rem(place // 2 + zh, 2) * 2 + place % 2, LANES
                else:
                    row, pitch = place, side
                for upper in range(2):
                    for col in range(blocks):
                        tiles_ref[
                            col // half,
                            upper * blocks + row,
                            pl.ds((col % half) * own + ch, strip, stride=pitch_rows),
                            :,
                        ] = product[
                            place * pitch + upper * strip : place * pitch + (upper + 1) * strip,
                            col * LANES : (col + 1) * LANES,
                        ]

    @pl.when(step >= blocks)
    def _repack():
        for r in range(2):
            place = (step - blocks) * 2 + r
            for piece in range(2):
                y_ref, first = piece_of(y_refs, piece)
                for group in range(strip // 4):
                    p, q, t, s = (
                        tiles_ref[piece, place, pl.ds((group * 4 + k) * pitch_rows, pair), :]
                        for k in range(4)
                    )
                    q, t, s = pltpu.roll(q, 96, 1), pltpu.roll(t, 64, 1), pltpu.roll(s, 32, 1)
                    flat = jnp.concatenate(
                        [
                            jnp.where(inside, p, q),
                            jnp.where(lane < 64, q, t),
                            jnp.where(lane < 32, t, s),
                        ],
                        axis=1,
                    )
                    y_ref[
                        r * pair : (r + 1) * pair, first + group * span : first + (group + 1) * span
                    ] = flat.astype(jnp.bfloat16)


def fits(mesh, residues, width):
    rows, cols = mesh.shape["row"], mesh.shape["col"]
    return (
        mesh.shape["groups"] == 2
        and rows == 4
        and cols == 4
        and 4 * residues == 3 * LANES * cols
        and width == 8 * rows * cols
    )


def whole_spec(array):
    return pl.BlockSpec(array.shape, lambda i: (0,) * array.ndim)


def triangle_call(received, n_out, blocks, side, own, incoming):
    pair = 2 * own
    pixels = side * side
    padded = blocks * LANES
    strip = side // 2
    left_rows = blocks * side
    right_rows = left_rows if incoming else padded
    return pl.pallas_call(
        functools.partial(triangle_kernel, blocks, side, own, incoming, len(received)),
        grid=(2 * blocks,),
        in_specs=[
            pl.BlockSpec((blocks * pair, a.shape[1]), lambda i: (jnp.minimum(i, blocks - 1), 0))
            for a in received
        ],
        out_specs=[
            pl.BlockSpec((2 * pair, pixels // n_out), lambda i: (jnp.maximum(i - blocks, 0), 0))
        ] * n_out,
        out_shape=[
            pltpu.HBM((blocks * blocks * own, pixels // n_out), jnp.bfloat16)
        ] * n_out,
        scratch_shapes=[
            pltpu.VMEM((own, left_rows, padded), jnp.bfloat16),
            pltpu.VMEM((own, right_rows, padded), jnp.bfloat16),
            pltpu.VMEM((strip * (pair + 1), LANES), jnp.float32),
            pltpu.VMEM((2, 2 * blocks, strip * (pair + 1), LANES), jnp.float32),
        ],
        compiler_params=pltpu.CompilerParams(vmem_limit_bytes=48 * 1024 * 1024),
        cost_estimate=pl.CostEstimate(
            flops=2 * own * (blocks * side) ** 3,
            bytes_accessed=12 * blocks * blocks * pair * pixels // 2,
            transcendentals=0,
        ),
    )(*received)


def pixel_call(body, tiled, fixed, outs, steps, tile, flops, start=0, pixels=None, kept=(), scratch=(), row_major_out=False):
    pixels = pixels or steps * tile

    def spec(channels, first, count, row_major):
        if row_major:
            return pl.BlockSpec(
                (tile, channels), lambda i: (jnp.clip(i + first, 0, count - 1), 0)
            )
        return pl.BlockSpec((channels, tile), lambda i: (0, jnp.clip(i + first, 0, count - 1)))

    def packed(a, first, count):
        return pl.BlockSpec(
            (1, *a.shape[1:]), lambda i: (jnp.clip(i + first, 0, count - 1), 0, 0)
        )

    in_specs = [
        packed(a, first, count) if a.ndim == 3 else spec(a.shape[0], first, count, False)
        for a, first, count in tiled
    ]
    in_specs += [whole_spec(a) for a in fixed]
    in_specs += [pl.BlockSpec(memory_space=pl.ANY)] * len(kept)
    n_in, n_kept = len(in_specs), len(kept)

    def kernel(*refs):
        body(*refs[: n_in - n_kept], *refs[n_in:])

    return pl.pallas_call(
        kernel,
        grid=(steps,),
        in_specs=in_specs,
        out_specs=[spec(ch, start, pixels // tile, row_major_out) for ch in outs],
        out_shape=[
            pltpu.HBM((pixels, ch) if row_major_out else (ch, pixels), jnp.bfloat16)
            for ch in outs
        ],
        input_output_aliases={n_in - n_kept + k: k for k in range(n_kept)},
        scratch_shapes=list(scratch),
        compiler_params=pltpu.CompilerParams(vmem_limit_bytes=48 * 1024 * 1024),
        cost_estimate=pl.CostEstimate(
            flops=flops, bytes_accessed=2 * steps * tile * (sum(outs) + 256), transcendentals=0
        ),
    )(*(a for a, *_ in tiled), *fixed, *kept)


LINE = ("groups", "zh")
CUBE = ("groups", "row", "zl")


def pack(pair_act, mask, cuts, tile):
    per_strip = cuts[-1]
    shape = (tile + mask.shape[1], pair_act.shape[1])
    outs = [end - begin for begin, end in zip((0, *cuts), cuts)] + [per_strip, per_strip]
    anywhere = pl.BlockSpec(memory_space=pltpu.HBM)
    return pl.pallas_call(
        functools.partial(pack_kernel, cuts, tile),
        in_specs=[anywhere] * 2,
        out_specs=[anywhere] * len(outs),
        out_shape=[pltpu.HBM((n, *shape), jnp.bfloat16) for n in outs],
        scratch_shapes=[
            pltpu.VMEM((2, per_strip, *shape), jnp.bfloat16),
            pltpu.SemaphoreType.DMA((2, per_strip)),
            pltpu.SemaphoreType.DMA((2, per_strip)),
            pltpu.SemaphoreType.DMA((len(outs),)),
        ],
        compiler_params=pltpu.CompilerParams(vmem_limit_bytes=48 * 1024 * 1024),
    )(pair_act, mask)


def by_kernels(
    pair_act,
    pair_mask,
    input_gain,
    input_bias,
    project_weight,
    gate_weight,
    output_gain,
    output_bias,
    output_weight,
):
    blocks = lax.axis_size("row")
    peers = blocks * blocks
    side, _, channels = pair_act.shape
    width = output_weight.shape[1]
    own = width // peers
    pixels = side * side
    strip = side // 2
    mult = 2 * channels

    tile = 9 * LANES
    per_piece = pixels // 2 // tile
    cuts = (1, per_piece - 1, per_piece)
    marks = pair_mask.astype(jnp.bfloat16).reshape(2 * per_piece, tile // LANES, LANES)
    marks = jnp.pad(marks, ((0, 0), (0, 16 - tile // LANES), (0, 0)))
    *z_parts, z_own, z_next = pack(pair_act.reshape(pixels, channels), marks, cuts, tile)
    z_far = []
    for part in z_parts[:-1]:
        over = lax.ppermute(part, LINE, ((1, 3), (2, 0)))
        z_far.append(lax.ppermute(over, LINE, ((0, 1), (3, 2))))
    z_over = lax.ppermute(z_next, LINE, ((0, 2), (3, 1)))
    z_near = lax.ppermute(z_next, LINE, ((1, 0), (2, 3)))
    z_far.append(lax.ppermute(z_parts[-1], LINE, ((1, 2), (2, 1))))
    small = jnp.stack([input_gain, input_bias, output_gain, output_bias], axis=1)
    small = small.reshape(-1, channels).T
    weights = jnp.concatenate(
        [project_weight * 0.5, gate_weight * 0.5, output_weight], axis=2
    ).transpose(0, 2, 1)
    fixed = (small, weights)

    def first(piece, ours, far, parts, kept):
        tiled = [(ours, 0, per_piece)]
        tiled += [(part, -begin, end - begin) for part, (begin, end) in zip(far, parts)]
        return pixel_call(
            functools.partial(first_kernel, peers, parts),
            tiled, fixed, (2 * width, channels, 16), per_piece, tile, pixels // 2 * mult * 4 * width,
            start=piece * per_piece, pixels=pixels, kept=kept,
        )

    begun = first(0, z_own, [z_over], [(0, per_piece)], ())
    sent, zt, mask = first(1, z_near, z_far, list(zip((0, *cuts), cuts)), begun)
    wide = 2 * tile
    steps = pixels // wide

    def gate_of(zt, u):
        return pixel_call(
            functools.partial(gate_kernel, u), [(zt, 0, steps)], fixed, (channels,),
            steps, wide, pixels * mult * channels,
        )[0]

    def exchange(array):
        there = lax.all_to_all(array.reshape(peers, -1, array.shape[1]), CUBE, 0, 0)
        return there.reshape(array.shape)

    gate = gate_of(zt, 0)
    triangle = exchange(*triangle_call([exchange(sent)], 1, blocks, side, own, False))
    sent, zt = pixel_call(
        functools.partial(middle_kernel, peers),
        [(a, 0, steps) for a in (triangle, zt, gate, mask)], fixed, (2 * width, channels),
        steps, wide, pixels * mult * 5 * width,
    )
    gate = gate_of(zt, 1)
    products = triangle_call([exchange(sent)], 2, blocks, side, own, True)

    def finish(piece, triangle):
        at = piece * steps // 2
        return pixel_call(
            last_kernel,
            [(triangle, 0, steps // 2), (zt, at, steps), (gate, at, steps)],
            fixed, (channels,), steps // 2, wide, pixels // 2 * mult * channels, row_major_out=True,
        )[0]

    there = finish(1, exchange(products[1]))
    beside, across = (
        lax.ppermute(there, LINE, pairs) for pairs in (((0, 1), (3, 2)), ((1, 2), (2, 1)))
    )
    there, waiting = lax.optimization_barrier((there, products[0]))
    here = finish(0, exchange(waiting))
    back = lax.ppermute(here, LINE, ((1, 3), (2, 0)))
    return pl.pallas_call(
        assemble_kernel,
        in_specs=[pl.BlockSpec(memory_space=pl.ANY)] * 4,
        out_specs=pl.BlockSpec(memory_space=pl.ANY),
        out_shape=pltpu.HBM((2, *here.shape), here.dtype),
        scratch_shapes=[
            pltpu.VMEM((2, *here.shape), here.dtype),
            pltpu.SemaphoreType.DMA((2, 2)),
            pltpu.SemaphoreType.DMA((2, 2)),
        ],
        compiler_params=pltpu.CompilerParams(vmem_limit_bytes=48 * 1024 * 1024),
    )(here, beside, back, across).reshape(side, side, channels)


def layer_norm(values, gain, bias, axis):
    average = jnp.mean(values, axis=axis, keepdims=True)
    centred = values - average
    spread_sq = jnp.mean(centred * centred, axis=axis, keepdims=True)
    return centred * lax.rsqrt(spread_sq + 1e-05) * gain + bias


def triangle_update(
    pair_act,
    mask_float,
    layer_index,
    input_gain,
    input_bias,
    project_weight,
    gate_weight,
    output_gain,
    output_bias,
    output_weight,
    incoming,
):
    rows, cols = lax.axis_size("row"), lax.axis_size("col")
    peers = rows * cols
    rows_here, cols_here, channels_here = pair_act.shape
    width = output_weight.shape[1]
    own = width // peers
    pixels = rows_here * cols_here
    pair_float = pair_act.astype(jnp.float32).reshape(pixels, channels_here)
    normed = layer_norm(
        pair_float, input_gain[layer_index], input_bias[layer_index], -1
    ).astype(jnp.bfloat16)
    projected = lax.dot_general(
        project_weight[layer_index],
        normed,
        (((0,), (1,)), ((), ())),
        preferred_element_type=jnp.float32,
    ).reshape(4, peers, own, pixels)
    mask_row = mask_float.reshape(1, 1, pixels)
    left_proj = (jax.nn.sigmoid(projected[0]) * projected[1] * mask_row).astype(jnp.bfloat16)
    right_proj = (jax.nn.sigmoid(projected[2]) * projected[3] * mask_row).astype(jnp.bfloat16)
    both = jnp.concatenate([left_proj, right_proj], axis=1)
    both = lax.all_to_all(both, GRID, 0, 0)
    both = both.reshape(rows, cols, 2, own, rows_here, cols_here)
    both = both.transpose(2, 3, 0, 4, 1, 5).reshape(2, own, rows * rows_here, cols * cols_here)
    spec = "cki,ckj->cij" if incoming else "cik,cjk->cij"
    triangle = jnp.einsum(spec, both[0], both[1], preferred_element_type=jnp.float32)
    triangle = triangle.astype(jnp.bfloat16).reshape(own, rows, rows_here, cols, cols_here)
    triangle = triangle.transpose(1, 3, 0, 2, 4).reshape(peers, own, pixels)
    triangle = lax.all_to_all(triangle, GRID, 0, 0).reshape(width, pixels)
    normed_sum = layer_norm(
        triangle.astype(jnp.float32),
        output_gain[layer_index][:, None],
        output_bias[layer_index][:, None],
        0,
    ).astype(jnp.bfloat16)
    gate_value = jax.nn.sigmoid(
        jnp.dot(normed, gate_weight[layer_index], preferred_element_type=jnp.float32)
    )
    mapped = lax.dot_general(
        normed_sum,
        output_weight[layer_index],
        (((0,), (0,)), ((), ())),
        preferred_element_type=jnp.float32,
    )
    return (
        (pair_float + gate_value * mapped)
        .astype(jnp.bfloat16)
        .reshape(rows_here, cols_here, channels_here)
    )


def shards(pair_act, pair_mask, *params):
    mask_float = pair_mask.astype(jnp.float32)
    for index in range(2):
        pair_act = triangle_update(pair_act, mask_float, index, *params, index == 1)
    return pair_act


def solution(mesh):
    def updates(pair_act, pair_mask, *params):
        body, grid, cols = shards, mesh, "col"
        if fits(mesh, pair_act.shape[1], params[-1].shape[1]):
            sizes = mesh.devices.shape
            grid = jax.sharding.Mesh(
                mesh.devices.reshape(*sizes[:2], 2, sizes[2] // 2), ("groups", "row", "zh", "zl")
            )
            body, cols = by_kernels, ("zh", "zl")
        pixels = (("groups", "row"), cols)
        return jax.shard_map(
            body,
            mesh=grid,
            in_specs=(P(*pixels, None), P(*pixels)) + (P(),) * 7,
            out_specs=P(*pixels, None),
            check_vma=False,
        )(pair_act, pair_mask, *params)

    return updates
```

```python
import functools

import jax
import jax.numpy as jnp
from jax import lax
from jax.experimental import pallas as pl
from jax.experimental.pallas import tpu as pltpu
from jax.sharding import PartitionSpec as P

GRID = ("row", "col")
LANES = 128


IN_GAIN, IN_BIAS, OUT_GAIN, OUT_BIAS = range(4)


def channel_norm(values, gain, bias):
    average = jnp.mean(values, axis=0, keepdims=True)
    centred = values - average
    spread_sq = jnp.mean(centred * centred, axis=0, keepdims=True)
    return centred * lax.rsqrt(spread_sq + 1e-05) * gain + bias


def dot(left, right):
    return jnp.dot(left, right, preferred_element_type=jnp.float32)


def norm_of(values, small_ref, update, which):
    at = 4 * update + which
    return channel_norm(values, small_ref[:, at : at + 1], small_ref[:, at + 1 : at + 2])


def emit_projections(peers, update, zt, mask, small_ref, weight_ref, lr_ref):
    width = lr_ref.shape[0] // 2
    own = width // peers
    tile = zt.shape[1]
    normed = norm_of(zt, small_ref, update, IN_GAIN) * mask
    projected = dot(weight_ref[update, : 4 * width], normed.astype(jnp.bfloat16))
    left = (jnp.tanh(projected[:width]) + 1.0) * projected[width : 2 * width]
    right = (jnp.tanh(projected[2 * width : 3 * width]) + 1.0) * projected[3 * width :]
    both = jnp.concatenate(
        [left.reshape(peers, own, tile), right.reshape(peers, own, tile)], axis=1
    )
    lr_ref[...] = both.reshape(2 * width, tile).astype(jnp.bfloat16)


def pack_kernel(cuts, tile, z_ref, mask_ref, *refs):
    out_refs, (held_ref, z_sems, mask_sems, out_sems) = refs[:-4], refs[-4:]
    part_refs, (own_ref, next_ref) = out_refs[:-2], out_refs[-2:]
    upper = lax.axis_index("groups")
    home = upper == lax.axis_index("zh")
    per_strip = cuts[-1]
    rows = held_ref.shape[2]
    fetches = []
    for which in range(2):
        strip = lax.rem(upper + 1 - which, 2)
        for t in range(per_strip):
            at = pl.multiple_of((strip * per_strip + t) * tile, tile)
            fetches.append(
                pltpu.make_async_copy(
                    z_ref.at[pl.ds(at, tile)], held_ref.at[which, t, 0:tile], z_sems.at[which, t]
                )
            )
            fetches.append(
                pltpu.make_async_copy(
                    mask_ref.at[strip * per_strip + t], held_ref.at[which, t, tile:rows],
                    mask_sems.at[which, t],
                )
            )
    stores = [
        pltpu.make_async_copy(held_ref.at[0, begin:end], part_ref, out_sems.at[k])
        for k, (begin, end, part_ref) in enumerate(zip((0, *cuts), cuts, part_refs))
    ]
    stores += [
        pltpu.make_async_copy(held_ref.at[1], own_ref, out_sems.at[len(cuts)]),
        pltpu.make_async_copy(
            held_ref.at[1 - home.astype(jnp.int32)], next_ref, out_sems.at[len(cuts) + 1]
        ),
    ]
    for fetch in fetches:
        fetch.start()
    for fetch in fetches[: 2 * per_strip]:
        fetch.wait()
    for store in stores[: len(cuts)]:
        store.start()
    for fetch in fetches[2 * per_strip :]:
        fetch.wait()
    for store in stores[len(cuts) :]:
        store.start()
    for store in stores:
        store.wait()


def first_kernel(peers, parts, own_ref, *refs):
    far_refs, (small_ref, weight_ref), (lr_ref, zt_ref, mask_ref) = (
        refs[: len(parts)], refs[len(parts) : -3], refs[-3:],
    )
    home = lax.axis_index("groups") == lax.axis_index("zh")
    step = pl.program_id(0)
    tile = zt_ref.shape[1]

    def put(z_ref):
        zt_ref[...] = z_ref[0, :tile].astype(jnp.float32).T.astype(jnp.bfloat16)
        marks = z_ref[0, tile:].astype(jnp.float32)
        flat = jnp.concatenate([marks[k : k + 1] for k in range(tile // LANES)], axis=1)
        mask_ref[...] = jnp.broadcast_to(flat, mask_ref.shape).astype(jnp.bfloat16)

    pl.when(home)(lambda: put(own_ref))
    for (begin, end), far_ref in zip(parts, far_refs):
        here = jnp.logical_and(step >= begin, step < end)
        pl.when(jnp.logical_and(jnp.logical_not(home), here))(functools.partial(put, far_ref))
    zt = zt_ref[...].astype(jnp.float32)
    mask = mask_ref[...].astype(jnp.float32)[:1]
    emit_projections(peers, 0, zt, mask, small_ref, weight_ref, lr_ref)


def gate_kernel(update, zt_ref, small_ref, weight_ref, gate_ref):
    channels = gate_ref.shape[0]
    normed = norm_of(zt_ref[...].astype(jnp.float32), small_ref, update, IN_GAIN)
    at = weight_ref.shape[1] - 2 * channels
    gates = dot(weight_ref[update, at : at + channels], normed.astype(jnp.bfloat16))
    gate_ref[...] = (0.5 * jnp.tanh(gates) + 0.5).astype(jnp.bfloat16)


def updated(update, t_ref, zt_ref, gate_ref, small_ref, weight_ref):
    normed_sum = norm_of(t_ref[...].astype(jnp.float32), small_ref, update, OUT_GAIN)
    at = weight_ref.shape[1] - zt_ref.shape[0]
    mapped = dot(weight_ref[update, at:], normed_sum.astype(jnp.bfloat16))
    return zt_ref[...].astype(jnp.float32) + gate_ref[...].astype(jnp.float32) * mapped


def middle_kernel(
    peers, t_ref, zt_ref, gate_ref, mask_ref, small_ref, weight_ref, lr_ref, out_ref
):
    fresh = updated(0, t_ref, zt_ref, gate_ref, small_ref, weight_ref).astype(jnp.bfloat16)
    out_ref[...] = fresh
    mask = mask_ref[...].astype(jnp.float32)[:1]
    emit_projections(peers, 1, fresh.astype(jnp.float32), mask, small_ref, weight_ref, lr_ref)


def last_kernel(t_ref, zt_ref, gate_ref, small_ref, weight_ref, out_ref):
    fresh = updated(1, t_ref, zt_ref, gate_ref, small_ref, weight_ref)
    out_ref[...] = fresh.T.astype(jnp.bfloat16)


def assemble_kernel(here_ref, beside_ref, back_ref, across_ref, out_ref, held_ref, in_sems, out_sems):
    upper = lax.axis_index("groups")
    home = upper == lax.axis_index("zh")
    parts = in_sems.shape[1]
    size = here_ref.shape[0] // parts

    def move(*sources):
        pieces = [(which, k, slice(k * size, (k + 1) * size)) for k in range(parts) for which in range(2)]
        fetches = [
            pltpu.make_async_copy(
                sources[which].at[rows], held_ref.at[which, rows], in_sems.at[which, k]
            )
            for which, k, rows in pieces
        ]
        stores = [
            pltpu.make_async_copy(
                held_ref.at[which, rows], out_ref.at[lax.rem(upper + which, 2), rows],
                out_sems.at[which, k],
            )
            for which, k, rows in pieces
        ]
        for fetch in fetches:
            fetch.start()
        for fetch, store in zip(fetches, stores):
            fetch.wait()
            store.start()
        for store in stores:
            store.wait()

    pl.when(home)(lambda: move(here_ref, back_ref))
    pl.when(jnp.logical_not(home))(lambda: move(beside_ref, across_ref))


def triangle_kernel(blocks, side, own, incoming, n_in, *refs):
    x_refs, y_refs, (left_ref, right_ref, rows_ref, tiles_ref) = refs[:n_in], refs[n_in:-4], refs[-4:]
    step = pl.program_id(0)
    zh = lax.axis_index("zh")
    pair = 2 * own
    span = 4 * side
    strip = side // 2
    half = blocks // 2
    pitch_rows = pair + 1
    lane = lax.broadcasted_iota(jnp.int32, (pair, LANES), 1)
    inside = lane < side

    def piece_of(piece_refs, piece):
        if len(piece_refs) == 1:
            return piece_refs[0], piece * strip * side
        return piece_refs[piece], 0

    @pl.when(step < blocks)
    def _unpack():
        upper, row_pair = step // half, lax.rem(step, half)
        mirror = lax.rem(row_pair + zh, 2)
        for r in range(2):
            at = pl.multiple_of((row_pair * 2 + r) * side + upper * strip, 16)
            if incoming:
                at_right = at
            else:
                at_right = pl.multiple_of((mirror * 2 + r) * LANES + upper * strip, 16)
            for zl in range(half):
                for piece in range(2):
                    x_ref, first = piece_of(x_refs, piece)
                    for group in range(strip // 4):
                        x = x_ref[
                            (r * half + zl) * pair : (r * half + zl + 1) * pair,
                            first + group * span : first + (group + 1) * span,
                        ].astype(jnp.float32)
                        a, b, c = x[:, :LANES], x[:, LANES : 2 * LANES], x[:, 2 * LANES :]
                        picked = (
                            a,
                            pltpu.roll(jnp.where(lane >= 96, a, b), 32, 1),
                            pltpu.roll(jnp.where(lane >= 64, b, c), 64, 1),
                            pltpu.roll(c, 96, 1),
                        )
                        for k, row in enumerate(picked):
                            rows_ref[pl.ds((group * 4 + k) * pitch_rows, pair), :] = jnp.where(
                                inside, row, 0.0
                            )
                    lanes = slice((piece * half + zl) * LANES, (piece * half + zl + 1) * LANES)
                    for ch in range(own):
                        left_ref[ch, pl.ds(at, strip), lanes] = rows_ref[
                            pl.ds(ch, strip, stride=pitch_rows), :
                        ].astype(jnp.bfloat16)
                        right_ref[ch, pl.ds(at_right, strip), lanes] = rows_ref[
                            pl.ds(own + ch, strip, stride=pitch_rows), :
                        ].astype(jnp.bfloat16)

    @pl.when(step == blocks - 1)
    def _multiply():
        contract = ((0,), (0,)) if incoming else ((1,), (1,))
        for ch in range(own):
            product = lax.dot_general(
                left_ref[ch], right_ref[ch], (contract, ((), ())), preferred_element_type=jnp.float32
            )
            for place in range(blocks):
                if incoming:
                    row, pitch = lax.rem(place // 2 + zh, 2) * 2 + place % 2, LANES
                else:
                    row, pitch = place, side
                for upper in range(2):
                    for col in range(blocks):
                        tiles_ref[
                            col // half,
                            upper * blocks + row,
                            pl.ds((col % half) * own + ch, strip, stride=pitch_rows),
                            :,
                        ] = product[
                            place * pitch + upper * strip : place * pitch + (upper + 1) * strip,
                            col * LANES : (col + 1) * LANES,
                        ]

    @pl.when(step >= blocks)
    def _repack():
        for r in range(2):
            place = (step - blocks) * 2 + r
            for piece in range(2):
                y_ref, first = piece_of(y_refs, piece)
                for group in range(strip // 4):
                    p, q, t, s = (
                        tiles_ref[piece, place, pl.ds((group * 4 + k) * pitch_rows, pair), :]
                        for k in range(4)
                    )
                    q, t, s = pltpu.roll(q, 96, 1), pltpu.roll(t, 64, 1), pltpu.roll(s, 32, 1)
                    flat = jnp.concatenate(
                        [
                            jnp.where(inside, p, q),
                            jnp.where(lane < 64, q, t),
                            jnp.where(lane < 32, t, s),
                        ],
                        axis=1,
                    )
                    y_ref[
                        r * pair : (r + 1) * pair, first + group * span : first + (group + 1) * span
                    ] = flat.astype(jnp.bfloat16)


def fits(mesh, residues, width):
    rows, cols = mesh.shape["row"], mesh.shape["col"]
    return (
        mesh.shape["groups"] == 2
        and rows == 4
        and cols == 4
        and 4 * residues == 3 * LANES * cols
        and width == 8 * rows * cols
    )


def whole_spec(array):
    return pl.BlockSpec(array.shape, lambda i: (0,) * array.ndim)


def triangle_call(received, n_out, blocks, side, own, incoming):
    pair = 2 * own
    pixels = side * side
    padded = blocks * LANES
    strip = side // 2
    left_rows = blocks * side
    right_rows = left_rows if incoming else padded
    return pl.pallas_call(
        functools.partial(triangle_kernel, blocks, side, own, incoming, len(received)),
        grid=(2 * blocks,),
        in_specs=[
            pl.BlockSpec((blocks * pair, a.shape[1]), lambda i: (jnp.minimum(i, blocks - 1), 0))
            for a in received
        ],
        out_specs=[
            pl.BlockSpec((2 * pair, pixels // n_out), lambda i: (jnp.maximum(i - blocks, 0), 0))
        ] * n_out,
        out_shape=[
            pltpu.HBM((blocks * blocks * own, pixels // n_out), jnp.bfloat16)
        ] * n_out,
        scratch_shapes=[
            pltpu.VMEM((own, left_rows, padded), jnp.bfloat16),
            pltpu.VMEM((own, right_rows, padded), jnp.bfloat16),
            pltpu.VMEM((strip * (pair + 1), LANES), jnp.float32),
            pltpu.VMEM((2, 2 * blocks, strip * (pair + 1), LANES), jnp.float32),
        ],
        compiler_params=pltpu.CompilerParams(vmem_limit_bytes=48 * 1024 * 1024),
        cost_estimate=pl.CostEstimate(
            flops=2 * own * (blocks * side) ** 3,
            bytes_accessed=12 * blocks * blocks * pair * pixels // 2,
            transcendentals=0,
        ),
    )(*received)


def pixel_call(body, tiled, fixed, outs, steps, tile, flops, start=0, pixels=None, kept=(), scratch=(), row_major_out=False):
    pixels = pixels or steps * tile

    def spec(channels, first, count, row_major):
        if row_major:
            return pl.BlockSpec(
                (tile, channels), lambda i: (jnp.clip(i + first, 0, count - 1), 0)
            )
        return pl.BlockSpec((channels, tile), lambda i: (0, jnp.clip(i + first, 0, count - 1)))

    def packed(a, first, count):
        return pl.BlockSpec(
            (1, *a.shape[1:]), lambda i: (jnp.clip(i + first, 0, count - 1), 0, 0)
        )

    in_specs = [
        packed(a, first, count) if a.ndim == 3 else spec(a.shape[0], first, count, False)
        for a, first, count in tiled
    ]
    in_specs += [whole_spec(a) for a in fixed]
    in_specs += [pl.BlockSpec(memory_space=pl.ANY)] * len(kept)
    n_in, n_kept = len(in_specs), len(kept)

    def kernel(*refs):
        body(*refs[: n_in - n_kept], *refs[n_in:])

    return pl.pallas_call(
        kernel,
        grid=(steps,),
        in_specs=in_specs,
        out_specs=[spec(ch, start, pixels // tile, row_major_out) for ch in outs],
        out_shape=[
            pltpu.HBM((pixels, ch) if row_major_out else (ch, pixels), jnp.bfloat16)
            for ch in outs
        ],
        input_output_aliases={n_in - n_kept + k: k for k in range(n_kept)},
        scratch_shapes=list(scratch),
        compiler_params=pltpu.CompilerParams(vmem_limit_bytes=48 * 1024 * 1024),
        cost_estimate=pl.CostEstimate(
            flops=flops, bytes_accessed=2 * steps * tile * (sum(outs) + 256), transcendentals=0
        ),
    )(*(a for a, *_ in tiled), *fixed, *kept)


LINE = ("groups", "zh")
CUBE = ("groups", "row", "zl")


def pack(pair_act, mask, cuts, tile):
    per_strip = cuts[-1]
    shape = (tile + mask.shape[1], pair_act.shape[1])
    outs = [end - begin for begin, end in zip((0, *cuts), cuts)] + [per_strip, per_strip]
    anywhere = pl.BlockSpec(memory_space=pltpu.HBM)
    return pl.pallas_call(
        functools.partial(pack_kernel, cuts, tile),
        in_specs=[anywhere] * 2,
        out_specs=[anywhere] * len(outs),
        out_shape=[pltpu.HBM((n, *shape), jnp.bfloat16) for n in outs],
        scratch_shapes=[
            pltpu.VMEM((2, per_strip, *shape), jnp.bfloat16),
            pltpu.SemaphoreType.DMA((2, per_strip)),
            pltpu.SemaphoreType.DMA((2, per_strip)),
            pltpu.SemaphoreType.DMA((len(outs),)),
        ],
        compiler_params=pltpu.CompilerParams(vmem_limit_bytes=48 * 1024 * 1024),
    )(pair_act, mask)


def by_kernels(
    pair_act,
    pair_mask,
    input_gain,
    input_bias,
    project_weight,
    gate_weight,
    output_gain,
    output_bias,
    output_weight,
):
    blocks = lax.axis_size("row")
    peers = blocks * blocks
    side, _, channels = pair_act.shape
    width = output_weight.shape[1]
    own = width // peers
    pixels = side * side
    strip = side // 2
    mult = 2 * channels

    tile = 9 * LANES
    per_piece = pixels // 2 // tile
    cuts = (1, per_piece - 1, per_piece)
    marks = pair_mask.astype(jnp.bfloat16).reshape(2 * per_piece, tile // LANES, LANES)
    marks = jnp.pad(marks, ((0, 0), (0, 16 - tile // LANES), (0, 0)))
    *z_parts, z_own, z_next = pack(pair_act.reshape(pixels, channels), marks, cuts, tile)
    z_far = []
    for part in z_parts[:-1]:
        over = lax.ppermute(part, LINE, ((1, 3), (2, 0)))
        z_far.append(lax.ppermute(over, LINE, ((0, 1), (3, 2))))
    z_near = lax.ppermute(z_next, LINE, ((1, 0), (2, 3), (0, 2), (3, 1)))
    z_far.append(lax.ppermute(z_parts[-1], LINE, ((1, 2), (2, 1))))
    small = jnp.stack([input_gain, input_bias, output_gain, output_bias], axis=1)
    small = small.reshape(-1, channels).T
    weights = jnp.concatenate(
        [project_weight * 0.5, gate_weight * 0.5, output_weight], axis=2
    ).transpose(0, 2, 1)
    fixed = (small, weights)

    def first(piece, ours, far, parts, kept):
        tiled = [(ours, 0, per_piece)]
        tiled += [(part, -begin, end - begin) for part, (begin, end) in zip(far, parts)]
        return pixel_call(
            functools.partial(first_kernel, peers, parts),
            tiled, fixed, (2 * width, channels, 16), per_piece, tile, pixels // 2 * mult * 4 * width,
            start=piece * per_piece, pixels=pixels, kept=kept,
        )

    begun = first(0, z_own, [z_near], [(0, per_piece)], ())
    sent, zt, mask = first(1, z_near, z_far, list(zip((0, *cuts), cuts)), begun)
    wide = 2 * tile
    steps = pixels // wide

    def gate_of(zt, u):
        return pixel_call(
            functools.partial(gate_kernel, u), [(zt, 0, steps)], fixed, (channels,),
            steps, wide, pixels * mult * channels,
        )[0]

    def exchange(array):
        there = lax.all_to_all(array.reshape(peers, -1, array.shape[1]), CUBE, 0, 0)
        return there.reshape(array.shape)

    gate = gate_of(zt, 0)
    triangle = exchange(*triangle_call([exchange(sent)], 1, blocks, side, own, False))
    sent, zt = pixel_call(
        functools.partial(middle_kernel, peers),
        [(a, 0, steps) for a in (triangle, zt, gate, mask)], fixed, (2 * width, channels),
        steps, wide, pixels * mult * 5 * width,
    )
    gate = gate_of(zt, 1)
    products = triangle_call([exchange(sent)], 2, blocks, side, own, True)

    def finish(piece, triangle):
        at = piece * steps // 2
        return pixel_call(
            last_kernel,
            [(triangle, 0, steps // 2), (zt, at, steps), (gate, at, steps)],
            fixed, (channels,), steps // 2, wide, pixels // 2 * mult * channels, row_major_out=True,
        )[0]

    arrived = [exchange(product) for product in products[::-1]]
    there = finish(1, arrived[0])
    beside, across = (
        lax.ppermute(there, LINE, pairs) for pairs in (((0, 1), (3, 2)), ((1, 2), (2, 1)))
    )
    there, waiting = lax.optimization_barrier((there, arrived[1]))
    here = finish(0, waiting)
    back = lax.ppermute(here, LINE, ((1, 3), (2, 0)))
    return pl.pallas_call(
        assemble_kernel,
        in_specs=[pl.BlockSpec(memory_space=pl.ANY)] * 4,
        out_specs=pl.BlockSpec(memory_space=pl.ANY),
        out_shape=pltpu.HBM((2, *here.shape), here.dtype),
        scratch_shapes=[
            pltpu.VMEM((2, *here.shape), here.dtype),
            pltpu.SemaphoreType.DMA((2, 2)),
            pltpu.SemaphoreType.DMA((2, 2)),
        ],
        compiler_params=pltpu.CompilerParams(vmem_limit_bytes=48 * 1024 * 1024),
    )(here, beside, back, across).reshape(side, side, channels)


def layer_norm(values, gain, bias, axis):
    average = jnp.mean(values, axis=axis, keepdims=True)
    centred = values - average
    spread_sq = jnp.mean(centred * centred, axis=axis, keepdims=True)
    return centred * lax.rsqrt(spread_sq + 1e-05) * gain + bias


def triangle_update(
    pair_act,
    mask_float,
    layer_index,
    input_gain,
    input_bias,
    project_weight,
    gate_weight,
    output_gain,
    output_bias,
    output_weight,
    incoming,
):
    rows, cols = lax.axis_size("row"), lax.axis_size("col")
    peers = rows * cols
    rows_here, cols_here, channels_here = pair_act.shape
    width = output_weight.shape[1]
    own = width // peers
    pixels = rows_here * cols_here
    pair_float = pair_act.astype(jnp.float32).reshape(pixels, channels_here)
    normed = layer_norm(
        pair_float, input_gain[layer_index], input_bias[layer_index], -1
    ).astype(jnp.bfloat16)
    projected = lax.dot_general(
        project_weight[layer_index],
        normed,
        (((0,), (1,)), ((), ())),
        preferred_element_type=jnp.float32,
    ).reshape(4, peers, own, pixels)
    mask_row = mask_float.reshape(1, 1, pixels)
    left_proj = (jax.nn.sigmoid(projected[0]) * projected[1] * mask_row).astype(jnp.bfloat16)
    right_proj = (jax.nn.sigmoid(projected[2]) * projected[3] * mask_row).astype(jnp.bfloat16)
    both = jnp.concatenate([left_proj, right_proj], axis=1)
    both = lax.all_to_all(both, GRID, 0, 0)
    both = both.reshape(rows, cols, 2, own, rows_here, cols_here)
    both = both.transpose(2, 3, 0, 4, 1, 5).reshape(2, own, rows * rows_here, cols * cols_here)
    spec = "cki,ckj->cij" if incoming else "cik,cjk->cij"
    triangle = jnp.einsum(spec, both[0], both[1], preferred_element_type=jnp.float32)
    triangle = triangle.astype(jnp.bfloat16).reshape(own, rows, rows_here, cols, cols_here)
    triangle = triangle.transpose(1, 3, 0, 2, 4).reshape(peers, own, pixels)
    triangle = lax.all_to_all(triangle, GRID, 0, 0).reshape(width, pixels)
    normed_sum = layer_norm(
        triangle.astype(jnp.float32),
        output_gain[layer_index][:, None],
        output_bias[layer_index][:, None],
        0,
    ).astype(jnp.bfloat16)
    gate_value = jax.nn.sigmoid(
        jnp.dot(normed, gate_weight[layer_index], preferred_element_type=jnp.float32)
    )
    mapped = lax.dot_general(
        normed_sum,
        output_weight[layer_index],
        (((0,), (0,)), ((), ())),
        preferred_element_type=jnp.float32,
    )
    return (
        (pair_float + gate_value * mapped)
        .astype(jnp.bfloat16)
        .reshape(rows_here, cols_here, channels_here)
    )


def shards(pair_act, pair_mask, *params):
    mask_float = pair_mask.astype(jnp.float32)
    for index in range(2):
        pair_act = triangle_update(pair_act, mask_float, index, *params, index == 1)
    return pair_act


def solution(mesh):
    def updates(pair_act, pair_mask, *params):
        body, grid, cols = shards, mesh, "col"
        if fits(mesh, pair_act.shape[1], params[-1].shape[1]):
            sizes = mesh.devices.shape
            grid = jax.sharding.Mesh(
                mesh.devices.reshape(*sizes[:2], 2, sizes[2] // 2), ("groups", "row", "zh", "zl")
            )
            body, cols = by_kernels, ("zh", "zl")
        pixels = (("groups", "row"), cols)
        return jax.shard_map(
            body,
            mesh=grid,
            in_specs=(P(*pixels, None), P(*pixels)) + (P(),) * 7,
            out_specs=P(*pixels, None),
            check_vma=False,
        )(pair_act, pair_mask, *params)

    return updates
```

```python
import functools

import jax
import jax.numpy as jnp
from jax import lax
from jax.experimental import pallas as pl
from jax.experimental.pallas import tpu as pltpu
from jax.sharding import PartitionSpec as P

GRID = ("row", "col")
LANES = 128


IN_GAIN, IN_BIAS, OUT_GAIN, OUT_BIAS = range(4)


def channel_norm(values, gain, bias):
    average = jnp.mean(values, axis=0, keepdims=True)
    centred = values - average
    spread_sq = jnp.mean(centred * centred, axis=0, keepdims=True)
    return centred * lax.rsqrt(spread_sq + 1e-05) * gain + bias


def dot(left, right):
    return jnp.dot(left, right, preferred_element_type=jnp.float32)


def norm_of(values, small_ref, update, which):
    at = 4 * update + which
    return channel_norm(values, small_ref[:, at : at + 1], small_ref[:, at + 1 : at + 2])


def emit_projections(peers, update, zt, mask, small_ref, weight_ref, lr_ref):
    width = lr_ref.shape[0] // 2
    own = width // peers
    tile = zt.shape[1]
    normed = norm_of(zt, small_ref, update, IN_GAIN) * mask
    projected = dot(weight_ref[update, : 4 * width], normed.astype(jnp.bfloat16))
    left = (jnp.tanh(projected[:width]) + 1.0) * projected[width : 2 * width]
    right = (jnp.tanh(projected[2 * width : 3 * width]) + 1.0) * projected[3 * width :]
    both = jnp.concatenate(
        [left.reshape(peers, own, tile), right.reshape(peers, own, tile)], axis=1
    )
    lr_ref[...] = both.reshape(2 * width, tile).astype(jnp.bfloat16)


def pack_kernel(cuts, tile, z_ref, mask_ref, *refs):
    out_refs, (held_ref, z_sems, mask_sems, out_sems) = refs[:-4], refs[-4:]
    part_refs, (own_ref, next_ref) = out_refs[:-2], out_refs[-2:]
    upper = lax.axis_index("groups")
    home = upper == lax.axis_index("zh")
    per_strip = cuts[-1]
    rows = held_ref.shape[2]
    fetches = []
    for which in range(2):
        strip = lax.rem(upper + 1 - which, 2)
        for t in range(per_strip):
            at = pl.multiple_of((strip * per_strip + t) * tile, tile)
            fetches.append(
                pltpu.make_async_copy(
                    z_ref.at[pl.ds(at, tile)], held_ref.at[which, t, 0:tile], z_sems.at[which, t]
                )
            )
            fetches.append(
                pltpu.make_async_copy(
                    mask_ref.at[strip * per_strip + t], held_ref.at[which, t, tile:rows],
                    mask_sems.at[which, t],
                )
            )
    stores = [
        pltpu.make_async_copy(held_ref.at[0, begin:end], part_ref, out_sems.at[k])
        for k, (begin, end, part_ref) in enumerate(zip((0, *cuts), cuts, part_refs))
    ]
    stores += [
        pltpu.make_async_copy(held_ref.at[1], own_ref, out_sems.at[len(cuts)]),
        pltpu.make_async_copy(
            held_ref.at[1 - home.astype(jnp.int32)], next_ref, out_sems.at[len(cuts) + 1]
        ),
    ]
    for fetch in fetches:
        fetch.start()
    for fetch in fetches[: 2 * per_strip]:
        fetch.wait()
    for store in stores[: len(cuts)]:
        store.start()
    for fetch in fetches[2 * per_strip :]:
        fetch.wait()
    for store in stores[len(cuts) :]:
        store.start()
    for store in stores:
        store.wait()


def first_kernel(peers, parts, own_ref, *refs):
    far_refs, (small_ref, weight_ref), (lr_ref, zt_ref, mask_ref) = (
        refs[: len(parts)], refs[len(parts) : -3], refs[-3:],
    )
    home = lax.axis_index("groups") == lax.axis_index("zh")
    step = pl.program_id(0)
    tile = zt_ref.shape[1]

    def put(z_ref):
        zt_ref[...] = z_ref[0, :tile].astype(jnp.float32).T.astype(jnp.bfloat16)
        marks = z_ref[0, tile:].astype(jnp.float32)
        flat = jnp.concatenate([marks[k : k + 1] for k in range(tile // LANES)], axis=1)
        mask_ref[...] = jnp.broadcast_to(flat, mask_ref.shape).astype(jnp.bfloat16)

    pl.when(home)(lambda: put(own_ref))
    for (begin, end), far_ref in zip(parts, far_refs):
        here = jnp.logical_and(step >= begin, step < end)
        pl.when(jnp.logical_and(jnp.logical_not(home), here))(functools.partial(put, far_ref))
    zt = zt_ref[...].astype(jnp.float32)
    mask = mask_ref[...].astype(jnp.float32)[:1]
    emit_projections(peers, 0, zt, mask, small_ref, weight_ref, lr_ref)


def gate_kernel(update, zt_ref, small_ref, weight_ref, gate_ref):
    channels = gate_ref.shape[0]
    normed = norm_of(zt_ref[...].astype(jnp.float32), small_ref, update, IN_GAIN)
    at = weight_ref.shape[1] - 2 * channels
    gates = dot(weight_ref[update, at : at + channels], normed.astype(jnp.bfloat16))
    gate_ref[...] = (0.5 * jnp.tanh(gates) + 0.5).astype(jnp.bfloat16)


def updated(update, t_ref, zt_ref, gate_ref, small_ref, weight_ref):
    normed_sum = norm_of(t_ref[...].astype(jnp.float32), small_ref, update, OUT_GAIN)
    at = weight_ref.shape[1] - zt_ref.shape[0]
    mapped = dot(weight_ref[update, at:], normed_sum.astype(jnp.bfloat16))
    return zt_ref[...].astype(jnp.float32) + gate_ref[...].astype(jnp.float32) * mapped


def middle_kernel(
    peers, t_ref, zt_ref, gate_ref, mask_ref, small_ref, weight_ref, lr_ref, out_ref
):
    fresh = updated(0, t_ref, zt_ref, gate_ref, small_ref, weight_ref).astype(jnp.bfloat16)
    out_ref[...] = fresh
    mask = mask_ref[...].astype(jnp.float32)[:1]
    emit_projections(peers, 1, fresh.astype(jnp.float32), mask, small_ref, weight_ref, lr_ref)


def last_kernel(t_ref, zt_ref, gate_ref, small_ref, weight_ref, out_ref):
    fresh = updated(1, t_ref, zt_ref, gate_ref, small_ref, weight_ref)
    out_ref[...] = fresh.T.astype(jnp.bfloat16)


def assemble_kernel(here_ref, beside_ref, back_ref, across_ref, out_ref, held_ref, in_sems, out_sems):
    upper = lax.axis_index("groups")
    home = upper == lax.axis_index("zh")
    parts = in_sems.shape[1]
    size = here_ref.shape[0] // parts

    def move(*sources):
        pieces = [(which, k, slice(k * size, (k + 1) * size)) for k in range(parts) for which in range(2)]
        fetches = [
            pltpu.make_async_copy(
                sources[which].at[rows], held_ref.at[which, rows], in_sems.at[which, k]
            )
            for which, k, rows in pieces
        ]
        stores = [
            pltpu.make_async_copy(
                held_ref.at[which, rows], out_ref.at[lax.rem(upper + which, 2), rows],
                out_sems.at[which, k],
            )
            for which, k, rows in pieces
        ]
        for fetch in fetches:
            fetch.start()
        for fetch, store in zip(fetches, stores):
            fetch.wait()
            store.start()
        for store in stores:
            store.wait()

    pl.when(home)(lambda: move(here_ref, back_ref))
    pl.when(jnp.logical_not(home))(lambda: move(beside_ref, across_ref))


def triangle_kernel(blocks, side, own, incoming, made, x_ref, y_ref, left_ref, right_ref, rows_ref, tiles_ref):
    step = pl.program_id(0)
    zh = lax.axis_index("zh")
    pair = 2 * own
    span = 4 * side
    strip = side // 2
    half = blocks // 2
    pitch_rows = pair + 1
    lane = lax.broadcasted_iota(jnp.int32, (pair, LANES), 1)
    inside = lane < side

    wanted = range(blocks) if len(made) == 2 else range(made[0] * half, (made[0] + 1) * half)

    @pl.when(step < blocks)
    def _unpack():
        upper, row_pair = step // half, lax.rem(step, half)
        mirror = lax.rem(row_pair + zh, 2)
        for r in range(2):
            at = pl.multiple_of((row_pair * 2 + r) * side + upper * strip, 16)
            if incoming:
                at_right = at
            else:
                at_right = pl.multiple_of((mirror * 2 + r) * LANES + upper * strip, 16)
            for zl in range(half):
                for piece in range(2):
                    first = piece * strip * side
                    for group in range(strip // 4):
                        x = x_ref[
                            (r * half + zl) * pair : (r * half + zl + 1) * pair,
                            first + group * span : first + (group + 1) * span,
                        ].astype(jnp.float32)
                        a, b, c = x[:, :LANES], x[:, LANES : 2 * LANES], x[:, 2 * LANES :]
                        picked = (
                            a,
                            pltpu.roll(jnp.where(lane >= 96, a, b), 32, 1),
                            pltpu.roll(jnp.where(lane >= 64, b, c), 64, 1),
                            pltpu.roll(c, 96, 1),
                        )
                        for k, row in enumerate(picked):
                            rows_ref[pl.ds((group * 4 + k) * pitch_rows, pair), :] = jnp.where(
                                inside, row, 0.0
                            )
                    lanes = slice((piece * half + zl) * LANES, (piece * half + zl + 1) * LANES)
                    for ch in range(own):
                        left_ref[ch, pl.ds(at, strip), lanes] = rows_ref[
                            pl.ds(ch, strip, stride=pitch_rows), :
                        ].astype(jnp.bfloat16)
                        if incoming and piece not in made:
                            continue
                        right_ref[ch, pl.ds(at_right, strip), lanes] = rows_ref[
                            pl.ds(own + ch, strip, stride=pitch_rows), :
                        ].astype(jnp.bfloat16)

    @pl.when(step == blocks - 1)
    def _multiply():
        contract = ((0,), (0,)) if incoming else ((1,), (1,))
        for ch in range(own):
            right = right_ref[ch]
            if incoming:
                right = right[:, wanted[0] * LANES : (wanted[-1] + 1) * LANES]
            product = lax.dot_general(
                left_ref[ch], right, (contract, ((), ())), preferred_element_type=jnp.float32
            )
            for place in range(blocks):
                if incoming:
                    row, pitch = lax.rem(place // 2 + zh, 2) * 2 + place % 2, LANES
                else:
                    row, pitch = place, side
                for upper in range(2):
                    for col in range(len(wanted)):
                        tiles_ref[
                            col // half,
                            upper * blocks + row,
                            pl.ds((col % half) * own + ch, strip, stride=pitch_rows),
                            :,
                        ] = product[
                            place * pitch + upper * strip : place * pitch + (upper + 1) * strip,
                            col * LANES : (col + 1) * LANES,
                        ]

    @pl.when(step >= blocks)
    def _repack():
        for r in range(2):
            place = (step - blocks) * 2 + r
            for piece in range(len(made)):
                first = piece * strip * side
                for group in range(strip // 4):
                    p, q, t, s = (
                        tiles_ref[piece, place, pl.ds((group * 4 + k) * pitch_rows, pair), :]
                        for k in range(4)
                    )
                    q, t, s = pltpu.roll(q, 96, 1), pltpu.roll(t, 64, 1), pltpu.roll(s, 32, 1)
                    flat = jnp.concatenate(
                        [
                            jnp.where(inside, p, q),
                            jnp.where(lane < 64, q, t),
                            jnp.where(lane < 32, t, s),
                        ],
                        axis=1,
                    )
                    y_ref[
                        r * pair : (r + 1) * pair, first + group * span : first + (group + 1) * span
                    ] = flat.astype(jnp.bfloat16)


def fits(mesh, residues, width):
    rows, cols = mesh.shape["row"], mesh.shape["col"]
    return (
        mesh.shape["groups"] == 2
        and rows == 4
        and cols == 4
        and 4 * residues == 3 * LANES * cols
        and width == 8 * rows * cols
    )


def whole_spec(array):
    return pl.BlockSpec(array.shape, lambda i: (0,) * array.ndim)


def triangle_call(received, made, blocks, side, own, incoming):
    pair = 2 * own
    pixels = side * side
    padded = blocks * LANES
    strip = side // 2
    left_rows = blocks * side
    right_rows = left_rows if incoming else padded
    return pl.pallas_call(
        functools.partial(triangle_kernel, blocks, side, own, incoming, made),
        grid=(2 * blocks,),
        in_specs=[
            pl.BlockSpec((blocks * pair, pixels), lambda i: (jnp.minimum(i, blocks - 1), 0))
        ],
        out_specs=pl.BlockSpec(
            (2 * pair, pixels // 2 * len(made)), lambda i: (jnp.maximum(i - blocks, 0), 0)
        ),
        out_shape=pltpu.HBM((blocks * blocks * own, pixels // 2 * len(made)), jnp.bfloat16),
        scratch_shapes=[
            pltpu.VMEM((own, left_rows, padded), jnp.bfloat16),
            pltpu.VMEM((own, right_rows, padded), jnp.bfloat16),
            pltpu.VMEM((strip * (pair + 1), LANES), jnp.float32),
            pltpu.VMEM((len(made), 2 * blocks, strip * (pair + 1), LANES), jnp.float32),
        ],
        compiler_params=pltpu.CompilerParams(vmem_limit_bytes=48 * 1024 * 1024),
        cost_estimate=pl.CostEstimate(
            flops=own * (blocks * side) ** 3 * len(made),
            bytes_accessed=12 * blocks * blocks * pair * pixels // 2,
            transcendentals=0,
        ),
    )(received)


def pixel_call(body, tiled, fixed, outs, steps, tile, flops, start=0, pixels=None, kept=(), scratch=(), row_major_out=False):
    pixels = pixels or steps * tile

    def spec(channels, first, count, row_major):
        if row_major:
            return pl.BlockSpec(
                (tile, channels), lambda i: (jnp.clip(i + first, 0, count - 1), 0)
            )
        return pl.BlockSpec((channels, tile), lambda i: (0, jnp.clip(i + first, 0, count - 1)))

    def packed(a, first, count):
        return pl.BlockSpec(
            (1, *a.shape[1:]), lambda i: (jnp.clip(i + first, 0, count - 1), 0, 0)
        )

    in_specs = [
        packed(a, first, count) if a.ndim == 3 else spec(a.shape[0], first, count, False)
        for a, first, count in tiled
    ]
    in_specs += [whole_spec(a) for a in fixed]
    in_specs += [pl.BlockSpec(memory_space=pl.ANY)] * len(kept)
    n_in, n_kept = len(in_specs), len(kept)

    def kernel(*refs):
        body(*refs[: n_in - n_kept], *refs[n_in:])

    return pl.pallas_call(
        kernel,
        grid=(steps,),
        in_specs=in_specs,
        out_specs=[spec(ch, start, pixels // tile, row_major_out) for ch in outs],
        out_shape=[
            pltpu.HBM((pixels, ch) if row_major_out else (ch, pixels), jnp.bfloat16)
            for ch in outs
        ],
        input_output_aliases={n_in - n_kept + k: k for k in range(n_kept)},
        scratch_shapes=list(scratch),
        compiler_params=pltpu.CompilerParams(vmem_limit_bytes=48 * 1024 * 1024),
        cost_estimate=pl.CostEstimate(
            flops=flops, bytes_accessed=2 * steps * tile * (sum(outs) + 256), transcendentals=0
        ),
    )(*(a for a, *_ in tiled), *fixed, *kept)


LINE = ("groups", "zh")
CUBE = ("groups", "row", "zl")


def pack(pair_act, mask, cuts, tile):
    per_strip = cuts[-1]
    shape = (tile + mask.shape[1], pair_act.shape[1])
    outs = [end - begin for begin, end in zip((0, *cuts), cuts)] + [per_strip, per_strip]
    anywhere = pl.BlockSpec(memory_space=pltpu.HBM)
    return pl.pallas_call(
        functools.partial(pack_kernel, cuts, tile),
        in_specs=[anywhere] * 2,
        out_specs=[anywhere] * len(outs),
        out_shape=[pltpu.HBM((n, *shape), jnp.bfloat16) for n in outs],
        scratch_shapes=[
            pltpu.VMEM((2, per_strip, *shape), jnp.bfloat16),
            pltpu.SemaphoreType.DMA((2, per_strip)),
            pltpu.SemaphoreType.DMA((2, per_strip)),
            pltpu.SemaphoreType.DMA((len(outs),)),
        ],
        compiler_params=pltpu.CompilerParams(vmem_limit_bytes=48 * 1024 * 1024),
    )(pair_act, mask)


def by_kernels(
    pair_act,
    pair_mask,
    input_gain,
    input_bias,
    project_weight,
    gate_weight,
    output_gain,
    output_bias,
    output_weight,
):
    blocks = lax.axis_size("row")
    peers = blocks * blocks
    side, _, channels = pair_act.shape
    width = output_weight.shape[1]
    own = width // peers
    pixels = side * side
    strip = side // 2
    mult = 2 * channels

    tile = 9 * LANES
    per_piece = pixels // 2 // tile
    cuts = (1, per_piece - 1, per_piece)
    marks = pair_mask.astype(jnp.bfloat16).reshape(2 * per_piece, tile // LANES, LANES)
    marks = jnp.pad(marks, ((0, 0), (0, 16 - tile // LANES), (0, 0)))
    *z_parts, z_own, z_next = pack(pair_act.reshape(pixels, channels), marks, cuts, tile)
    z_far = []
    for part in z_parts[:-1]:
        over = lax.ppermute(part, LINE, ((1, 3), (2, 0)))
        z_far.append(lax.ppermute(over, LINE, ((0, 1), (3, 2))))
    z_near = lax.ppermute(z_next, LINE, ((1, 0), (2, 3), (0, 2), (3, 1)))
    z_far.append(lax.ppermute(z_parts[-1], LINE, ((1, 2), (2, 1))))
    small = jnp.stack([input_gain, input_bias, output_gain, output_bias], axis=1)
    small = small.reshape(-1, channels).T
    weights = jnp.concatenate(
        [project_weight * 0.5, gate_weight * 0.5, output_weight], axis=2
    ).transpose(0, 2, 1)
    fixed = (small, weights)

    def first(piece, ours, far, parts, kept):
        tiled = [(ours, 0, per_piece)]
        tiled += [(part, -begin, end - begin) for part, (begin, end) in zip(far, parts)]
        return pixel_call(
            functools.partial(first_kernel, peers, parts),
            tiled, fixed, (2 * width, channels, 16), per_piece, tile, pixels // 2 * mult * 4 * width,
            start=piece * per_piece, pixels=pixels, kept=kept,
        )

    begun = first(0, z_own, [z_near], [(0, per_piece)], ())
    sent, zt, mask = first(1, z_near, z_far, list(zip((0, *cuts), cuts)), begun)
    wide = 2 * tile
    steps = pixels // wide

    def gate_of(zt, u):
        return pixel_call(
            functools.partial(gate_kernel, u), [(zt, 0, steps)], fixed, (channels,),
            steps, wide, pixels * mult * channels,
        )[0]

    def exchange(array):
        there = lax.all_to_all(array.reshape(peers, -1, array.shape[1]), CUBE, 0, 0)
        return there.reshape(array.shape)

    gate = gate_of(zt, 0)
    triangle = exchange(triangle_call(exchange(sent), (0, 1), blocks, side, own, False))
    sent, zt = pixel_call(
        functools.partial(middle_kernel, peers),
        [(a, 0, steps) for a in (triangle, zt, gate, mask)], fixed, (2 * width, channels),
        steps, wide, pixels * mult * 5 * width,
    )
    gate = gate_of(zt, 1)
    received = exchange(sent)
    product = lambda piece: triangle_call(received, (piece,), blocks, side, own, True)

    def finish(piece, triangle):
        at = piece * steps // 2
        return pixel_call(
            last_kernel,
            [(triangle, 0, steps // 2), (zt, at, steps), (gate, at, steps)],
            fixed, (channels,), steps // 2, wide, pixels // 2 * mult * channels, row_major_out=True,
        )[0]

    there = finish(1, exchange(product(1)))
    beside, across = (
        lax.ppermute(there, LINE, pairs) for pairs in (((0, 1), (3, 2)), ((1, 2), (2, 1)))
    )
    there, waiting = lax.optimization_barrier((there, product(0)))
    here = finish(0, exchange(waiting))
    back = lax.ppermute(here, LINE, ((1, 3), (2, 0)))
    return pl.pallas_call(
        assemble_kernel,
        in_specs=[pl.BlockSpec(memory_space=pl.ANY)] * 4,
        out_specs=pl.BlockSpec(memory_space=pl.ANY),
        out_shape=pltpu.HBM((2, *here.shape), here.dtype),
        scratch_shapes=[
            pltpu.VMEM((2, *here.shape), here.dtype),
            pltpu.SemaphoreType.DMA((2, 2)),
            pltpu.SemaphoreType.DMA((2, 2)),
        ],
        compiler_params=pltpu.CompilerParams(vmem_limit_bytes=48 * 1024 * 1024),
    )(here, beside, back, across).reshape(side, side, channels)


def layer_norm(values, gain, bias, axis):
    average = jnp.mean(values, axis=axis, keepdims=True)
    centred = values - average
    spread_sq = jnp.mean(centred * centred, axis=axis, keepdims=True)
    return centred * lax.rsqrt(spread_sq + 1e-05) * gain + bias


def triangle_update(
    pair_act,
    mask_float,
    layer_index,
    input_gain,
    input_bias,
    project_weight,
    gate_weight,
    output_gain,
    output_bias,
    output_weight,
    incoming,
):
    rows, cols = lax.axis_size("row"), lax.axis_size("col")
    peers = rows * cols
    rows_here, cols_here, channels_here = pair_act.shape
    width = output_weight.shape[1]
    own = width // peers
    pixels = rows_here * cols_here
    pair_float = pair_act.astype(jnp.float32).reshape(pixels, channels_here)
    normed = layer_norm(
        pair_float, input_gain[layer_index], input_bias[layer_index], -1
    ).astype(jnp.bfloat16)
    projected = lax.dot_general(
        project_weight[layer_index],
        normed,
        (((0,), (1,)), ((), ())),
        preferred_element_type=jnp.float32,
    ).reshape(4, peers, own, pixels)
    mask_row = mask_float.reshape(1, 1, pixels)
    left_proj = (jax.nn.sigmoid(projected[0]) * projected[1] * mask_row).astype(jnp.bfloat16)
    right_proj = (jax.nn.sigmoid(projected[2]) * projected[3] * mask_row).astype(jnp.bfloat16)
    both = jnp.concatenate([left_proj, right_proj], axis=1)
    both = lax.all_to_all(both, GRID, 0, 0)
    both = both.reshape(rows, cols, 2, own, rows_here, cols_here)
    both = both.transpose(2, 3, 0, 4, 1, 5).reshape(2, own, rows * rows_here, cols * cols_here)
    spec = "cki,ckj->cij" if incoming else "cik,cjk->cij"
    triangle = jnp.einsum(spec, both[0], both[1], preferred_element_type=jnp.float32)
    triangle = triangle.astype(jnp.bfloat16).reshape(own, rows, rows_here, cols, cols_here)
    triangle = triangle.transpose(1, 3, 0, 2, 4).reshape(peers, own, pixels)
    triangle = lax.all_to_all(triangle, GRID, 0, 0).reshape(width, pixels)
    normed_sum = layer_norm(
        triangle.astype(jnp.float32),
        output_gain[layer_index][:, None],
        output_bias[layer_index][:, None],
        0,
    ).astype(jnp.bfloat16)
    gate_value = jax.nn.sigmoid(
        jnp.dot(normed, gate_weight[layer_index], preferred_element_type=jnp.float32)
    )
    mapped = lax.dot_general(
        normed_sum,
        output_weight[layer_index],
        (((0,), (0,)), ((), ())),
        preferred_element_type=jnp.float32,
    )
    return (
        (pair_float + gate_value * mapped)
        .astype(jnp.bfloat16)
        .reshape(rows_here, cols_here, channels_here)
    )


def shards(pair_act, pair_mask, *params):
    mask_float = pair_mask.astype(jnp.float32)
    for index in range(2):
        pair_act = triangle_update(pair_act, mask_float, index, *params, index == 1)
    return pair_act


def solution(mesh):
    def updates(pair_act, pair_mask, *params):
        body, grid, cols = shards, mesh, "col"
        if fits(mesh, pair_act.shape[1], params[-1].shape[1]):
            sizes = mesh.devices.shape
            grid = jax.sharding.Mesh(
                mesh.devices.reshape(*sizes[:2], 2, sizes[2] // 2), ("groups", "row", "zh", "zl")
            )
            body, cols = by_kernels, ("zh", "zl")
        pixels = (("groups", "row"), cols)
        return jax.shard_map(
            body,
            mesh=grid,
            in_specs=(P(*pixels, None), P(*pixels)) + (P(),) * 7,
            out_specs=P(*pixels, None),
            check_vma=False,
        )(pair_act, pair_mask, *params)

    return updates
```

```python
import functools

import jax
import jax.numpy as jnp
from jax import lax
from jax.experimental import pallas as pl
from jax.experimental.pallas import tpu as pltpu
from jax.sharding import PartitionSpec as P

GRID = ("row", "col")
LANES = 128


IN_GAIN, IN_BIAS, OUT_GAIN, OUT_BIAS = range(4)


def channel_norm(values, gain, bias):
    average = jnp.mean(values, axis=0, keepdims=True)
    centred = values - average
    spread_sq = jnp.mean(centred * centred, axis=0, keepdims=True)
    return centred * lax.rsqrt(spread_sq + 1e-05) * gain + bias


def dot(left, right):
    return jnp.dot(left, right, preferred_element_type=jnp.float32)


def norm_of(values, small_ref, update, which):
    at = 4 * update + which
    return channel_norm(values, small_ref[:, at : at + 1], small_ref[:, at + 1 : at + 2])


def emit_projections(peers, update, zt, mask, small_ref, weight_ref, lr_ref):
    width = lr_ref.shape[0] // 2
    own = width // peers
    tile = zt.shape[1]
    normed = norm_of(zt, small_ref, update, IN_GAIN) * mask
    projected = dot(weight_ref[update, : 4 * width], normed.astype(jnp.bfloat16))
    left = (jnp.tanh(projected[:width]) + 1.0) * projected[width : 2 * width]
    right = (jnp.tanh(projected[2 * width : 3 * width]) + 1.0) * projected[3 * width :]
    both = jnp.concatenate(
        [left.reshape(peers, own, tile), right.reshape(peers, own, tile)], axis=1
    )
    lr_ref[...] = both.reshape(2 * width, tile).astype(jnp.bfloat16)


def pack_kernel(cuts, tile, z_ref, mask_ref, *refs):
    out_refs, (held_ref, z_sems, mask_sems, out_sems) = refs[:-4], refs[-4:]
    part_refs, (own_ref, next_ref) = out_refs[:-2], out_refs[-2:]
    upper = lax.axis_index("groups")
    home = upper == lax.axis_index("zh")
    per_strip = cuts[-1]
    rows = held_ref.shape[2]
    fetches = []
    for which in range(2):
        strip = lax.rem(upper + 1 - which, 2)
        for t in range(per_strip):
            at = pl.multiple_of((strip * per_strip + t) * tile, tile)
            fetches.append(
                pltpu.make_async_copy(
                    z_ref.at[pl.ds(at, tile)], held_ref.at[which, t, 0:tile], z_sems.at[which, t]
                )
            )
            fetches.append(
                pltpu.make_async_copy(
                    mask_ref.at[strip * per_strip + t], held_ref.at[which, t, tile:rows],
                    mask_sems.at[which, t],
                )
            )
    stores = [
        pltpu.make_async_copy(held_ref.at[0, begin:end], part_ref, out_sems.at[k])
        for k, (begin, end, part_ref) in enumerate(zip((0, *cuts), cuts, part_refs))
    ]
    stores += [
        pltpu.make_async_copy(held_ref.at[1], own_ref, out_sems.at[len(cuts)]),
        pltpu.make_async_copy(
            held_ref.at[1 - home.astype(jnp.int32)], next_ref, out_sems.at[len(cuts) + 1]
        ),
    ]
    for fetch in fetches:
        fetch.start()
    for fetch in fetches[: 2 * per_strip]:
        fetch.wait()
    for store in stores[: len(cuts)]:
        store.start()
    for fetch in fetches[2 * per_strip :]:
        fetch.wait()
    for store in stores[len(cuts) :]:
        store.start()
    for store in stores:
        store.wait()


def first_kernel(peers, parts, own_ref, *refs):
    far_refs, (small_ref, weight_ref), (lr_ref, zt_ref, mask_ref) = (
        refs[: len(parts)], refs[len(parts) : -3], refs[-3:],
    )
    home = lax.axis_index("groups") == lax.axis_index("zh")
    step = pl.program_id(0)
    tile = zt_ref.shape[1]

    def put(z_ref):
        zt_ref[...] = z_ref[0, :tile].astype(jnp.float32).T.astype(jnp.bfloat16)
        marks = z_ref[0, tile:].astype(jnp.float32)
        flat = jnp.concatenate([marks[k : k + 1] for k in range(tile // LANES)], axis=1)
        mask_ref[...] = jnp.broadcast_to(flat, mask_ref.shape).astype(jnp.bfloat16)

    pl.when(home)(lambda: put(own_ref))
    for (begin, end), far_ref in zip(parts, far_refs):
        here = jnp.logical_and(step >= begin, step < end)
        pl.when(jnp.logical_and(jnp.logical_not(home), here))(functools.partial(put, far_ref))
    zt = zt_ref[...].astype(jnp.float32)
    mask = mask_ref[...].astype(jnp.float32)[:1]
    emit_projections(peers, 0, zt, mask, small_ref, weight_ref, lr_ref)


def gate_kernel(update, zt_ref, small_ref, weight_ref, gate_ref):
    channels = gate_ref.shape[0]
    normed = norm_of(zt_ref[...].astype(jnp.float32), small_ref, update, IN_GAIN)
    at = weight_ref.shape[1] - 2 * channels
    gates = dot(weight_ref[update, at : at + channels], normed.astype(jnp.bfloat16))
    gate_ref[...] = (0.5 * jnp.tanh(gates) + 0.5).astype(jnp.bfloat16)


def updated(update, t_ref, zt_ref, gate_ref, small_ref, weight_ref):
    normed_sum = norm_of(t_ref[...].astype(jnp.float32), small_ref, update, OUT_GAIN)
    at = weight_ref.shape[1] - zt_ref.shape[0]
    mapped = dot(weight_ref[update, at:], normed_sum.astype(jnp.bfloat16))
    return zt_ref[...].astype(jnp.float32) + gate_ref[...].astype(jnp.float32) * mapped


def middle_kernel(
    peers, t_ref, zt_ref, gate_ref, mask_ref, small_ref, weight_ref, lr_ref, out_ref
):
    fresh = updated(0, t_ref, zt_ref, gate_ref, small_ref, weight_ref).astype(jnp.bfloat16)
    out_ref[...] = fresh
    mask = mask_ref[...].astype(jnp.float32)[:1]
    emit_projections(peers, 1, fresh.astype(jnp.float32), mask, small_ref, weight_ref, lr_ref)


def last_kernel(t_ref, zt_ref, gate_ref, small_ref, weight_ref, out_ref):
    fresh = updated(1, t_ref, zt_ref, gate_ref, small_ref, weight_ref)
    out_ref[...] = fresh.T.astype(jnp.bfloat16)


def assemble_kernel(here_ref, beside_ref, back_ref, across_ref, out_ref, held_ref, in_sems, out_sems):
    upper = lax.axis_index("groups")
    home = upper == lax.axis_index("zh")
    parts = in_sems.shape[1]
    size = here_ref.shape[0] // parts

    def move(*sources):
        pieces = [(which, k, slice(k * size, (k + 1) * size)) for k in range(parts) for which in range(2)]
        fetches = [
            pltpu.make_async_copy(
                sources[which].at[rows], held_ref.at[which, rows], in_sems.at[which, k]
            )
            for which, k, rows in pieces
        ]
        stores = [
            pltpu.make_async_copy(
                held_ref.at[which, rows], out_ref.at[lax.rem(upper + which, 2), rows],
                out_sems.at[which, k],
            )
            for which, k, rows in pieces
        ]
        for fetch in fetches:
            fetch.start()
        for fetch, store in zip(fetches, stores):
            fetch.wait()
            store.start()
        for store in stores:
            store.wait()

    pl.when(home)(lambda: move(here_ref, back_ref))
    pl.when(jnp.logical_not(home))(lambda: move(beside_ref, across_ref))


def triangle_kernel(blocks, side, own, incoming, made, x_ref, y_ref, left_ref, right_ref, rows_ref, tiles_ref):
    step = pl.program_id(0)
    zh = lax.axis_index("zh")
    pair = 2 * own
    span = 4 * side
    strip = side // 2
    half = blocks // 2
    pitch_rows = pair + 1
    lane = lax.broadcasted_iota(jnp.int32, (pair, LANES), 1)
    inside = lane < side

    wanted = range(blocks) if len(made) == 2 else range(made[0] * half, (made[0] + 1) * half)

    @pl.when(step < blocks)
    def _unpack():
        upper, row_pair = step // half, lax.rem(step, half)
        mirror = lax.rem(row_pair + zh, 2)
        for r in range(2):
            at = pl.multiple_of((row_pair * 2 + r) * side + upper * strip, 16)
            if incoming:
                at_right = at
            else:
                at_right = pl.multiple_of((mirror * 2 + r) * LANES + upper * strip, 16)
            for zl in range(half):
                for piece in range(2):
                    first = piece * strip * side
                    for group in range(strip // 4):
                        x = x_ref[
                            (r * half + zl) * pair : (r * half + zl + 1) * pair,
                            first + group * span : first + (group + 1) * span,
                        ].astype(jnp.float32)
                        a, b, c = x[:, :LANES], x[:, LANES : 2 * LANES], x[:, 2 * LANES :]
                        picked = (
                            a,
                            pltpu.roll(jnp.where(lane >= 96, a, b), 32, 1),
                            pltpu.roll(jnp.where(lane >= 64, b, c), 64, 1),
                            pltpu.roll(c, 96, 1),
                        )
                        for k, row in enumerate(picked):
                            rows_ref[pl.ds((group * 4 + k) * pitch_rows, pair), :] = jnp.where(
                                inside, row, 0.0
                            )
                    lanes = slice((piece * half + zl) * LANES, (piece * half + zl + 1) * LANES)
                    for ch in range(own):
                        left_ref[ch, pl.ds(at, strip), lanes] = rows_ref[
                            pl.ds(ch, strip, stride=pitch_rows), :
                        ].astype(jnp.bfloat16)
                        if incoming and piece not in made:
                            continue
                        right_ref[ch, pl.ds(at_right, strip), lanes] = rows_ref[
                            pl.ds(own + ch, strip, stride=pitch_rows), :
                        ].astype(jnp.bfloat16)

    @pl.when(step == blocks - 1)
    def _multiply():
        contract = ((0,), (0,)) if incoming else ((1,), (1,))
        for ch in range(own):
            right = right_ref[ch]
            if incoming:
                right = right[:, wanted[0] * LANES : (wanted[-1] + 1) * LANES]
            product = lax.dot_general(
                left_ref[ch], right, (contract, ((), ())), preferred_element_type=jnp.float32
            )
            for place in range(blocks):
                if incoming:
                    row, pitch = lax.rem(place // 2 + zh, 2) * 2 + place % 2, LANES
                else:
                    row, pitch = place, side
                for upper in range(2):
                    for col in range(len(wanted)):
                        tiles_ref[
                            col // half,
                            upper * blocks + row,
                            pl.ds((col % half) * own + ch, strip, stride=pitch_rows),
                            :,
                        ] = product[
                            place * pitch + upper * strip : place * pitch + (upper + 1) * strip,
                            col * LANES : (col + 1) * LANES,
                        ]

    @pl.when(step >= blocks)
    def _repack():
        for r in range(2):
            place = (step - blocks) * 2 + r
            for piece in range(len(made)):
                first = piece * strip * side
                for group in range(strip // 4):
                    p, q, t, s = (
                        tiles_ref[piece, place, pl.ds((group * 4 + k) * pitch_rows, pair), :]
                        for k in range(4)
                    )
                    q, t, s = pltpu.roll(q, 96, 1), pltpu.roll(t, 64, 1), pltpu.roll(s, 32, 1)
                    flat = jnp.concatenate(
                        [
                            jnp.where(inside, p, q),
                            jnp.where(lane < 64, q, t),
                            jnp.where(lane < 32, t, s),
                        ],
                        axis=1,
                    )
                    y_ref[
                        r * pair : (r + 1) * pair, first + group * span : first + (group + 1) * span
                    ] = flat.astype(jnp.bfloat16)


def fits(mesh, residues, width):
    rows, cols = mesh.shape["row"], mesh.shape["col"]
    return (
        mesh.shape["groups"] == 2
        and rows == 4
        and cols == 4
        and 4 * residues == 3 * LANES * cols
        and width == 8 * rows * cols
    )


def in_hbm(array):
    return pltpu.with_memory_space_constraint(array, pltpu.HBM)


def whole_spec(array):
    return pl.BlockSpec(array.shape, lambda i: (0,) * array.ndim)


def triangle_call(received, made, blocks, side, own, incoming):
    pair = 2 * own
    pixels = side * side
    padded = blocks * LANES
    strip = side // 2
    left_rows = blocks * side
    right_rows = left_rows if incoming else padded
    return pl.pallas_call(
        functools.partial(triangle_kernel, blocks, side, own, incoming, made),
        grid=(2 * blocks,),
        in_specs=[
            pl.BlockSpec((blocks * pair, pixels), lambda i: (jnp.minimum(i, blocks - 1), 0))
        ],
        out_specs=pl.BlockSpec(
            (2 * pair, pixels // 2 * len(made)), lambda i: (jnp.maximum(i - blocks, 0), 0)
        ),
        out_shape=pltpu.HBM((blocks * blocks * own, pixels // 2 * len(made)), jnp.bfloat16),
        scratch_shapes=[
            pltpu.VMEM((own, left_rows, padded), jnp.bfloat16),
            pltpu.VMEM((own, right_rows, padded), jnp.bfloat16),
            pltpu.VMEM((strip * (pair + 1), LANES), jnp.float32),
            pltpu.VMEM((len(made), 2 * blocks, strip * (pair + 1), LANES), jnp.float32),
        ],
        compiler_params=pltpu.CompilerParams(vmem_limit_bytes=48 * 1024 * 1024),
        cost_estimate=pl.CostEstimate(
            flops=own * (blocks * side) ** 3 * len(made),
            bytes_accessed=12 * blocks * blocks * pair * pixels // 2,
            transcendentals=0,
        ),
    )(received)


def pixel_call(body, tiled, fixed, outs, steps, tile, flops, start=0, pixels=None, kept=(), scratch=(), row_major_out=False):
    pixels = pixels or steps * tile

    def spec(channels, first, count, row_major):
        if row_major:
            return pl.BlockSpec(
                (tile, channels), lambda i: (jnp.clip(i + first, 0, count - 1), 0)
            )
        return pl.BlockSpec((channels, tile), lambda i: (0, jnp.clip(i + first, 0, count - 1)))

    def packed(a, first, count):
        return pl.BlockSpec(
            (1, *a.shape[1:]), lambda i: (jnp.clip(i + first, 0, count - 1), 0, 0)
        )

    in_specs = [
        packed(a, first, count) if a.ndim == 3 else spec(a.shape[0], first, count, False)
        for a, first, count in tiled
    ]
    in_specs += [whole_spec(a) for a in fixed]
    in_specs += [pl.BlockSpec(memory_space=pl.ANY)] * len(kept)
    n_in, n_kept = len(in_specs), len(kept)

    def kernel(*refs):
        body(*refs[: n_in - n_kept], *refs[n_in:])

    return pl.pallas_call(
        kernel,
        grid=(steps,),
        in_specs=in_specs,
        out_specs=[spec(ch, start, pixels // tile, row_major_out) for ch in outs],
        out_shape=[
            pltpu.HBM((pixels, ch) if row_major_out else (ch, pixels), jnp.bfloat16)
            for ch in outs
        ],
        input_output_aliases={n_in - n_kept + k: k for k in range(n_kept)},
        scratch_shapes=list(scratch),
        compiler_params=pltpu.CompilerParams(vmem_limit_bytes=48 * 1024 * 1024),
        cost_estimate=pl.CostEstimate(
            flops=flops, bytes_accessed=2 * steps * tile * (sum(outs) + 256), transcendentals=0
        ),
    )(*(a for a, *_ in tiled), *fixed, *kept)


LINE = ("groups", "zh")
CUBE = ("groups", "row", "zl")


def pack(pair_act, mask, cuts, tile):
    per_strip = cuts[-1]
    shape = (tile + mask.shape[1], pair_act.shape[1])
    outs = [end - begin for begin, end in zip((0, *cuts), cuts)] + [per_strip, per_strip]
    anywhere = pl.BlockSpec(memory_space=pltpu.HBM)
    return pl.pallas_call(
        functools.partial(pack_kernel, cuts, tile),
        in_specs=[anywhere] * 2,
        out_specs=[anywhere] * len(outs),
        out_shape=[pltpu.HBM((n, *shape), jnp.bfloat16) for n in outs],
        scratch_shapes=[
            pltpu.VMEM((2, per_strip, *shape), jnp.bfloat16),
            pltpu.SemaphoreType.DMA((2, per_strip)),
            pltpu.SemaphoreType.DMA((2, per_strip)),
            pltpu.SemaphoreType.DMA((len(outs),)),
        ],
        compiler_params=pltpu.CompilerParams(vmem_limit_bytes=48 * 1024 * 1024),
    )(in_hbm(pair_act), mask)


def by_kernels(
    pair_act,
    pair_mask,
    input_gain,
    input_bias,
    project_weight,
    gate_weight,
    output_gain,
    output_bias,
    output_weight,
):
    blocks = lax.axis_size("row")
    peers = blocks * blocks
    side, _, channels = pair_act.shape
    width = output_weight.shape[1]
    own = width // peers
    pixels = side * side
    strip = side // 2
    mult = 2 * channels

    tile = 9 * LANES
    per_piece = pixels // 2 // tile
    cuts = (1, per_piece - 1, per_piece)
    marks = pair_mask.astype(jnp.bfloat16).reshape(2 * per_piece, tile // LANES, LANES)
    marks = jnp.pad(marks, ((0, 0), (0, 16 - tile // LANES), (0, 0)))
    *z_parts, z_own, z_next = pack(pair_act.reshape(pixels, channels), marks, cuts, tile)
    z_far = []
    for part in z_parts[:-1]:
        over = lax.ppermute(part, LINE, ((1, 3), (2, 0)))
        z_far.append(lax.ppermute(over, LINE, ((0, 1), (3, 2))))
    z_near = lax.ppermute(z_next, LINE, ((1, 0), (2, 3), (0, 2), (3, 1)))
    z_far.append(lax.ppermute(z_parts[-1], LINE, ((1, 2), (2, 1))))
    small = jnp.stack([input_gain, input_bias, output_gain, output_bias], axis=1)
    small = small.reshape(-1, channels).T
    weights = jnp.concatenate(
        [project_weight * 0.5, gate_weight * 0.5, output_weight], axis=2
    ).transpose(0, 2, 1)
    fixed = (small, weights)

    def first(piece, ours, far, parts, kept):
        tiled = [(ours, 0, per_piece)]
        tiled += [(part, -begin, end - begin) for part, (begin, end) in zip(far, parts)]
        return pixel_call(
            functools.partial(first_kernel, peers, parts),
            tiled, fixed, (2 * width, channels, 16), per_piece, tile, pixels // 2 * mult * 4 * width,
            start=piece * per_piece, pixels=pixels, kept=kept,
        )

    z_near = in_hbm(z_near)
    begun = first(0, z_own, [z_near], [(0, per_piece)], ())
    sent, zt, mask = first(1, z_near, z_far, list(zip((0, *cuts), cuts)), begun)
    wide = 2 * tile
    steps = pixels // wide

    def gate_of(zt, u):
        return pixel_call(
            functools.partial(gate_kernel, u), [(zt, 0, steps)], fixed, (channels,),
            steps, wide, pixels * mult * channels,
        )[0]

    def exchange(array):
        there = lax.all_to_all(array.reshape(peers, -1, array.shape[1]), CUBE, 0, 0)
        return there.reshape(array.shape)

    gate = gate_of(zt, 0)
    triangle = exchange(triangle_call(exchange(sent), (0, 1), blocks, side, own, False))
    sent, zt = pixel_call(
        functools.partial(middle_kernel, peers),
        [(a, 0, steps) for a in (triangle, zt, gate, mask)], fixed, (2 * width, channels),
        steps, wide, pixels * mult * 5 * width,
    )
    gate = gate_of(zt, 1)
    received = exchange(sent)
    product = lambda piece: triangle_call(received, (piece,), blocks, side, own, True)

    def finish(piece, triangle):
        at = piece * steps // 2
        return pixel_call(
            last_kernel,
            [(triangle, 0, steps // 2), (zt, at, steps), (gate, at, steps)],
            fixed, (channels,), steps // 2, wide, pixels // 2 * mult * channels, row_major_out=True,
        )[0]

    there = finish(1, exchange(product(1)))
    beside, across = (
        lax.ppermute(there, LINE, pairs) for pairs in (((0, 1), (3, 2)), ((1, 2), (2, 1)))
    )
    there, waiting = lax.optimization_barrier((there, product(0)))
    here = finish(0, exchange(waiting))
    back = lax.ppermute(here, LINE, ((1, 3), (2, 0)))
    return pl.pallas_call(
        assemble_kernel,
        in_specs=[pl.BlockSpec(memory_space=pl.ANY)] * 4,
        out_specs=pl.BlockSpec(memory_space=pl.ANY),
        out_shape=pltpu.HBM((2, *here.shape), here.dtype),
        scratch_shapes=[
            pltpu.VMEM((2, *here.shape), here.dtype),
            pltpu.SemaphoreType.DMA((2, 2)),
            pltpu.SemaphoreType.DMA((2, 2)),
        ],
        compiler_params=pltpu.CompilerParams(vmem_limit_bytes=48 * 1024 * 1024),
    )(*map(in_hbm, (here, beside, back, across))).reshape(side, side, channels)


def layer_norm(values, gain, bias, axis):
    average = jnp.mean(values, axis=axis, keepdims=True)
    centred = values - average
    spread_sq = jnp.mean(centred * centred, axis=axis, keepdims=True)
    return centred * lax.rsqrt(spread_sq + 1e-05) * gain + bias


def triangle_update(
    pair_act,
    mask_float,
    layer_index,
    input_gain,
    input_bias,
    project_weight,
    gate_weight,
    output_gain,
    output_bias,
    output_weight,
    incoming,
):
    rows, cols = lax.axis_size("row"), lax.axis_size("col")
    peers = rows * cols
    rows_here, cols_here, channels_here = pair_act.shape
    width = output_weight.shape[1]
    own = width // peers
    pixels = rows_here * cols_here
    pair_float = pair_act.astype(jnp.float32).reshape(pixels, channels_here)
    normed = layer_norm(
        pair_float, input_gain[layer_index], input_bias[layer_index], -1
    ).astype(jnp.bfloat16)
    projected = lax.dot_general(
        project_weight[layer_index],
        normed,
        (((0,), (1,)), ((), ())),
        preferred_element_type=jnp.float32,
    ).reshape(4, peers, own, pixels)
    mask_row = mask_float.reshape(1, 1, pixels)
    left_proj = (jax.nn.sigmoid(projected[0]) * projected[1] * mask_row).astype(jnp.bfloat16)
    right_proj = (jax.nn.sigmoid(projected[2]) * projected[3] * mask_row).astype(jnp.bfloat16)
    both = jnp.concatenate([left_proj, right_proj], axis=1)
    both = lax.all_to_all(both, GRID, 0, 0)
    both = both.reshape(rows, cols, 2, own, rows_here, cols_here)
    both = both.transpose(2, 3, 0, 4, 1, 5).reshape(2, own, rows * rows_here, cols * cols_here)
    spec = "cki,ckj->cij" if incoming else "cik,cjk->cij"
    triangle = jnp.einsum(spec, both[0], both[1], preferred_element_type=jnp.float32)
    triangle = triangle.astype(jnp.bfloat16).reshape(own, rows, rows_here, cols, cols_here)
    triangle = triangle.transpose(1, 3, 0, 2, 4).reshape(peers, own, pixels)
    triangle = lax.all_to_all(triangle, GRID, 0, 0).reshape(width, pixels)
    normed_sum = layer_norm(
        triangle.astype(jnp.float32),
        output_gain[layer_index][:, None],
        output_bias[layer_index][:, None],
        0,
    ).astype(jnp.bfloat16)
    gate_value = jax.nn.sigmoid(
        jnp.dot(normed, gate_weight[layer_index], preferred_element_type=jnp.float32)
    )
    mapped = lax.dot_general(
        normed_sum,
        output_weight[layer_index],
        (((0,), (0,)), ((), ())),
        preferred_element_type=jnp.float32,
    )
    return (
        (pair_float + gate_value * mapped)
        .astype(jnp.bfloat16)
        .reshape(rows_here, cols_here, channels_here)
    )


def shards(pair_act, pair_mask, *params):
    mask_float = pair_mask.astype(jnp.float32)
    for index in range(2):
        pair_act = triangle_update(pair_act, mask_float, index, *params, index == 1)
    return pair_act


def solution(mesh):
    def updates(pair_act, pair_mask, *params):
        body, grid, cols = shards, mesh, "col"
        if fits(mesh, pair_act.shape[1], params[-1].shape[1]):
            sizes = mesh.devices.shape
            grid = jax.sharding.Mesh(
                mesh.devices.reshape(*sizes[:2], 2, sizes[2] // 2), ("groups", "row", "zh", "zl")
            )
            body, cols = by_kernels, ("zh", "zl")
        pixels = (("groups", "row"), cols)
        return jax.shard_map(
            body,
            mesh=grid,
            in_specs=(P(*pixels, None), P(*pixels)) + (P(),) * 7,
            out_specs=P(*pixels, None),
            check_vma=False,
        )(pair_act, pair_mask, *params)

    return updates
```

```python
import functools

import jax
import jax.numpy as jnp
from jax import lax
from jax.experimental import pallas as pl
from jax.experimental.pallas import tpu as pltpu
from jax.sharding import PartitionSpec as P

GRID = ("row", "col")
LANES = 128


IN_GAIN, IN_BIAS, OUT_GAIN, OUT_BIAS = range(4)


def channel_norm(values, gain, bias):
    average = jnp.mean(values, axis=0, keepdims=True)
    centred = values - average
    spread_sq = jnp.mean(centred * centred, axis=0, keepdims=True)
    return centred * lax.rsqrt(spread_sq + 1e-05) * gain + bias


def dot(left, right):
    return jnp.dot(left, right, preferred_element_type=jnp.float32)


def norm_of(values, small_ref, update, which):
    at = 4 * update + which
    return channel_norm(values, small_ref[:, at : at + 1], small_ref[:, at + 1 : at + 2])


def emit_projections(peers, update, zt, mask, small_ref, weight_ref, lr_ref):
    width = lr_ref.shape[0] // 2
    own = width // peers
    tile = zt.shape[1]
    normed = norm_of(zt, small_ref, update, IN_GAIN) * mask
    projected = dot(weight_ref[update, : 4 * width], normed.astype(jnp.bfloat16))
    left = (jnp.tanh(projected[:width]) + 1.0) * projected[width : 2 * width]
    right = (jnp.tanh(projected[2 * width : 3 * width]) + 1.0) * projected[3 * width :]
    both = jnp.concatenate(
        [left.reshape(peers, own, tile), right.reshape(peers, own, tile)], axis=1
    )
    lr_ref[...] = both.reshape(2 * width, tile).astype(jnp.bfloat16)


def pack_kernel(cuts, tile, z_ref, mask_ref, *refs):
    out_refs, (held_ref, z_sems, mask_sems, out_sems) = refs[:-4], refs[-4:]
    part_refs, (*next_refs, own_ref) = out_refs[: len(cuts)], out_refs[len(cuts) :]
    upper = lax.axis_index("groups")
    home = upper == lax.axis_index("zh")
    per_strip = cuts[-1]
    rows = held_ref.shape[2]
    fetches = []
    for which in range(2):
        strip = lax.rem(upper + 1 - which, 2)
        for t in range(per_strip):
            at = pl.multiple_of((strip * per_strip + t) * tile, tile)
            fetches.append(
                pltpu.make_async_copy(
                    z_ref.at[pl.ds(at, tile)], held_ref.at[which, t, 0:tile], z_sems.at[which, t]
                )
            )
            fetches.append(
                pltpu.make_async_copy(
                    mask_ref.at[strip * per_strip + t], held_ref.at[which, t, tile:rows],
                    mask_sems.at[which, t],
                )
            )
    stores = [
        pltpu.make_async_copy(held_ref.at[0, begin:end], part_ref, out_sems.at[k])
        for k, (begin, end, part_ref) in enumerate(zip((0, *cuts), cuts, part_refs))
    ]
    stores += [
        pltpu.make_async_copy(
            held_ref.at[1 - home.astype(jnp.int32), begin:end], next_ref, out_sems.at[len(cuts) + k]
        )
        for k, (begin, end, next_ref) in enumerate(
            zip((0, per_strip - 1), (per_strip - 1, per_strip), next_refs)
        )
    ]
    stores.append(pltpu.make_async_copy(held_ref.at[1], own_ref, out_sems.at[len(cuts) + 2]))
    for fetch in fetches:
        fetch.start()
    for fetch in fetches[: 2 * per_strip]:
        fetch.wait()
    for store in stores[: len(cuts)]:
        store.start()
    for fetch in fetches[2 * per_strip :]:
        fetch.wait()
    for store in stores[len(cuts) :]:
        store.start()
    for store in stores:
        store.wait()


def first_kernel(peers, sources, *refs):
    z_refs, (small_ref, weight_ref), (lr_ref, zt_ref, mask_ref) = (
        refs[: len(sources)], refs[len(sources) : -3], refs[-3:],
    )
    home = lax.axis_index("groups") == lax.axis_index("zh")
    step = pl.program_id(0)
    tile = zt_ref.shape[1]

    def put(z_ref):
        zt_ref[...] = z_ref[0, :tile].astype(jnp.float32).T.astype(jnp.bfloat16)
        marks = z_ref[0, tile:].astype(jnp.float32)
        flat = jnp.concatenate([marks[k : k + 1] for k in range(tile // LANES)], axis=1)
        mask_ref[...] = jnp.broadcast_to(flat, mask_ref.shape).astype(jnp.bfloat16)

    for (begin, end, at_home), z_ref in zip(sources, z_refs):
        here = jnp.logical_and(step >= begin, step < end)
        whose = home if at_home else jnp.logical_not(home)
        pl.when(jnp.logical_and(whose, here))(functools.partial(put, z_ref))
    zt = zt_ref[...].astype(jnp.float32)
    mask = mask_ref[...].astype(jnp.float32)[:1]
    emit_projections(peers, 0, zt, mask, small_ref, weight_ref, lr_ref)


def gate_kernel(update, zt_ref, small_ref, weight_ref, gate_ref):
    channels = gate_ref.shape[0]
    normed = norm_of(zt_ref[...].astype(jnp.float32), small_ref, update, IN_GAIN)
    at = weight_ref.shape[1] - 2 * channels
    gates = dot(weight_ref[update, at : at + channels], normed.astype(jnp.bfloat16))
    gate_ref[...] = (0.5 * jnp.tanh(gates) + 0.5).astype(jnp.bfloat16)


def updated(update, t_ref, zt_ref, gate_ref, small_ref, weight_ref):
    normed_sum = norm_of(t_ref[...].astype(jnp.float32), small_ref, update, OUT_GAIN)
    at = weight_ref.shape[1] - zt_ref.shape[0]
    mapped = dot(weight_ref[update, at:], normed_sum.astype(jnp.bfloat16))
    return zt_ref[...].astype(jnp.float32) + gate_ref[...].astype(jnp.float32) * mapped


def middle_kernel(
    peers, t_ref, zt_ref, gate_ref, mask_ref, small_ref, weight_ref, lr_ref, out_ref
):
    fresh = updated(0, t_ref, zt_ref, gate_ref, small_ref, weight_ref).astype(jnp.bfloat16)
    out_ref[...] = fresh
    mask = mask_ref[...].astype(jnp.float32)[:1]
    emit_projections(peers, 1, fresh.astype(jnp.float32), mask, small_ref, weight_ref, lr_ref)


def last_kernel(t_ref, zt_ref, gate_ref, small_ref, weight_ref, out_ref):
    fresh = updated(1, t_ref, zt_ref, gate_ref, small_ref, weight_ref)
    out_ref[...] = fresh.T.astype(jnp.bfloat16)


def assemble_kernel(here_ref, beside_ref, back_ref, across_ref, out_ref, held_ref, in_sems, out_sems):
    upper = lax.axis_index("groups")
    home = upper == lax.axis_index("zh")
    parts = in_sems.shape[1]
    size = here_ref.shape[0] // parts

    def move(*sources):
        pieces = [(which, k, slice(k * size, (k + 1) * size)) for k in range(parts) for which in range(2)]
        fetches = [
            pltpu.make_async_copy(
                sources[which].at[rows], held_ref.at[which, rows], in_sems.at[which, k]
            )
            for which, k, rows in pieces
        ]
        stores = [
            pltpu.make_async_copy(
                held_ref.at[which, rows], out_ref.at[lax.rem(upper + which, 2), rows],
                out_sems.at[which, k],
            )
            for which, k, rows in pieces
        ]
        for fetch in fetches:
            fetch.start()
        for fetch, store in zip(fetches, stores):
            fetch.wait()
            store.start()
        for store in stores:
            store.wait()

    pl.when(home)(lambda: move(here_ref, back_ref))
    pl.when(jnp.logical_not(home))(lambda: move(beside_ref, across_ref))


def triangle_kernel(blocks, side, own, incoming, made, x_ref, y_ref, left_ref, right_ref, rows_ref, tiles_ref):
    step = pl.program_id(0)
    zh = lax.axis_index("zh")
    pair = 2 * own
    span = 4 * side
    strip = side // 2
    half = blocks // 2
    pitch_rows = pair + 1
    lane = lax.broadcasted_iota(jnp.int32, (pair, LANES), 1)
    inside = lane < side

    wanted = range(blocks) if len(made) == 2 else range(made[0] * half, (made[0] + 1) * half)

    @pl.when(step < blocks)
    def _unpack():
        upper, row_pair = step // half, lax.rem(step, half)
        mirror = lax.rem(row_pair + zh, 2)
        for r in range(2):
            at = pl.multiple_of((row_pair * 2 + r) * side + upper * strip, 16)
            if incoming:
                at_right = at
            else:
                at_right = pl.multiple_of((mirror * 2 + r) * LANES + upper * strip, 16)
            for zl in range(half):
                for piece in range(2):
                    first = piece * strip * side
                    for group in range(strip // 4):
                        x = x_ref[
                            (r * half + zl) * pair : (r * half + zl + 1) * pair,
                            first + group * span : first + (group + 1) * span,
                        ].astype(jnp.float32)
                        a, b, c = x[:, :LANES], x[:, LANES : 2 * LANES], x[:, 2 * LANES :]
                        picked = (
                            a,
                            pltpu.roll(jnp.where(lane >= 96, a, b), 32, 1),
                            pltpu.roll(jnp.where(lane >= 64, b, c), 64, 1),
                            pltpu.roll(c, 96, 1),
                        )
                        for k, row in enumerate(picked):
                            rows_ref[pl.ds((group * 4 + k) * pitch_rows, pair), :] = jnp.where(
                                inside, row, 0.0
                            )
                    lanes = slice((piece * half + zl) * LANES, (piece * half + zl + 1) * LANES)
                    for ch in range(own):
                        left_ref[ch, pl.ds(at, strip), lanes] = rows_ref[
                            pl.ds(ch, strip, stride=pitch_rows), :
                        ].astype(jnp.bfloat16)
                        if incoming and piece not in made:
                            continue
                        right_ref[ch, pl.ds(at_right, strip), lanes] = rows_ref[
                            pl.ds(own + ch, strip, stride=pitch_rows), :
                        ].astype(jnp.bfloat16)

    @pl.when(step == blocks - 1)
    def _multiply():
        contract = ((0,), (0,)) if incoming else ((1,), (1,))
        for ch in range(own):
            right = right_ref[ch]
            if incoming:
                right = right[:, wanted[0] * LANES : (wanted[-1] + 1) * LANES]
            product = lax.dot_general(
                left_ref[ch], right, (contract, ((), ())), preferred_element_type=jnp.float32
            )
            for place in range(blocks):
                if incoming:
                    row, pitch = lax.rem(place // 2 + zh, 2) * 2 + place % 2, LANES
                else:
                    row, pitch = place, side
                for upper in range(2):
                    for col in range(len(wanted)):
                        tiles_ref[
                            col // half,
                            upper * blocks + row,
                            pl.ds((col % half) * own + ch, strip, stride=pitch_rows),
                            :,
                        ] = product[
                            place * pitch + upper * strip : place * pitch + (upper + 1) * strip,
                            col * LANES : (col + 1) * LANES,
                        ]

    @pl.when(step >= blocks)
    def _repack():
        for r in range(2):
            place = (step - blocks) * 2 + r
            for piece in range(len(made)):
                first = piece * strip * side
                for group in range(strip // 4):
                    p, q, t, s = (
                        tiles_ref[piece, place, pl.ds((group * 4 + k) * pitch_rows, pair), :]
                        for k in range(4)
                    )
                    q, t, s = pltpu.roll(q, 96, 1), pltpu.roll(t, 64, 1), pltpu.roll(s, 32, 1)
                    flat = jnp.concatenate(
                        [
                            jnp.where(inside, p, q),
                            jnp.where(lane < 64, q, t),
                            jnp.where(lane < 32, t, s),
                        ],
                        axis=1,
                    )
                    y_ref[
                        r * pair : (r + 1) * pair, first + group * span : first + (group + 1) * span
                    ] = flat.astype(jnp.bfloat16)


def fits(mesh, residues, width):
    rows, cols = mesh.shape["row"], mesh.shape["col"]
    return (
        mesh.shape["groups"] == 2
        and rows == 4
        and cols == 4
        and 4 * residues == 3 * LANES * cols
        and width == 8 * rows * cols
    )


def whole_spec(array):
    return pl.BlockSpec(array.shape, lambda i: (0,) * array.ndim)


def triangle_call(received, made, blocks, side, own, incoming):
    pair = 2 * own
    pixels = side * side
    padded = blocks * LANES
    strip = side // 2
    left_rows = blocks * side
    right_rows = left_rows if incoming else padded
    return pl.pallas_call(
        functools.partial(triangle_kernel, blocks, side, own, incoming, made),
        grid=(2 * blocks,),
        in_specs=[
            pl.BlockSpec((blocks * pair, pixels), lambda i: (jnp.minimum(i, blocks - 1), 0))
        ],
        out_specs=pl.BlockSpec(
            (2 * pair, pixels // 2 * len(made)), lambda i: (jnp.maximum(i - blocks, 0), 0)
        ),
        out_shape=pltpu.HBM((blocks * blocks * own, pixels // 2 * len(made)), jnp.bfloat16),
        scratch_shapes=[
            pltpu.VMEM((own, left_rows, padded), jnp.bfloat16),
            pltpu.VMEM((own, right_rows, padded), jnp.bfloat16),
            pltpu.VMEM((strip * (pair + 1), LANES), jnp.float32),
            pltpu.VMEM((len(made), 2 * blocks, strip * (pair + 1), LANES), jnp.float32),
        ],
        compiler_params=pltpu.CompilerParams(vmem_limit_bytes=48 * 1024 * 1024),
        cost_estimate=pl.CostEstimate(
            flops=own * (blocks * side) ** 3 * len(made),
            bytes_accessed=12 * blocks * blocks * pair * pixels // 2,
            transcendentals=0,
        ),
    )(received)


def pixel_call(body, tiled, fixed, outs, steps, tile, flops, start=0, pixels=None, kept=(), scratch=(), row_major_out=False):
    pixels = pixels or steps * tile

    def spec(channels, first, count, row_major):
        if row_major:
            return pl.BlockSpec(
                (tile, channels), lambda i: (jnp.clip(i + first, 0, count - 1), 0)
            )
        return pl.BlockSpec((channels, tile), lambda i: (0, jnp.clip(i + first, 0, count - 1)))

    def packed(a, first, count):
        return pl.BlockSpec(
            (1, *a.shape[1:]), lambda i: (jnp.clip(i + first, 0, count - 1), 0, 0)
        )

    in_specs = [
        packed(a, first, count) if a.ndim == 3 else spec(a.shape[0], first, count, False)
        for a, first, count in tiled
    ]
    in_specs += [whole_spec(a) for a in fixed]
    in_specs += [pl.BlockSpec(memory_space=pl.ANY)] * len(kept)
    n_in, n_kept = len(in_specs), len(kept)

    def kernel(*refs):
        body(*refs[: n_in - n_kept], *refs[n_in:])

    return pl.pallas_call(
        kernel,
        grid=(steps,),
        in_specs=in_specs,
        out_specs=[spec(ch, start, pixels // tile, row_major_out) for ch in outs],
        out_shape=[
            pltpu.HBM((pixels, ch) if row_major_out else (ch, pixels), jnp.bfloat16)
            for ch in outs
        ],
        input_output_aliases={n_in - n_kept + k: k for k in range(n_kept)},
        scratch_shapes=list(scratch),
        compiler_params=pltpu.CompilerParams(vmem_limit_bytes=48 * 1024 * 1024),
        cost_estimate=pl.CostEstimate(
            flops=flops, bytes_accessed=2 * steps * tile * (sum(outs) + 256), transcendentals=0
        ),
    )(*(a for a, *_ in tiled), *fixed, *kept)


LINE = ("groups", "zh")
CUBE = ("groups", "row", "zl")


def pack(pair_act, mask, cuts, tile):
    per_strip = cuts[-1]
    shape = (tile + mask.shape[1], pair_act.shape[1])
    outs = [end - begin for begin, end in zip((0, *cuts), cuts)] + [per_strip - 1, 1, per_strip]
    anywhere = pl.BlockSpec(memory_space=pltpu.HBM)
    return pl.pallas_call(
        functools.partial(pack_kernel, cuts, tile),
        in_specs=[anywhere] * 2,
        out_specs=[anywhere] * len(outs),
        out_shape=[pltpu.HBM((n, *shape), jnp.bfloat16) for n in outs],
        scratch_shapes=[
            pltpu.VMEM((2, per_strip, *shape), jnp.bfloat16),
            pltpu.SemaphoreType.DMA((2, per_strip)),
            pltpu.SemaphoreType.DMA((2, per_strip)),
            pltpu.SemaphoreType.DMA((len(outs),)),
        ],
        compiler_params=pltpu.CompilerParams(vmem_limit_bytes=48 * 1024 * 1024),
    )(pair_act, mask)


def by_kernels(
    pair_act,
    pair_mask,
    input_gain,
    input_bias,
    project_weight,
    gate_weight,
    output_gain,
    output_bias,
    output_weight,
):
    blocks = lax.axis_size("row")
    peers = blocks * blocks
    side, _, channels = pair_act.shape
    width = output_weight.shape[1]
    own = width // peers
    pixels = side * side
    strip = side // 2
    mult = 2 * channels

    tile = 9 * LANES
    per_piece = pixels // 2 // tile
    cuts = (1, per_piece - 1, per_piece)
    marks = pair_mask.astype(jnp.bfloat16).reshape(2 * per_piece, tile // LANES, LANES)
    marks = jnp.pad(marks, ((0, 0), (0, 16 - tile // LANES), (0, 0)))
    *z_parts, z_next, z_last, z_own = pack(pair_act.reshape(pixels, channels), marks, cuts, tile)
    z_far = []
    for part in z_parts[:-1]:
        over = lax.ppermute(part, LINE, ((1, 3), (2, 0)))
        z_far.append(lax.ppermute(over, LINE, ((0, 1), (3, 2))))
    z_near, z_rest = (
        lax.ppermute(part, LINE, ((1, 0), (2, 3), (0, 2), (3, 1))) for part in (z_next, z_last)
    )
    z_far.append(lax.ppermute(z_parts[-1], LINE, ((1, 2), (2, 1))))
    small = jnp.stack([input_gain, input_bias, output_gain, output_bias], axis=1)
    small = small.reshape(-1, channels).T
    weights = jnp.concatenate(
        [project_weight * 0.5, gate_weight * 0.5, output_weight], axis=2
    ).transpose(0, 2, 1)
    fixed = (small, weights)

    def first(start, steps, sources, kept):
        return pixel_call(
            functools.partial(first_kernel, peers, [served for _, _, *served in sources]),
            [(a, at - begin, a.shape[0]) for a, at, begin, *_ in sources],
            fixed, (2 * width, channels, 16), steps, tile, steps * tile * mult * 4 * width,
            start=start, pixels=pixels, kept=kept,
        )

    soon = per_piece - 1
    begun = first(0, soon, [(z_own, 0, 0, soon, True), (z_near, 0, 0, soon, False)], ())
    sources = [(z_own, soon, 0, 1, True), (z_near, 0, 1, per_piece, True), (z_rest, 0, per_piece, per_piece + 1, True)]
    sources += [(z_rest, 0, 0, 1, False)]
    sources += [
        (part, 0, 1 + begin, 1 + end, False) for part, begin, end in zip(z_far, (0, *cuts), cuts)
    ]
    sent, zt, mask = first(soon, per_piece + 1, sources, begun)
    wide = 2 * tile
    steps = pixels // wide

    def gate_of(zt, u):
        return pixel_call(
            functools.partial(gate_kernel, u), [(zt, 0, steps)], fixed, (channels,),
            steps, wide, pixels * mult * channels,
        )[0]

    def exchange(array):
        there = lax.all_to_all(array.reshape(peers, -1, array.shape[1]), CUBE, 0, 0)
        return there.reshape(array.shape)

    gate = gate_of(zt, 0)
    triangle = exchange(triangle_call(exchange(sent), (0, 1), blocks, side, own, False))
    sent, zt = pixel_call(
        functools.partial(middle_kernel, peers),
        [(a, 0, steps) for a in (triangle, zt, gate, mask)], fixed, (2 * width, channels),
        steps, wide, pixels * mult * 5 * width,
    )
    gate = gate_of(zt, 1)
    received = exchange(sent)
    product = lambda piece: triangle_call(received, (piece,), blocks, side, own, True)

    def finish(piece, triangle):
        at = piece * steps // 2
        return pixel_call(
            last_kernel,
            [(triangle, 0, steps // 2), (zt, at, steps), (gate, at, steps)],
            fixed, (channels,), steps // 2, wide, pixels // 2 * mult * channels, row_major_out=True,
        )[0]

    there = finish(1, exchange(product(1)))
    beside, across = (
        lax.ppermute(there, LINE, pairs) for pairs in (((0, 1), (3, 2)), ((1, 2), (2, 1)))
    )
    there, waiting = lax.optimization_barrier((there, product(0)))
    here = finish(0, exchange(waiting))
    back = lax.ppermute(here, LINE, ((1, 3), (2, 0)))
    return pl.pallas_call(
        assemble_kernel,
        in_specs=[pl.BlockSpec(memory_space=pl.ANY)] * 4,
        out_specs=pl.BlockSpec(memory_space=pl.ANY),
        out_shape=pltpu.HBM((2, *here.shape), here.dtype),
        scratch_shapes=[
            pltpu.VMEM((2, *here.shape), here.dtype),
            pltpu.SemaphoreType.DMA((2, 2)),
            pltpu.SemaphoreType.DMA((2, 2)),
        ],
        compiler_params=pltpu.CompilerParams(vmem_limit_bytes=48 * 1024 * 1024),
    )(here, beside, back, across).reshape(side, side, channels)


def layer_norm(values, gain, bias, axis):
    average = jnp.mean(values, axis=axis, keepdims=True)
    centred = values - average
    spread_sq = jnp.mean(centred * centred, axis=axis, keepdims=True)
    return centred * lax.rsqrt(spread_sq + 1e-05) * gain + bias


def triangle_update(
    pair_act,
    mask_float,
    layer_index,
    input_gain,
    input_bias,
    project_weight,
    gate_weight,
    output_gain,
    output_bias,
    output_weight,
    incoming,
):
    rows, cols = lax.axis_size("row"), lax.axis_size("col")
    peers = rows * cols
    rows_here, cols_here, channels_here = pair_act.shape
    width = output_weight.shape[1]
    own = width // peers
    pixels = rows_here * cols_here
    pair_float = pair_act.astype(jnp.float32).reshape(pixels, channels_here)
    normed = layer_norm(
        pair_float, input_gain[layer_index], input_bias[layer_index], -1
    ).astype(jnp.bfloat16)
    projected = lax.dot_general(
        project_weight[layer_index],
        normed,
        (((0,), (1,)), ((), ())),
        preferred_element_type=jnp.float32,
    ).reshape(4, peers, own, pixels)
    mask_row = mask_float.reshape(1, 1, pixels)
    left_proj = (jax.nn.sigmoid(projected[0]) * projected[1] * mask_row).astype(jnp.bfloat16)
    right_proj = (jax.nn.sigmoid(projected[2]) * projected[3] * mask_row).astype(jnp.bfloat16)
    both = jnp.concatenate([left_proj, right_proj], axis=1)
    both = lax.all_to_all(both, GRID, 0, 0)
    both = both.reshape(rows, cols, 2, own, rows_here, cols_here)
    both = both.transpose(2, 3, 0, 4, 1, 5).reshape(2, own, rows * rows_here, cols * cols_here)
    spec = "cki,ckj->cij" if incoming else "cik,cjk->cij"
    triangle = jnp.einsum(spec, both[0], both[1], preferred_element_type=jnp.float32)
    triangle = triangle.astype(jnp.bfloat16).reshape(own, rows, rows_here, cols, cols_here)
    triangle = triangle.transpose(1, 3, 0, 2, 4).reshape(peers, own, pixels)
    triangle = lax.all_to_all(triangle, GRID, 0, 0).reshape(width, pixels)
    normed_sum = layer_norm(
        triangle.astype(jnp.float32),
        output_gain[layer_index][:, None],
        output_bias[layer_index][:, None],
        0,
    ).astype(jnp.bfloat16)
    gate_value = jax.nn.sigmoid(
        jnp.dot(normed, gate_weight[layer_index], preferred_element_type=jnp.float32)
    )
    mapped = lax.dot_general(
        normed_sum,
        output_weight[layer_index],
        (((0,), (0,)), ((), ())),
        preferred_element_type=jnp.float32,
    )
    return (
        (pair_float + gate_value * mapped)
        .astype(jnp.bfloat16)
        .reshape(rows_here, cols_here, channels_here)
    )


def shards(pair_act, pair_mask, *params):
    mask_float = pair_mask.astype(jnp.float32)
    for index in range(2):
        pair_act = triangle_update(pair_act, mask_float, index, *params, index == 1)
    return pair_act


def solution(mesh):
    def updates(pair_act, pair_mask, *params):
        body, grid, cols = shards, mesh, "col"
        if fits(mesh, pair_act.shape[1], params[-1].shape[1]):
            sizes = mesh.devices.shape
            grid = jax.sharding.Mesh(
                mesh.devices.reshape(*sizes[:2], 2, sizes[2] // 2), ("groups", "row", "zh", "zl")
            )
            body, cols = by_kernels, ("zh", "zl")
        pixels = (("groups", "row"), cols)
        return jax.shard_map(
            body,
            mesh=grid,
            in_specs=(P(*pixels, None), P(*pixels)) + (P(),) * 7,
            out_specs=P(*pixels, None),
            check_vma=False,
        )(pair_act, pair_mask, *params)

    return updates
```

```python
import functools

import jax
import jax.numpy as jnp
from jax import lax
from jax.experimental import pallas as pl
from jax.experimental.pallas import tpu as pltpu
from jax.sharding import PartitionSpec as P

GRID = ("row", "col")
LANES = 128


IN_GAIN, IN_BIAS, OUT_GAIN, OUT_BIAS = range(4)


def channel_norm(values, gain, bias):
    average = jnp.mean(values, axis=0, keepdims=True)
    centred = values - average
    spread_sq = jnp.mean(centred * centred, axis=0, keepdims=True)
    return centred * lax.rsqrt(spread_sq + 1e-05) * gain + bias


def dot(left, right):
    return jnp.dot(left, right, preferred_element_type=jnp.float32)


def norm_of(values, small_ref, update, which):
    at = 4 * update + which
    return channel_norm(values, small_ref[:, at : at + 1], small_ref[:, at + 1 : at + 2])


def emit_projections(peers, update, zt, mask, small_ref, weight_ref, lr_ref):
    width = lr_ref.shape[0] // 2
    own = width // peers
    tile = zt.shape[1]
    normed = norm_of(zt, small_ref, update, IN_GAIN) * mask
    projected = dot(weight_ref[update, : 4 * width], normed.astype(jnp.bfloat16))
    left = (jnp.tanh(projected[:width]) + 1.0) * projected[width : 2 * width]
    right = (jnp.tanh(projected[2 * width : 3 * width]) + 1.0) * projected[3 * width :]
    both = jnp.concatenate(
        [left.reshape(peers, own, tile), right.reshape(peers, own, tile)], axis=1
    )
    lr_ref[...] = both.reshape(2 * width, tile).astype(jnp.bfloat16)


def pack_kernel(cuts, tile, z_ref, mask_ref, *refs):
    out_refs, (held_ref, z_sems, mask_sems, out_sems) = refs[:-4], refs[-4:]
    part_refs, (next_ref, own_ref) = out_refs[:-2], out_refs[-2:]
    upper = lax.axis_index("groups")
    home = upper == lax.axis_index("zh")
    per_strip = cuts[-1]
    rows = held_ref.shape[2]
    fetches = []
    for which in range(2):
        strip = lax.rem(upper + 1 - which, 2)
        for t in range(per_strip):
            at = pl.multiple_of((strip * per_strip + t) * tile, tile)
            fetches.append(
                pltpu.make_async_copy(
                    z_ref.at[pl.ds(at, tile)], held_ref.at[which, t, 0:tile], z_sems.at[which, t]
                )
            )
            fetches.append(
                pltpu.make_async_copy(
                    mask_ref.at[strip * per_strip + t], held_ref.at[which, t, tile:rows],
                    mask_sems.at[which, t],
                )
            )
    stores = [
        pltpu.make_async_copy(held_ref.at[0, begin:end], part_ref, out_sems.at[k])
        for k, (begin, end, part_ref) in enumerate(zip((0, *cuts), cuts, part_refs))
    ]
    stores += [
        pltpu.make_async_copy(
            held_ref.at[1 - home.astype(jnp.int32)], next_ref, out_sems.at[len(cuts)]
        ),
        pltpu.make_async_copy(held_ref.at[1], own_ref, out_sems.at[len(cuts) + 1]),
    ]
    for fetch in fetches:
        fetch.start()
    for fetch in fetches[: 2 * per_strip]:
        fetch.wait()
    for store in stores[: len(cuts)]:
        store.start()
    for fetch in fetches[2 * per_strip :]:
        fetch.wait()
    for store in stores[len(cuts) :]:
        store.start()
    for store in stores:
        store.wait()


def first_kernel(peers, sources, *refs):
    z_refs, (small_ref, weight_ref), (lr_ref, zt_ref, mask_ref) = (
        refs[: len(sources)], refs[len(sources) : -3], refs[-3:],
    )
    home = lax.axis_index("groups") == lax.axis_index("zh")
    step = pl.program_id(0)
    tile = zt_ref.shape[1]

    def put(z_ref):
        zt_ref[...] = z_ref[0, :tile].astype(jnp.float32).T.astype(jnp.bfloat16)
        marks = z_ref[0, tile:].astype(jnp.float32)
        flat = jnp.concatenate([marks[k : k + 1] for k in range(tile // LANES)], axis=1)
        mask_ref[...] = jnp.broadcast_to(flat, mask_ref.shape).astype(jnp.bfloat16)

    for (begin, end, at_home), z_ref in zip(sources, z_refs):
        here = jnp.logical_and(step >= begin, step < end)
        whose = home if at_home else jnp.logical_not(home)
        pl.when(jnp.logical_and(whose, here))(functools.partial(put, z_ref))
    zt = zt_ref[...].astype(jnp.float32)
    mask = mask_ref[...].astype(jnp.float32)[:1]
    emit_projections(peers, 0, zt, mask, small_ref, weight_ref, lr_ref)


def gate_kernel(update, zt_ref, small_ref, weight_ref, gate_ref):
    channels = gate_ref.shape[0]
    normed = norm_of(zt_ref[...].astype(jnp.float32), small_ref, update, IN_GAIN)
    at = weight_ref.shape[1] - 2 * channels
    gates = dot(weight_ref[update, at : at + channels], normed.astype(jnp.bfloat16))
    gate_ref[...] = (0.5 * jnp.tanh(gates) + 0.5).astype(jnp.bfloat16)


def updated(update, t_ref, zt_ref, gate_ref, small_ref, weight_ref):
    normed_sum = norm_of(t_ref[...].astype(jnp.float32), small_ref, update, OUT_GAIN)
    at = weight_ref.shape[1] - zt_ref.shape[0]
    mapped = dot(weight_ref[update, at:], normed_sum.astype(jnp.bfloat16))
    return zt_ref[...].astype(jnp.float32) + gate_ref[...].astype(jnp.float32) * mapped


def middle_kernel(
    peers, t_ref, zt_ref, gate_ref, mask_ref, small_ref, weight_ref, lr_ref, out_ref
):
    fresh = updated(0, t_ref, zt_ref, gate_ref, small_ref, weight_ref).astype(jnp.bfloat16)
    out_ref[...] = fresh
    mask = mask_ref[...].astype(jnp.float32)[:1]
    emit_projections(peers, 1, fresh.astype(jnp.float32), mask, small_ref, weight_ref, lr_ref)


def last_kernel(t_ref, zt_ref, gate_ref, small_ref, weight_ref, out_ref):
    fresh = updated(1, t_ref, zt_ref, gate_ref, small_ref, weight_ref)
    out_ref[...] = fresh.T.astype(jnp.bfloat16)


def assemble_kernel(here_ref, beside_ref, back_ref, across_ref, out_ref, held_ref, in_sems, out_sems):
    upper = lax.axis_index("groups")
    home = upper == lax.axis_index("zh")
    parts = in_sems.shape[1]
    size = here_ref.shape[0] // parts

    def move(*sources):
        pieces = [(which, k, slice(k * size, (k + 1) * size)) for k in range(parts) for which in range(2)]
        fetches = [
            pltpu.make_async_copy(
                sources[which].at[rows], held_ref.at[which, rows], in_sems.at[which, k]
            )
            for which, k, rows in pieces
        ]
        stores = [
            pltpu.make_async_copy(
                held_ref.at[which, rows], out_ref.at[lax.rem(upper + which, 2), rows],
                out_sems.at[which, k],
            )
            for which, k, rows in pieces
        ]
        for fetch in fetches:
            fetch.start()
        for fetch, store in zip(fetches, stores):
            fetch.wait()
            store.start()
        for store in stores:
            store.wait()

    pl.when(home)(lambda: move(here_ref, back_ref))
    pl.when(jnp.logical_not(home))(lambda: move(beside_ref, across_ref))


def triangle_kernel(blocks, side, own, incoming, made, x_ref, y_ref, left_ref, right_ref, rows_ref, tiles_ref):
    step = pl.program_id(0)
    zh = lax.axis_index("zh")
    pair = 2 * own
    span = 4 * side
    strip = side // 2
    half = blocks // 2
    pitch_rows = pair + 1
    lane = lax.broadcasted_iota(jnp.int32, (pair, LANES), 1)
    inside = lane < side

    wanted = range(blocks) if len(made) == 2 else range(made[0] * half, (made[0] + 1) * half)

    @pl.when(step < blocks)
    def _unpack():
        upper, row_pair = step // half, lax.rem(step, half)
        mirror = lax.rem(row_pair + zh, 2)
        for r in range(2):
            at = pl.multiple_of((row_pair * 2 + r) * side + upper * strip, 16)
            if incoming:
                at_right = at
            else:
                at_right = pl.multiple_of((mirror * 2 + r) * LANES + upper * strip, 16)
            for zl in range(half):
                for piece in range(2):
                    first = piece * strip * side
                    for group in range(strip // 4):
                        x = x_ref[
                            (r * half + zl) * pair : (r * half + zl + 1) * pair,
                            first + group * span : first + (group + 1) * span,
                        ].astype(jnp.float32)
                        a, b, c = x[:, :LANES], x[:, LANES : 2 * LANES], x[:, 2 * LANES :]
                        picked = (
                            a,
                            pltpu.roll(jnp.where(lane >= 96, a, b), 32, 1),
                            pltpu.roll(jnp.where(lane >= 64, b, c), 64, 1),
                            pltpu.roll(c, 96, 1),
                        )
                        for k, row in enumerate(picked):
                            rows_ref[pl.ds((group * 4 + k) * pitch_rows, pair), :] = jnp.where(
                                inside, row, 0.0
                            )
                    lanes = slice((piece * half + zl) * LANES, (piece * half + zl + 1) * LANES)
                    for ch in range(own):
                        left_ref[ch, pl.ds(at, strip), lanes] = rows_ref[
                            pl.ds(ch, strip, stride=pitch_rows), :
                        ].astype(jnp.bfloat16)
                        if incoming and piece not in made:
                            continue
                        right_ref[ch, pl.ds(at_right, strip), lanes] = rows_ref[
                            pl.ds(own + ch, strip, stride=pitch_rows), :
                        ].astype(jnp.bfloat16)

    @pl.when(step == blocks - 1)
    def _multiply():
        contract = ((0,), (0,)) if incoming else ((1,), (1,))
        for ch in range(own):
            right = right_ref[ch]
            if incoming:
                right = right[:, wanted[0] * LANES : (wanted[-1] + 1) * LANES]
            product = lax.dot_general(
                left_ref[ch], right, (contract, ((), ())), preferred_element_type=jnp.float32
            )
            for place in range(blocks):
                if incoming:
                    row, pitch = lax.rem(place // 2 + zh, 2) * 2 + place % 2, LANES
                else:
                    row, pitch = place, side
                for upper in range(2):
                    for col in range(len(wanted)):
                        tiles_ref[
                            col // half,
                            upper * blocks + row,
                            pl.ds((col % half) * own + ch, strip, stride=pitch_rows),
                            :,
                        ] = product[
                            place * pitch + upper * strip : place * pitch + (upper + 1) * strip,
                            col * LANES : (col + 1) * LANES,
                        ]

    @pl.when(step >= blocks)
    def _repack():
        for r in range(2):
            place = (step - blocks) * 2 + r
            for piece in range(len(made)):
                first = piece * strip * side
                for group in range(strip // 4):
                    p, q, t, s = (
                        tiles_ref[piece, place, pl.ds((group * 4 + k) * pitch_rows, pair), :]
                        for k in range(4)
                    )
                    q, t, s = pltpu.roll(q, 96, 1), pltpu.roll(t, 64, 1), pltpu.roll(s, 32, 1)
                    flat = jnp.concatenate(
                        [
                            jnp.where(inside, p, q),
                            jnp.where(lane < 64, q, t),
                            jnp.where(lane < 32, t, s),
                        ],
                        axis=1,
                    )
                    y_ref[
                        r * pair : (r + 1) * pair, first + group * span : first + (group + 1) * span
                    ] = flat.astype(jnp.bfloat16)


def fits(mesh, residues, width):
    rows, cols = mesh.shape["row"], mesh.shape["col"]
    return (
        mesh.shape["groups"] == 2
        and rows == 4
        and cols == 4
        and 4 * residues == 3 * LANES * cols
        and width == 8 * rows * cols
    )


def whole_spec(array):
    return pl.BlockSpec(array.shape, lambda i: (0,) * array.ndim)


def triangle_call(received, made, blocks, side, own, incoming):
    pair = 2 * own
    pixels = side * side
    padded = blocks * LANES
    strip = side // 2
    left_rows = blocks * side
    right_rows = left_rows if incoming else padded
    return pl.pallas_call(
        functools.partial(triangle_kernel, blocks, side, own, incoming, made),
        grid=(2 * blocks,),
        in_specs=[
            pl.BlockSpec((blocks * pair, pixels), lambda i: (jnp.minimum(i, blocks - 1), 0))
        ],
        out_specs=pl.BlockSpec(
            (2 * pair, pixels // 2 * len(made)), lambda i: (jnp.maximum(i - blocks, 0), 0)
        ),
        out_shape=pltpu.HBM((blocks * blocks * own, pixels // 2 * len(made)), jnp.bfloat16),
        scratch_shapes=[
            pltpu.VMEM((own, left_rows, padded), jnp.bfloat16),
            pltpu.VMEM((own, right_rows, padded), jnp.bfloat16),
            pltpu.VMEM((strip * (pair + 1), LANES), jnp.float32),
            pltpu.VMEM((len(made), 2 * blocks, strip * (pair + 1), LANES), jnp.float32),
        ],
        compiler_params=pltpu.CompilerParams(vmem_limit_bytes=48 * 1024 * 1024),
        cost_estimate=pl.CostEstimate(
            flops=own * (blocks * side) ** 3 * len(made),
            bytes_accessed=12 * blocks * blocks * pair * pixels // 2,
            transcendentals=0,
        ),
    )(received)


def pixel_call(body, tiled, fixed, outs, steps, tile, flops, start=0, pixels=None, kept=(), scratch=(), row_major_out=False):
    pixels = pixels or steps * tile

    def spec(channels, first, count, row_major):
        if row_major:
            return pl.BlockSpec(
                (tile, channels), lambda i: (jnp.clip(i + first, 0, count - 1), 0)
            )
        return pl.BlockSpec((channels, tile), lambda i: (0, jnp.clip(i + first, 0, count - 1)))

    def packed(a, first, count):
        return pl.BlockSpec(
            (1, *a.shape[1:]), lambda i: (jnp.clip(i + first, 0, count - 1), 0, 0)
        )

    in_specs = [
        packed(a, first, count) if a.ndim == 3 else spec(a.shape[0], first, count, False)
        for a, first, count in tiled
    ]
    in_specs += [whole_spec(a) for a in fixed]
    in_specs += [pl.BlockSpec(memory_space=pl.ANY)] * len(kept)
    n_in, n_kept = len(in_specs), len(kept)

    def kernel(*refs):
        body(*refs[: n_in - n_kept], *refs[n_in:])

    return pl.pallas_call(
        kernel,
        grid=(steps,),
        in_specs=in_specs,
        out_specs=[spec(ch, start, pixels // tile, row_major_out) for ch in outs],
        out_shape=[
            pltpu.HBM((pixels, ch) if row_major_out else (ch, pixels), jnp.bfloat16)
            for ch in outs
        ],
        input_output_aliases={n_in - n_kept + k: k for k in range(n_kept)},
        scratch_shapes=list(scratch),
        compiler_params=pltpu.CompilerParams(vmem_limit_bytes=48 * 1024 * 1024),
        cost_estimate=pl.CostEstimate(
            flops=flops, bytes_accessed=2 * steps * tile * (sum(outs) + 256), transcendentals=0
        ),
    )(*(a for a, *_ in tiled), *fixed, *kept)


LINE = ("groups", "zh")
CUBE = ("groups", "row", "zl")


def pack(pair_act, mask, cuts, tile):
    per_strip = cuts[-1]
    shape = (tile + mask.shape[1], pair_act.shape[1])
    outs = [end - begin for begin, end in zip((0, *cuts), cuts)] + [per_strip, per_strip]
    anywhere = pl.BlockSpec(memory_space=pltpu.HBM)
    return pl.pallas_call(
        functools.partial(pack_kernel, cuts, tile),
        in_specs=[anywhere] * 2,
        out_specs=[anywhere] * len(outs),
        out_shape=[pltpu.HBM((n, *shape), jnp.bfloat16) for n in outs],
        scratch_shapes=[
            pltpu.VMEM((2, per_strip, *shape), jnp.bfloat16),
            pltpu.SemaphoreType.DMA((2, per_strip)),
            pltpu.SemaphoreType.DMA((2, per_strip)),
            pltpu.SemaphoreType.DMA((len(outs),)),
        ],
        compiler_params=pltpu.CompilerParams(vmem_limit_bytes=48 * 1024 * 1024),
    )(pair_act, mask)


def by_kernels(
    pair_act,
    pair_mask,
    input_gain,
    input_bias,
    project_weight,
    gate_weight,
    output_gain,
    output_bias,
    output_weight,
):
    blocks = lax.axis_size("row")
    peers = blocks * blocks
    side, _, channels = pair_act.shape
    width = output_weight.shape[1]
    own = width // peers
    pixels = side * side
    strip = side // 2
    mult = 2 * channels

    tile = 9 * LANES
    per_piece = pixels // 2 // tile
    cuts = (1, per_piece - 1, per_piece)
    marks = pair_mask.astype(jnp.bfloat16).reshape(2 * per_piece, tile // LANES, LANES)
    marks = jnp.pad(marks, ((0, 0), (0, 16 - tile // LANES), (0, 0)))
    *z_parts, z_next, z_own = pack(pair_act.reshape(pixels, channels), marks, cuts, tile)
    z_far = []
    for part in z_parts[:-1]:
        over = lax.ppermute(part, LINE, ((1, 3), (2, 0)))
        z_far.append(lax.ppermute(over, LINE, ((0, 1), (3, 2))))
    z_near = lax.ppermute(z_next, LINE, ((1, 0), (2, 3), (0, 2), (3, 1)))
    z_far.append(lax.ppermute(z_parts[-1], LINE, ((1, 2), (2, 1))))
    small = jnp.stack([input_gain, input_bias, output_gain, output_bias], axis=1)
    small = small.reshape(-1, channels).T
    weights = jnp.concatenate(
        [project_weight * 0.5, gate_weight * 0.5, output_weight], axis=2
    ).transpose(0, 2, 1)
    fixed = (small, weights)

    sources = [(z_own, 0, per_piece, True), (z_near, per_piece, 2 * per_piece, True)]
    sources += [(z_near, 0, per_piece, False)]
    sources += [
        (part, per_piece + begin, per_piece + end, False)
        for part, begin, end in zip(z_far, (0, *cuts), cuts)
    ]
    sent, zt, mask = pixel_call(
        functools.partial(first_kernel, peers, [served for _, *served in sources]),
        [(a, -begin, a.shape[0]) for a, begin, *_ in sources],
        fixed, (2 * width, channels, 16), 2 * per_piece, tile, pixels * mult * 4 * width,
    )
    wide = 2 * tile
    steps = pixels // wide

    def gate_of(zt, u):
        return pixel_call(
            functools.partial(gate_kernel, u), [(zt, 0, steps)], fixed, (channels,),
            steps, wide, pixels * mult * channels,
        )[0]

    def exchange(array):
        there = lax.all_to_all(array.reshape(peers, -1, array.shape[1]), CUBE, 0, 0)
        return there.reshape(array.shape)

    gate = gate_of(zt, 0)
    triangle = exchange(triangle_call(exchange(sent), (0, 1), blocks, side, own, False))
    sent, zt = pixel_call(
        functools.partial(middle_kernel, peers),
        [(a, 0, steps) for a in (triangle, zt, gate, mask)], fixed, (2 * width, channels),
        steps, wide, pixels * mult * 5 * width,
    )
    gate = gate_of(zt, 1)
    received = exchange(sent)
    product = lambda piece: triangle_call(received, (piece,), blocks, side, own, True)

    def finish(piece, triangle):
        at = piece * steps // 2
        return pixel_call(
            last_kernel,
            [(triangle, 0, steps // 2), (zt, at, steps), (gate, at, steps)],
            fixed, (channels,), steps // 2, wide, pixels // 2 * mult * channels, row_major_out=True,
        )[0]

    there = finish(1, exchange(product(1)))
    beside, across = (
        lax.ppermute(there, LINE, pairs) for pairs in (((0, 1), (3, 2)), ((1, 2), (2, 1)))
    )
    there, waiting = lax.optimization_barrier((there, product(0)))
    here = finish(0, exchange(waiting))
    back = lax.ppermute(here, LINE, ((1, 3), (2, 0)))
    return pl.pallas_call(
        assemble_kernel,
        in_specs=[pl.BlockSpec(memory_space=pl.ANY)] * 4,
        out_specs=pl.BlockSpec(memory_space=pl.ANY),
        out_shape=pltpu.HBM((2, *here.shape), here.dtype),
        scratch_shapes=[
            pltpu.VMEM((2, *here.shape), here.dtype),
            pltpu.SemaphoreType.DMA((2, 2)),
            pltpu.SemaphoreType.DMA((2, 2)),
        ],
        compiler_params=pltpu.CompilerParams(vmem_limit_bytes=48 * 1024 * 1024),
    )(here, beside, back, across).reshape(side, side, channels)


def layer_norm(values, gain, bias, axis):
    average = jnp.mean(values, axis=axis, keepdims=True)
    centred = values - average
    spread_sq = jnp.mean(centred * centred, axis=axis, keepdims=True)
    return centred * lax.rsqrt(spread_sq + 1e-05) * gain + bias


def triangle_update(
    pair_act,
    mask_float,
    layer_index,
    input_gain,
    input_bias,
    project_weight,
    gate_weight,
    output_gain,
    output_bias,
    output_weight,
    incoming,
):
    rows, cols = lax.axis_size("row"), lax.axis_size("col")
    peers = rows * cols
    rows_here, cols_here, channels_here = pair_act.shape
    width = output_weight.shape[1]
    own = width // peers
    pixels = rows_here * cols_here
    pair_float = pair_act.astype(jnp.float32).reshape(pixels, channels_here)
    normed = layer_norm(
        pair_float, input_gain[layer_index], input_bias[layer_index], -1
    ).astype(jnp.bfloat16)
    projected = lax.dot_general(
        project_weight[layer_index],
        normed,
        (((0,), (1,)), ((), ())),
        preferred_element_type=jnp.float32,
    ).reshape(4, peers, own, pixels)
    mask_row = mask_float.reshape(1, 1, pixels)
    left_proj = (jax.nn.sigmoid(projected[0]) * projected[1] * mask_row).astype(jnp.bfloat16)
    right_proj = (jax.nn.sigmoid(projected[2]) * projected[3] * mask_row).astype(jnp.bfloat16)
    both = jnp.concatenate([left_proj, right_proj], axis=1)
    both = lax.all_to_all(both, GRID, 0, 0)
    both = both.reshape(rows, cols, 2, own, rows_here, cols_here)
    both = both.transpose(2, 3, 0, 4, 1, 5).reshape(2, own, rows * rows_here, cols * cols_here)
    spec = "cki,ckj->cij" if incoming else "cik,cjk->cij"
    triangle = jnp.einsum(spec, both[0], both[1], preferred_element_type=jnp.float32)
    triangle = triangle.astype(jnp.bfloat16).reshape(own, rows, rows_here, cols, cols_here)
    triangle = triangle.transpose(1, 3, 0, 2, 4).reshape(peers, own, pixels)
    triangle = lax.all_to_all(triangle, GRID, 0, 0).reshape(width, pixels)
    normed_sum = layer_norm(
        triangle.astype(jnp.float32),
        output_gain[layer_index][:, None],
        output_bias[layer_index][:, None],
        0,
    ).astype(jnp.bfloat16)
    gate_value = jax.nn.sigmoid(
        jnp.dot(normed, gate_weight[layer_index], preferred_element_type=jnp.float32)
    )
    mapped = lax.dot_general(
        normed_sum,
        output_weight[layer_index],
        (((0,), (0,)), ((), ())),
        preferred_element_type=jnp.float32,
    )
    return (
        (pair_float + gate_value * mapped)
        .astype(jnp.bfloat16)
        .reshape(rows_here, cols_here, channels_here)
    )


def shards(pair_act, pair_mask, *params):
    mask_float = pair_mask.astype(jnp.float32)
    for index in range(2):
        pair_act = triangle_update(pair_act, mask_float, index, *params, index == 1)
    return pair_act


def solution(mesh):
    def updates(pair_act, pair_mask, *params):
        body, grid, cols = shards, mesh, "col"
        if fits(mesh, pair_act.shape[1], params[-1].shape[1]):
            sizes = mesh.devices.shape
            grid = jax.sharding.Mesh(
                mesh.devices.reshape(*sizes[:2], 2, sizes[2] // 2), ("groups", "row", "zh", "zl")
            )
            body, cols = by_kernels, ("zh", "zl")
        pixels = (("groups", "row"), cols)
        return jax.shard_map(
            body,
            mesh=grid,
            in_specs=(P(*pixels, None), P(*pixels)) + (P(),) * 7,
            out_specs=P(*pixels, None),
            check_vma=False,
        )(pair_act, pair_mask, *params)

    return updates
```

```python
import functools
import itertools

import jax
import jax.numpy as jnp
from jax import lax
from jax.experimental import pallas as pl
from jax.experimental.pallas import tpu as pltpu
from jax.sharding import PartitionSpec as P

GRID = ("row", "col")
LANES = 128
FOLD = 2


IN_GAIN, IN_BIAS, OUT_GAIN, OUT_BIAS = range(4)


def channel_norm(values, gain, bias):
    average = jnp.mean(values, axis=0, keepdims=True)
    centred = values - average
    spread_sq = jnp.mean(centred * centred, axis=0, keepdims=True)
    return centred * lax.rsqrt(spread_sq + 1e-05) * gain + bias


def dot(left, right):
    return jnp.dot(left, right, preferred_element_type=jnp.float32)


def norm_of(values, small_ref, update, which):
    at = 4 * update + which
    return channel_norm(values, small_ref[:, at : at + 1], small_ref[:, at + 1 : at + 2])


def emit_projections(peers, update, zt, mask, small_ref, weight_ref, lr_ref):
    width = lr_ref.shape[0] // 2
    own = width // peers
    tile = zt.shape[1]
    normed = norm_of(zt, small_ref, update, IN_GAIN) * mask
    projected = dot(weight_ref[update, : 4 * width], normed.astype(jnp.bfloat16))
    left = (jnp.tanh(projected[:width]) + 1.0) * projected[width : 2 * width]
    right = (jnp.tanh(projected[2 * width : 3 * width]) + 1.0) * projected[3 * width :]
    both = jnp.concatenate(
        [left.reshape(peers, own, tile), right.reshape(peers, own, tile)], axis=1
    )
    lr_ref[...] = both.reshape(2 * width, tile).astype(jnp.bfloat16)


def pack_kernel(cuts, tile, z_ref, mask_ref, *refs):
    out_refs, (held_ref, z_sems, mask_sems, out_sems) = refs[:-4], refs[-4:]
    part_refs, (own_ref, next_ref) = out_refs[:-2], out_refs[-2:]
    upper = lax.axis_index("groups")
    home = upper == lax.axis_index("zh")
    per_strip = cuts[-1]
    rows = held_ref.shape[2]
    fetches = []
    for which in range(2):
        strip = lax.rem(upper + 1 - which, 2)
        for t in range(per_strip):
            at = pl.multiple_of((strip * per_strip + t) * tile, tile)
            fetches.append(
                pltpu.make_async_copy(
                    z_ref.at[pl.ds(at, tile)], held_ref.at[which, t, 0:tile], z_sems.at[which, t]
                )
            )
            fetches.append(
                pltpu.make_async_copy(
                    mask_ref.at[strip * per_strip + t], held_ref.at[which, t, tile:rows],
                    mask_sems.at[which, t],
                )
            )
    stores = [
        pltpu.make_async_copy(held_ref.at[0, begin:end], part_ref, out_sems.at[k])
        for k, (begin, end, part_ref) in enumerate(zip((0, *cuts), cuts, part_refs))
    ]
    stores += [
        pltpu.make_async_copy(held_ref.at[1], own_ref, out_sems.at[len(cuts)]),
        pltpu.make_async_copy(
            held_ref.at[1 - home.astype(jnp.int32)], next_ref, out_sems.at[len(cuts) + 1]
        ),
    ]
    for fetch in fetches:
        fetch.start()
    for fetch in fetches[: 2 * per_strip]:
        fetch.wait()
    for store in stores[: len(cuts)]:
        store.start()
    for fetch in fetches[2 * per_strip :]:
        fetch.wait()
    for store in stores[len(cuts) :]:
        store.start()
    for store in stores:
        store.wait()


def first_kernel(peers, parts, own_ref, *refs):
    far_refs, (small_ref, weight_ref), (lr_ref, zt_ref, mask_ref) = (
        refs[: len(parts)], refs[len(parts) : -3], refs[-3:],
    )
    home = lax.axis_index("groups") == lax.axis_index("zh")
    step = pl.program_id(0)
    tile = zt_ref.shape[1]

    def put(z_ref):
        zt_ref[...] = z_ref[0, :tile].astype(jnp.float32).T.astype(jnp.bfloat16)
        marks = z_ref[0, tile:].astype(jnp.float32)
        flat = jnp.concatenate([marks[k : k + 1] for k in range(tile // LANES)], axis=1)
        mask_ref[...] = jnp.broadcast_to(flat, mask_ref.shape).astype(jnp.bfloat16)

    pl.when(home)(lambda: put(own_ref))
    for (begin, end), far_ref in zip(parts, far_refs):
        here = jnp.logical_and(step >= begin, step < end)
        pl.when(jnp.logical_and(jnp.logical_not(home), here))(functools.partial(put, far_ref))
    zt = zt_ref[...].astype(jnp.float32)
    mask = mask_ref[...].astype(jnp.float32)[:1]
    emit_projections(peers, 0, zt, mask, small_ref, weight_ref, lr_ref)


def gate_kernel(update, zt_ref, small_ref, weight_ref, gate_ref):
    channels = gate_ref.shape[0]
    normed = norm_of(zt_ref[...].astype(jnp.float32), small_ref, update, IN_GAIN)
    at = weight_ref.shape[1] - 2 * channels
    gates = dot(weight_ref[update, at : at + channels], normed.astype(jnp.bfloat16))
    gate_ref[...] = (0.5 * jnp.tanh(gates) + 0.5).astype(jnp.bfloat16)


def updated(update, t_ref, zt_ref, gate_ref, small_ref, weight_ref):
    normed_sum = norm_of(t_ref[...].astype(jnp.float32), small_ref, update, OUT_GAIN)
    at = weight_ref.shape[1] - zt_ref.shape[0]
    mapped = dot(weight_ref[update, at:], normed_sum.astype(jnp.bfloat16))
    return zt_ref[...].astype(jnp.float32) + gate_ref[...].astype(jnp.float32) * mapped


def middle_kernel(
    peers, t_ref, zt_ref, gate_ref, mask_ref, small_ref, weight_ref, lr_ref, out_ref
):
    fresh = updated(0, t_ref, zt_ref, gate_ref, small_ref, weight_ref).astype(jnp.bfloat16)
    out_ref[...] = fresh
    mask = mask_ref[...].astype(jnp.float32)[:1]
    emit_projections(peers, 1, fresh.astype(jnp.float32), mask, small_ref, weight_ref, lr_ref)


def last_kernel(t_ref, zt_ref, gate_ref, small_ref, weight_ref, out_ref):
    fresh = updated(1, t_ref, zt_ref, gate_ref, small_ref, weight_ref)
    out_ref[...] = fresh.T.astype(jnp.bfloat16)


def assemble_kernel(here_ref, beside_ref, back_ref, across_ref, out_ref, held_ref, in_sems, out_sems):
    upper = lax.axis_index("groups")
    home = upper == lax.axis_index("zh")
    parts = in_sems.shape[1]
    size = here_ref.shape[0] // parts

    def move(*sources):
        pieces = [(which, k, slice(k * size, (k + 1) * size)) for k in range(parts) for which in range(2)]
        fetches = [
            pltpu.make_async_copy(
                sources[which].at[rows], held_ref.at[which, rows], in_sems.at[which, k]
            )
            for which, k, rows in pieces
        ]
        stores = [
            pltpu.make_async_copy(
                held_ref.at[which, rows], out_ref.at[lax.rem(upper + which, 2), rows],
                out_sems.at[which, k],
            )
            for which, k, rows in pieces
        ]
        for fetch in fetches:
            fetch.start()
        for fetch, store in zip(fetches, stores):
            fetch.wait()
            store.start()
        for store in stores:
            store.wait()

    pl.when(home)(lambda: move(here_ref, back_ref))
    pl.when(jnp.logical_not(home))(lambda: move(beside_ref, across_ref))


def triangle_kernel(blocks, side, own, incoming, made, x_ref, y_ref, left_ref, right_ref, rows_ref, tiles_ref):
    step = pl.program_id(0)
    zh = lax.axis_index("zh")
    pair = 2 * own
    span = 4 * side
    strip = side // 2
    half = blocks // 2
    pitch_rows = pair + 1
    lane = lax.broadcasted_iota(jnp.int32, (pair, LANES), 1)
    inside = lane < side

    wanted = range(blocks) if len(made) == 2 else range(made[0] * half, (made[0] + 1) * half)

    @pl.when(step < blocks // FOLD)
    def _unpack():
        for fold, r in itertools.product(range(FOLD), range(2)):
            upper, row_pair = (step * FOLD + fold) // half, lax.rem(step * FOLD + fold, half)
            mirror = lax.rem(row_pair + zh, 2)
            source = (fold * 2 + r) * half
            at = pl.multiple_of((row_pair * 2 + r) * side + upper * strip, 16)
            if incoming:
                at_right = at
            else:
                at_right = pl.multiple_of((mirror * 2 + r) * LANES + upper * strip, 16)
            for zl in range(half):
                for piece in range(2):
                    first = piece * strip * side
                    for group in range(strip // 4):
                        x = x_ref[
                            (source + zl) * pair : (source + zl + 1) * pair,
                            first + group * span : first + (group + 1) * span,
                        ].astype(jnp.float32)
                        a, b, c = x[:, :LANES], x[:, LANES : 2 * LANES], x[:, 2 * LANES :]
                        picked = (
                            a,
                            pltpu.roll(jnp.where(lane >= 96, a, b), 32, 1),
                            pltpu.roll(jnp.where(lane >= 64, b, c), 64, 1),
                            pltpu.roll(c, 96, 1),
                        )
                        for k, row in enumerate(picked):
                            rows_ref[pl.ds((group * 4 + k) * pitch_rows, pair), :] = jnp.where(
                                inside, row, 0.0
                            )
                    lanes = slice((piece * half + zl) * LANES, (piece * half + zl + 1) * LANES)
                    for ch in range(own):
                        left_ref[ch, pl.ds(at, strip), lanes] = rows_ref[
                            pl.ds(ch, strip, stride=pitch_rows), :
                        ].astype(jnp.bfloat16)
                        if incoming and piece not in made:
                            continue
                        right_ref[ch, pl.ds(at_right, strip), lanes] = rows_ref[
                            pl.ds(own + ch, strip, stride=pitch_rows), :
                        ].astype(jnp.bfloat16)

    @pl.when(step == blocks // FOLD - 1)
    def _multiply():
        contract = ((0,), (0,)) if incoming else ((1,), (1,))
        for ch in range(own):
            right = right_ref[ch]
            if incoming:
                right = right[:, wanted[0] * LANES : (wanted[-1] + 1) * LANES]
            product = lax.dot_general(
                left_ref[ch], right, (contract, ((), ())), preferred_element_type=jnp.float32
            )
            for place in range(blocks):
                if incoming:
                    row, pitch = lax.rem(place // 2 + zh, 2) * 2 + place % 2, LANES
                else:
                    row, pitch = place, side
                for upper in range(2):
                    for col in range(len(wanted)):
                        tiles_ref[
                            col // half,
                            upper * blocks + row,
                            pl.ds((col % half) * own + ch, strip, stride=pitch_rows),
                            :,
                        ] = product[
                            place * pitch + upper * strip : place * pitch + (upper + 1) * strip,
                            col * LANES : (col + 1) * LANES,
                        ]

    @pl.when(step >= blocks // FOLD)
    def _repack():
        for r in range(2 * FOLD):
            place = (step - blocks // FOLD) * 2 * FOLD + r
            for piece in range(len(made)):
                first = piece * strip * side
                for group in range(strip // 4):
                    p, q, t, s = (
                        tiles_ref[piece, place, pl.ds((group * 4 + k) * pitch_rows, pair), :]
                        for k in range(4)
                    )
                    q, t, s = pltpu.roll(q, 96, 1), pltpu.roll(t, 64, 1), pltpu.roll(s, 32, 1)
                    flat = jnp.concatenate(
                        [
                            jnp.where(inside, p, q),
                            jnp.where(lane < 64, q, t),
                            jnp.where(lane < 32, t, s),
                        ],
                        axis=1,
                    )
                    y_ref[
                        r * pair : (r + 1) * pair, first + group * span : first + (group + 1) * span
                    ] = flat.astype(jnp.bfloat16)


def fits(mesh, residues, width):
    rows, cols = mesh.shape["row"], mesh.shape["col"]
    return (
        mesh.shape["groups"] == 2
        and rows == 4
        and cols == 4
        and 4 * residues == 3 * LANES * cols
        and width == 8 * rows * cols
    )


def whole_spec(array):
    return pl.BlockSpec(array.shape, lambda i: (0,) * array.ndim)


def triangle_call(received, made, blocks, side, own, incoming):
    pair = 2 * own
    pixels = side * side
    padded = blocks * LANES
    strip = side // 2
    left_rows = blocks * side
    right_rows = left_rows if incoming else padded
    return pl.pallas_call(
        functools.partial(triangle_kernel, blocks, side, own, incoming, made),
        grid=(2 * blocks // FOLD,),
        in_specs=[
            pl.BlockSpec(
                (FOLD * blocks * pair, pixels), lambda i: (jnp.minimum(i, blocks // FOLD - 1), 0)
            )
        ],
        out_specs=pl.BlockSpec(
            (2 * FOLD * pair, pixels // 2 * len(made)),
            lambda i: (jnp.maximum(i - blocks // FOLD, 0), 0),
        ),
        out_shape=pltpu.HBM((blocks * blocks * own, pixels // 2 * len(made)), jnp.bfloat16),
        scratch_shapes=[
            pltpu.VMEM((own, left_rows, padded), jnp.bfloat16),
            pltpu.VMEM((own, right_rows, padded), jnp.bfloat16),
            pltpu.VMEM((strip * (pair + 1), LANES), jnp.float32),
            pltpu.VMEM((len(made), 2 * blocks, strip * (pair + 1), LANES), jnp.float32),
        ],
        compiler_params=pltpu.CompilerParams(vmem_limit_bytes=48 * 1024 * 1024),
        cost_estimate=pl.CostEstimate(
            flops=own * (blocks * side) ** 3 * len(made),
            bytes_accessed=12 * blocks * blocks * pair * pixels // 2,
            transcendentals=0,
        ),
    )(received)


def pixel_call(body, tiled, fixed, outs, steps, tile, flops, start=0, pixels=None, kept=(), scratch=(), row_major_out=False):
    pixels = pixels or steps * tile

    def spec(channels, first, count, row_major):
        if row_major:
            return pl.BlockSpec(
                (tile, channels), lambda i: (jnp.clip(i + first, 0, count - 1), 0)
            )
        return pl.BlockSpec((channels, tile), lambda i: (0, jnp.clip(i + first, 0, count - 1)))

    def packed(a, first, count):
        return pl.BlockSpec(
            (1, *a.shape[1:]), lambda i: (jnp.clip(i + first, 0, count - 1), 0, 0)
        )

    in_specs = [
        packed(a, first, count) if a.ndim == 3 else spec(a.shape[0], first, count, False)
        for a, first, count in tiled
    ]
    in_specs += [whole_spec(a) for a in fixed]
    in_specs += [pl.BlockSpec(memory_space=pl.ANY)] * len(kept)
    n_in, n_kept = len(in_specs), len(kept)

    def kernel(*refs):
        body(*refs[: n_in - n_kept], *refs[n_in:])

    return pl.pallas_call(
        kernel,
        grid=(steps,),
        in_specs=in_specs,
        out_specs=[spec(ch, start, pixels // tile, row_major_out) for ch in outs],
        out_shape=[
            pltpu.HBM((pixels, ch) if row_major_out else (ch, pixels), jnp.bfloat16)
            for ch in outs
        ],
        input_output_aliases={n_in - n_kept + k: k for k in range(n_kept)},
        scratch_shapes=list(scratch),
        compiler_params=pltpu.CompilerParams(vmem_limit_bytes=48 * 1024 * 1024),
        cost_estimate=pl.CostEstimate(
            flops=flops, bytes_accessed=2 * steps * tile * (sum(outs) + 256), transcendentals=0
        ),
    )(*(a for a, *_ in tiled), *fixed, *kept)


LINE = ("groups", "zh")
CUBE = ("groups", "row", "zl")


def pack(pair_act, mask, cuts, tile):
    per_strip = cuts[-1]
    shape = (tile + mask.shape[1], pair_act.shape[1])
    outs = [end - begin for begin, end in zip((0, *cuts), cuts)] + [per_strip, per_strip]
    anywhere = pl.BlockSpec(memory_space=pltpu.HBM)
    return pl.pallas_call(
        functools.partial(pack_kernel, cuts, tile),
        in_specs=[anywhere] * 2,
        out_specs=[anywhere] * len(outs),
        out_shape=[pltpu.HBM((n, *shape), jnp.bfloat16) for n in outs],
        scratch_shapes=[
            pltpu.VMEM((2, per_strip, *shape), jnp.bfloat16),
            pltpu.SemaphoreType.DMA((2, per_strip)),
            pltpu.SemaphoreType.DMA((2, per_strip)),
            pltpu.SemaphoreType.DMA((len(outs),)),
        ],
        compiler_params=pltpu.CompilerParams(vmem_limit_bytes=48 * 1024 * 1024),
    )(pair_act, mask)


def by_kernels(
    pair_act,
    pair_mask,
    input_gain,
    input_bias,
    project_weight,
    gate_weight,
    output_gain,
    output_bias,
    output_weight,
):
    blocks = lax.axis_size("row")
    peers = blocks * blocks
    side, _, channels = pair_act.shape
    width = output_weight.shape[1]
    own = width // peers
    pixels = side * side
    strip = side // 2
    mult = 2 * channels

    tile = 9 * LANES
    per_piece = pixels // 2 // tile
    cuts = (1, per_piece - 1, per_piece)
    marks = pair_mask.astype(jnp.bfloat16).reshape(2 * per_piece, tile // LANES, LANES)
    marks = jnp.pad(marks, ((0, 0), (0, 16 - tile // LANES), (0, 0)))
    *z_parts, z_own, z_next = pack(pair_act.reshape(pixels, channels), marks, cuts, tile)
    z_far = []
    for part in z_parts[:-1]:
        over = lax.ppermute(part, LINE, ((1, 3), (2, 0)))
        z_far.append(lax.ppermute(over, LINE, ((0, 1), (3, 2))))
    z_near = lax.ppermute(z_next, LINE, ((1, 0), (2, 3), (0, 2), (3, 1)))
    z_far.append(lax.ppermute(z_parts[-1], LINE, ((1, 2), (2, 1))))
    small = jnp.stack([input_gain, input_bias, output_gain, output_bias], axis=1)
    small = small.reshape(-1, channels).T
    weights = jnp.concatenate(
        [project_weight * 0.5, gate_weight * 0.5, output_weight], axis=2
    ).transpose(0, 2, 1)
    fixed = (small, weights)

    def first(piece, ours, far, parts, kept):
        tiled = [(ours, 0, per_piece)]
        tiled += [(part, -begin, end - begin) for part, (begin, end) in zip(far, parts)]
        return pixel_call(
            functools.partial(first_kernel, peers, parts),
            tiled, fixed, (2 * width, channels, 16), per_piece, tile, pixels // 2 * mult * 4 * width,
            start=piece * per_piece, pixels=pixels, kept=kept,
        )

    begun = first(0, z_own, [z_near], [(0, per_piece)], ())
    sent, zt, mask = first(1, z_near, z_far, list(zip((0, *cuts), cuts)), begun)
    wide = 2 * tile
    steps = pixels // wide

    def gate_of(zt, u):
        return pixel_call(
            functools.partial(gate_kernel, u), [(zt, 0, steps)], fixed, (channels,),
            steps, wide, pixels * mult * channels,
        )[0]

    def exchange(array):
        there = lax.all_to_all(array.reshape(peers, -1, array.shape[1]), CUBE, 0, 0)
        return there.reshape(array.shape)

    gate = gate_of(zt, 0)
    triangle = exchange(triangle_call(exchange(sent), (0, 1), blocks, side, own, False))
    sent, zt = pixel_call(
        functools.partial(middle_kernel, peers),
        [(a, 0, steps) for a in (triangle, zt, gate, mask)], fixed, (2 * width, channels),
        steps, wide, pixels * mult * 5 * width,
    )
    gate = gate_of(zt, 1)
    received = exchange(sent)
    product = lambda piece: triangle_call(received, (piece,), blocks, side, own, True)

    def finish(piece, triangle):
        at = piece * steps // 2
        return pixel_call(
            last_kernel,
            [(triangle, 0, steps // 2), (zt, at, steps), (gate, at, steps)],
            fixed, (channels,), steps // 2, wide, pixels // 2 * mult * channels, row_major_out=True,
        )[0]

    there = finish(1, exchange(product(1)))
    beside, across = (
        lax.ppermute(there, LINE, pairs) for pairs in (((0, 1), (3, 2)), ((1, 2), (2, 1)))
    )
    there, waiting = lax.optimization_barrier((there, product(0)))
    here = finish(0, exchange(waiting))
    back = lax.ppermute(here, LINE, ((1, 3), (2, 0)))
    return pl.pallas_call(
        assemble_kernel,
        in_specs=[pl.BlockSpec(memory_space=pl.ANY)] * 4,
        out_specs=pl.BlockSpec(memory_space=pl.ANY),
        out_shape=pltpu.HBM((2, *here.shape), here.dtype),
        scratch_shapes=[
            pltpu.VMEM((2, *here.shape), here.dtype),
            pltpu.SemaphoreType.DMA((2, 2)),
            pltpu.SemaphoreType.DMA((2, 2)),
        ],
        compiler_params=pltpu.CompilerParams(vmem_limit_bytes=48 * 1024 * 1024),
    )(here, beside, back, across).reshape(side, side, channels)


def layer_norm(values, gain, bias, axis):
    average = jnp.mean(values, axis=axis, keepdims=True)
    centred = values - average
    spread_sq = jnp.mean(centred * centred, axis=axis, keepdims=True)
    return centred * lax.rsqrt(spread_sq + 1e-05) * gain + bias


def triangle_update(
    pair_act,
    mask_float,
    layer_index,
    input_gain,
    input_bias,
    project_weight,
    gate_weight,
    output_gain,
    output_bias,
    output_weight,
    incoming,
):
    rows, cols = lax.axis_size("row"), lax.axis_size("col")
    peers = rows * cols
    rows_here, cols_here, channels_here = pair_act.shape
    width = output_weight.shape[1]
    own = width // peers
    pixels = rows_here * cols_here
    pair_float = pair_act.astype(jnp.float32).reshape(pixels, channels_here)
    normed = layer_norm(
        pair_float, input_gain[layer_index], input_bias[layer_index], -1
    ).astype(jnp.bfloat16)
    projected = lax.dot_general(
        project_weight[layer_index],
        normed,
        (((0,), (1,)), ((), ())),
        preferred_element_type=jnp.float32,
    ).reshape(4, peers, own, pixels)
    mask_row = mask_float.reshape(1, 1, pixels)
    left_proj = (jax.nn.sigmoid(projected[0]) * projected[1] * mask_row).astype(jnp.bfloat16)
    right_proj = (jax.nn.sigmoid(projected[2]) * projected[3] * mask_row).astype(jnp.bfloat16)
    both = jnp.concatenate([left_proj, right_proj], axis=1)
    both = lax.all_to_all(both, GRID, 0, 0)
    both = both.reshape(rows, cols, 2, own, rows_here, cols_here)
    both = both.transpose(2, 3, 0, 4, 1, 5).reshape(2, own, rows * rows_here, cols * cols_here)
    spec = "cki,ckj->cij" if incoming else "cik,cjk->cij"
    triangle = jnp.einsum(spec, both[0], both[1], preferred_element_type=jnp.float32)
    triangle = triangle.astype(jnp.bfloat16).reshape(own, rows, rows_here, cols, cols_here)
    triangle = triangle.transpose(1, 3, 0, 2, 4).reshape(peers, own, pixels)
    triangle = lax.all_to_all(triangle, GRID, 0, 0).reshape(width, pixels)
    normed_sum = layer_norm(
        triangle.astype(jnp.float32),
        output_gain[layer_index][:, None],
        output_bias[layer_index][:, None],
        0,
    ).astype(jnp.bfloat16)
    gate_value = jax.nn.sigmoid(
        jnp.dot(normed, gate_weight[layer_index], preferred_element_type=jnp.float32)
    )
    mapped = lax.dot_general(
        normed_sum,
        output_weight[layer_index],
        (((0,), (0,)), ((), ())),
        preferred_element_type=jnp.float32,
    )
    return (
        (pair_float + gate_value * mapped)
        .astype(jnp.bfloat16)
        .reshape(rows_here, cols_here, channels_here)
    )


def shards(pair_act, pair_mask, *params):
    mask_float = pair_mask.astype(jnp.float32)
    for index in range(2):
        pair_act = triangle_update(pair_act, mask_float, index, *params, index == 1)
    return pair_act


def solution(mesh):
    def updates(pair_act, pair_mask, *params):
        body, grid, cols = shards, mesh, "col"
        if fits(mesh, pair_act.shape[1], params[-1].shape[1]):
            sizes = mesh.devices.shape
            grid = jax.sharding.Mesh(
                mesh.devices.reshape(*sizes[:2], 2, sizes[2] // 2), ("groups", "row", "zh", "zl")
            )
            body, cols = by_kernels, ("zh", "zl")
        pixels = (("groups", "row"), cols)
        return jax.shard_map(
            body,
            mesh=grid,
            in_specs=(P(*pixels, None), P(*pixels)) + (P(),) * 7,
            out_specs=P(*pixels, None),
            check_vma=False,
        )(pair_act, pair_mask, *params)

    return updates
```

```python
import functools
import itertools

import jax
import jax.numpy as jnp
from jax import lax
from jax.experimental import pallas as pl
from jax.experimental.pallas import tpu as pltpu
from jax.sharding import PartitionSpec as P

GRID = ("row", "col")
LANES = 128


IN_GAIN, IN_BIAS, OUT_GAIN, OUT_BIAS = range(4)


def channel_norm(values, gain, bias):
    average = jnp.mean(values, axis=0, keepdims=True)
    centred = values - average
    spread_sq = jnp.mean(centred * centred, axis=0, keepdims=True)
    return centred * lax.rsqrt(spread_sq + 1e-05) * gain + bias


def dot(left, right):
    return jnp.dot(left, right, preferred_element_type=jnp.float32)


def norm_of(values, small_ref, update, which):
    at = 4 * update + which
    return channel_norm(values, small_ref[:, at : at + 1], small_ref[:, at + 1 : at + 2])


def emit_projections(peers, update, zt, mask, small_ref, weight_ref, lr_ref):
    width = lr_ref.shape[0] // 2
    own = width // peers
    tile = zt.shape[1]
    normed = norm_of(zt, small_ref, update, IN_GAIN) * mask
    projected = dot(weight_ref[update, : 4 * width], normed.astype(jnp.bfloat16))
    left = (jnp.tanh(projected[:width]) + 1.0) * projected[width : 2 * width]
    right = (jnp.tanh(projected[2 * width : 3 * width]) + 1.0) * projected[3 * width :]
    both = jnp.concatenate(
        [left.reshape(peers, own, tile), right.reshape(peers, own, tile)], axis=1
    )
    lr_ref[...] = both.reshape(2 * width, tile).astype(jnp.bfloat16)


def pack_kernel(cuts, tile, z_ref, mask_ref, *refs):
    out_refs, (held_ref, z_sems, mask_sems, out_sems) = refs[:-4], refs[-4:]
    part_refs, (own_ref, next_ref) = out_refs[:-2], out_refs[-2:]
    upper = lax.axis_index("groups")
    home = upper == lax.axis_index("zh")
    per_strip = cuts[-1]
    rows = held_ref.shape[2]
    fetches = []
    for which in range(2):
        strip = lax.rem(upper + 1 - which, 2)
        for t in range(per_strip):
            at = pl.multiple_of((strip * per_strip + t) * tile, tile)
            fetches.append(
                pltpu.make_async_copy(
                    z_ref.at[pl.ds(at, tile)], held_ref.at[which, t, 0:tile], z_sems.at[which, t]
                )
            )
            fetches.append(
                pltpu.make_async_copy(
                    mask_ref.at[strip * per_strip + t], held_ref.at[which, t, tile:rows],
                    mask_sems.at[which, t],
                )
            )
    stores = [
        pltpu.make_async_copy(held_ref.at[0, begin:end], part_ref, out_sems.at[k])
        for k, (begin, end, part_ref) in enumerate(zip((0, *cuts), cuts, part_refs))
    ]
    stores += [
        pltpu.make_async_copy(held_ref.at[1], own_ref, out_sems.at[len(cuts)]),
        pltpu.make_async_copy(
            held_ref.at[1 - home.astype(jnp.int32)], next_ref, out_sems.at[len(cuts) + 1]
        ),
    ]
    for fetch in fetches:
        fetch.start()
    for fetch in fetches[: 2 * per_strip]:
        fetch.wait()
    for store in stores[: len(cuts)]:
        store.start()
    for fetch in fetches[2 * per_strip :]:
        fetch.wait()
    for store in stores[len(cuts) :]:
        store.start()
    for store in stores:
        store.wait()


def first_kernel(peers, parts, own_ref, *refs):
    far_refs, (small_ref, weight_ref), (lr_ref, zt_ref, mask_ref) = (
        refs[: len(parts)], refs[len(parts) : -3], refs[-3:],
    )
    home = lax.axis_index("groups") == lax.axis_index("zh")
    step = pl.program_id(0)
    tile = zt_ref.shape[1]

    def put(z_ref):
        zt_ref[...] = z_ref[0, :tile].astype(jnp.float32).T.astype(jnp.bfloat16)
        marks = z_ref[0, tile:].astype(jnp.float32)
        flat = jnp.concatenate([marks[k : k + 1] for k in range(tile // LANES)], axis=1)
        mask_ref[...] = jnp.broadcast_to(flat, mask_ref.shape).astype(jnp.bfloat16)

    pl.when(home)(lambda: put(own_ref))
    for (begin, end), far_ref in zip(parts, far_refs):
        here = jnp.logical_and(step >= begin, step < end)
        pl.when(jnp.logical_and(jnp.logical_not(home), here))(functools.partial(put, far_ref))
    zt = zt_ref[...].astype(jnp.float32)
    mask = mask_ref[...].astype(jnp.float32)[:1]
    emit_projections(peers, 0, zt, mask, small_ref, weight_ref, lr_ref)


def gate_kernel(update, zt_ref, small_ref, weight_ref, gate_ref):
    channels = gate_ref.shape[0]
    normed = norm_of(zt_ref[...].astype(jnp.float32), small_ref, update, IN_GAIN)
    at = weight_ref.shape[1] - 2 * channels
    gates = dot(weight_ref[update, at : at + channels], normed.astype(jnp.bfloat16))
    gate_ref[...] = (0.5 * jnp.tanh(gates) + 0.5).astype(jnp.bfloat16)


def updated(update, t_ref, zt_ref, gate_ref, small_ref, weight_ref):
    normed_sum = norm_of(t_ref[...].astype(jnp.float32), small_ref, update, OUT_GAIN)
    at = weight_ref.shape[1] - zt_ref.shape[0]
    mapped = dot(weight_ref[update, at:], normed_sum.astype(jnp.bfloat16))
    return zt_ref[...].astype(jnp.float32) + gate_ref[...].astype(jnp.float32) * mapped


def middle_kernel(
    peers, t_ref, zt_ref, gate_ref, mask_ref, small_ref, weight_ref, lr_ref, out_ref
):
    fresh = updated(0, t_ref, zt_ref, gate_ref, small_ref, weight_ref).astype(jnp.bfloat16)
    out_ref[...] = fresh
    mask = mask_ref[...].astype(jnp.float32)[:1]
    emit_projections(peers, 1, fresh.astype(jnp.float32), mask, small_ref, weight_ref, lr_ref)


def last_kernel(t_ref, zt_ref, gate_ref, small_ref, weight_ref, out_ref):
    fresh = updated(1, t_ref, zt_ref, gate_ref, small_ref, weight_ref)
    out_ref[...] = fresh.T.astype(jnp.bfloat16)


def assemble_kernel(here_ref, beside_ref, back_ref, across_ref, out_ref, held_ref, in_sems, out_sems):
    upper = lax.axis_index("groups")
    home = upper == lax.axis_index("zh")
    parts = in_sems.shape[1]
    size = here_ref.shape[0] // parts

    def move(*sources):
        pieces = [(which, k, slice(k * size, (k + 1) * size)) for k in range(parts) for which in range(2)]
        fetches = [
            pltpu.make_async_copy(
                sources[which].at[rows], held_ref.at[which, rows], in_sems.at[which, k]
            )
            for which, k, rows in pieces
        ]
        stores = [
            pltpu.make_async_copy(
                held_ref.at[which, rows], out_ref.at[lax.rem(upper + which, 2), rows],
                out_sems.at[which, k],
            )
            for which, k, rows in pieces
        ]
        for fetch in fetches:
            fetch.start()
        for fetch, store in zip(fetches, stores):
            fetch.wait()
            store.start()
        for store in stores:
            store.wait()

    pl.when(home)(lambda: move(here_ref, back_ref))
    pl.when(jnp.logical_not(home))(lambda: move(beside_ref, across_ref))


def triangle_kernel(blocks, side, own, incoming, made, folded, x_ref, y_ref, left_ref, right_ref, rows_ref, tiles_ref):
    step = pl.program_id(0)
    zh = lax.axis_index("zh")
    pair = 2 * own
    span = 4 * side
    strip = side // 2
    half = blocks // 2
    pitch_rows = pair + 1
    lane = lax.broadcasted_iota(jnp.int32, (pair, LANES), 1)
    inside = lane < side

    wanted = range(blocks) if len(made) == 2 else range(made[0] * half, (made[0] + 1) * half)

    @pl.when(step < blocks // folded)
    def _unpack():
        for fold, r in itertools.product(range(folded), range(2)):
            upper, row_pair = (step * folded + fold) // half, lax.rem(step * folded + fold, half)
            mirror = lax.rem(row_pair + zh, 2)
            source = (fold * 2 + r) * half
            at = pl.multiple_of((row_pair * 2 + r) * side + upper * strip, 16)
            if incoming:
                at_right = at
            else:
                at_right = pl.multiple_of((mirror * 2 + r) * LANES + upper * strip, 16)
            for zl in range(half):
                for piece in range(2):
                    first = piece * strip * side
                    for group in range(strip // 4):
                        x = x_ref[
                            (source + zl) * pair : (source + zl + 1) * pair,
                            first + group * span : first + (group + 1) * span,
                        ].astype(jnp.float32)
                        a, b, c = x[:, :LANES], x[:, LANES : 2 * LANES], x[:, 2 * LANES :]
                        picked = (
                            a,
                            pltpu.roll(jnp.where(lane >= 96, a, b), 32, 1),
                            pltpu.roll(jnp.where(lane >= 64, b, c), 64, 1),
                            pltpu.roll(c, 96, 1),
                        )
                        for k, row in enumerate(picked):
                            rows_ref[pl.ds((group * 4 + k) * pitch_rows, pair), :] = jnp.where(
                                inside, row, 0.0
                            )
                    lanes = slice((piece * half + zl) * LANES, (piece * half + zl + 1) * LANES)
                    for ch in range(own):
                        left_ref[ch, pl.ds(at, strip), lanes] = rows_ref[
                            pl.ds(ch, strip, stride=pitch_rows), :
                        ].astype(jnp.bfloat16)
                        if incoming and piece not in made:
                            continue
                        right_ref[ch, pl.ds(at_right, strip), lanes] = rows_ref[
                            pl.ds(own + ch, strip, stride=pitch_rows), :
                        ].astype(jnp.bfloat16)

    @pl.when(step == blocks // folded - 1)
    def _multiply():
        contract = ((0,), (0,)) if incoming else ((1,), (1,))
        for ch in range(own):
            right = right_ref[ch]
            if incoming:
                right = right[:, wanted[0] * LANES : (wanted[-1] + 1) * LANES]
            product = lax.dot_general(
                left_ref[ch], right, (contract, ((), ())), preferred_element_type=jnp.float32
            )
            for place in range(blocks):
                if incoming:
                    row, pitch = lax.rem(place // 2 + zh, 2) * 2 + place % 2, LANES
                else:
                    row, pitch = place, side
                for upper in range(2):
                    for col in range(len(wanted)):
                        tiles_ref[
                            col // half,
                            upper * blocks + row,
                            pl.ds((col % half) * own + ch, strip, stride=pitch_rows),
                            :,
                        ] = product[
                            place * pitch + upper * strip : place * pitch + (upper + 1) * strip,
                            col * LANES : (col + 1) * LANES,
                        ]

    @pl.when(step >= blocks // folded)
    def _repack():
        for r in range(2 * folded):
            place = (step - blocks // folded) * 2 * folded + r
            for piece in range(len(made)):
                first = piece * strip * side
                for group in range(strip // 4):
                    p, q, t, s = (
                        tiles_ref[piece, place, pl.ds((group * 4 + k) * pitch_rows, pair), :]
                        for k in range(4)
                    )
                    q, t, s = pltpu.roll(q, 96, 1), pltpu.roll(t, 64, 1), pltpu.roll(s, 32, 1)
                    flat = jnp.concatenate(
                        [
                            jnp.where(inside, p, q),
                            jnp.where(lane < 64, q, t),
                            jnp.where(lane < 32, t, s),
                        ],
                        axis=1,
                    )
                    y_ref[
                        r * pair : (r + 1) * pair, first + group * span : first + (group + 1) * span
                    ] = flat.astype(jnp.bfloat16)


def fits(mesh, residues, width):
    rows, cols = mesh.shape["row"], mesh.shape["col"]
    return (
        mesh.shape["groups"] == 2
        and rows == 4
        and cols == 4
        and 4 * residues == 3 * LANES * cols
        and width == 8 * rows * cols
    )


def whole_spec(array):
    return pl.BlockSpec(array.shape, lambda i: (0,) * array.ndim)


def triangle_call(received, made, blocks, side, own, incoming):
    folded = 1 if incoming else 2
    pair = 2 * own
    pixels = side * side
    padded = blocks * LANES
    strip = side // 2
    left_rows = blocks * side
    right_rows = left_rows if incoming else padded
    return pl.pallas_call(
        functools.partial(triangle_kernel, blocks, side, own, incoming, made, folded),
        grid=(2 * blocks // folded,),
        in_specs=[
            pl.BlockSpec(
                (folded * blocks * pair, pixels), lambda i: (jnp.minimum(i, blocks // folded - 1), 0)
            )
        ],
        out_specs=pl.BlockSpec(
            (2 * folded * pair, pixels // 2 * len(made)),
            lambda i: (jnp.maximum(i - blocks // folded, 0), 0),
        ),
        out_shape=pltpu.HBM((blocks * blocks * own, pixels // 2 * len(made)), jnp.bfloat16),
        scratch_shapes=[
            pltpu.VMEM((own, left_rows, padded), jnp.bfloat16),
            pltpu.VMEM((own, right_rows, padded), jnp.bfloat16),
            pltpu.VMEM((strip * (pair + 1), LANES), jnp.float32),
            pltpu.VMEM((len(made), 2 * blocks, strip * (pair + 1), LANES), jnp.float32),
        ],
        compiler_params=pltpu.CompilerParams(vmem_limit_bytes=48 * 1024 * 1024),
        cost_estimate=pl.CostEstimate(
            flops=own * (blocks * side) ** 3 * len(made),
            bytes_accessed=12 * blocks * blocks * pair * pixels // 2,
            transcendentals=0,
        ),
    )(received)


def pixel_call(body, tiled, fixed, outs, steps, tile, flops, start=0, pixels=None, kept=(), scratch=(), row_major_out=False):
    pixels = pixels or steps * tile

    def spec(channels, first, count, row_major):
        if row_major:
            return pl.BlockSpec(
                (tile, channels), lambda i: (jnp.clip(i + first, 0, count - 1), 0)
            )
        return pl.BlockSpec((channels, tile), lambda i: (0, jnp.clip(i + first, 0, count - 1)))

    def packed(a, first, count):
        return pl.BlockSpec(
            (1, *a.shape[1:]), lambda i: (jnp.clip(i + first, 0, count - 1), 0, 0)
        )

    in_specs = [
        packed(a, first, count) if a.ndim == 3 else spec(a.shape[0], first, count, False)
        for a, first, count in tiled
    ]
    in_specs += [whole_spec(a) for a in fixed]
    in_specs += [pl.BlockSpec(memory_space=pl.ANY)] * len(kept)
    n_in, n_kept = len(in_specs), len(kept)

    def kernel(*refs):
        body(*refs[: n_in - n_kept], *refs[n_in:])

    return pl.pallas_call(
        kernel,
        grid=(steps,),
        in_specs=in_specs,
        out_specs=[spec(ch, start, pixels // tile, row_major_out) for ch in outs],
        out_shape=[
            pltpu.HBM((pixels, ch) if row_major_out else (ch, pixels), jnp.bfloat16)
            for ch in outs
        ],
        input_output_aliases={n_in - n_kept + k: k for k in range(n_kept)},
        scratch_shapes=list(scratch),
        compiler_params=pltpu.CompilerParams(vmem_limit_bytes=48 * 1024 * 1024),
        cost_estimate=pl.CostEstimate(
            flops=flops, bytes_accessed=2 * steps * tile * (sum(outs) + 256), transcendentals=0
        ),
    )(*(a for a, *_ in tiled), *fixed, *kept)


LINE = ("groups", "zh")
CUBE = ("groups", "row", "zl")


def pack(pair_act, mask, cuts, tile):
    per_strip = cuts[-1]
    shape = (tile + mask.shape[1], pair_act.shape[1])
    outs = [end - begin for begin, end in zip((0, *cuts), cuts)] + [per_strip, per_strip]
    anywhere = pl.BlockSpec(memory_space=pltpu.HBM)
    return pl.pallas_call(
        functools.partial(pack_kernel, cuts, tile),
        in_specs=[anywhere] * 2,
        out_specs=[anywhere] * len(outs),
        out_shape=[pltpu.HBM((n, *shape), jnp.bfloat16) for n in outs],
        scratch_shapes=[
            pltpu.VMEM((2, per_strip, *shape), jnp.bfloat16),
            pltpu.SemaphoreType.DMA((2, per_strip)),
            pltpu.SemaphoreType.DMA((2, per_strip)),
            pltpu.SemaphoreType.DMA((len(outs),)),
        ],
        compiler_params=pltpu.CompilerParams(vmem_limit_bytes=48 * 1024 * 1024),
    )(pair_act, mask)


def by_kernels(
    pair_act,
    pair_mask,
    input_gain,
    input_bias,
    project_weight,
    gate_weight,
    output_gain,
    output_bias,
    output_weight,
):
    blocks = lax.axis_size("row")
    peers = blocks * blocks
    side, _, channels = pair_act.shape
    width = output_weight.shape[1]
    own = width // peers
    pixels = side * side
    strip = side // 2
    mult = 2 * channels

    tile = 9 * LANES
    per_piece = pixels // 2 // tile
    cuts = (1, per_piece - 1, per_piece)
    marks = pair_mask.astype(jnp.bfloat16).reshape(2 * per_piece, tile // LANES, LANES)
    marks = jnp.pad(marks, ((0, 0), (0, 16 - tile // LANES), (0, 0)))
    *z_parts, z_own, z_next = pack(pair_act.reshape(pixels, channels), marks, cuts, tile)
    z_far = []
    for part in z_parts[:-1]:
        over = lax.ppermute(part, LINE, ((1, 3), (2, 0)))
        z_far.append(lax.ppermute(over, LINE, ((0, 1), (3, 2))))
    z_near = lax.ppermute(z_next, LINE, ((1, 0), (2, 3), (0, 2), (3, 1)))
    z_far.append(lax.ppermute(z_parts[-1], LINE, ((1, 2), (2, 1))))
    small = jnp.stack([input_gain, input_bias, output_gain, output_bias], axis=1)
    small = small.reshape(-1, channels).T
    weights = jnp.concatenate(
        [project_weight * 0.5, gate_weight * 0.5, output_weight], axis=2
    ).transpose(0, 2, 1)
    fixed = (small, weights)

    def first(piece, ours, far, parts, kept):
        tiled = [(ours, 0, per_piece)]
        tiled += [(part, -begin, end - begin) for part, (begin, end) in zip(far, parts)]
        return pixel_call(
            functools.partial(first_kernel, peers, parts),
            tiled, fixed, (2 * width, channels, 16), per_piece, tile, pixels // 2 * mult * 4 * width,
            start=piece * per_piece, pixels=pixels, kept=kept,
        )

    begun = first(0, z_own, [z_near], [(0, per_piece)], ())
    sent, zt, mask = first(1, z_near, z_far, list(zip((0, *cuts), cuts)), begun)
    wide = 2 * tile
    steps = pixels // wide

    def gate_of(zt, u):
        return pixel_call(
            functools.partial(gate_kernel, u), [(zt, 0, steps)], fixed, (channels,),
            steps, wide, pixels * mult * channels,
        )[0]

    def exchange(array):
        there = lax.all_to_all(array.reshape(peers, -1, array.shape[1]), CUBE, 0, 0)
        return there.reshape(array.shape)

    gate = gate_of(zt, 0)
    triangle = exchange(triangle_call(exchange(sent), (0, 1), blocks, side, own, False))
    sent, zt = pixel_call(
        functools.partial(middle_kernel, peers),
        [(a, 0, steps) for a in (triangle, zt, gate, mask)], fixed, (2 * width, channels),
        steps, wide, pixels * mult * 5 * width,
    )
    gate = gate_of(zt, 1)
    received = exchange(sent)
    product = lambda piece: triangle_call(received, (piece,), blocks, side, own, True)

    def finish(piece, triangle):
        at = piece * steps // 2
        return pixel_call(
            last_kernel,
            [(triangle, 0, steps // 2), (zt, at, steps), (gate, at, steps)],
            fixed, (channels,), steps // 2, wide, pixels // 2 * mult * channels, row_major_out=True,
        )[0]

    there = finish(1, exchange(product(1)))
    beside, across = (
        lax.ppermute(there, LINE, pairs) for pairs in (((0, 1), (3, 2)), ((1, 2), (2, 1)))
    )
    there, waiting = lax.optimization_barrier((there, product(0)))
    here = finish(0, exchange(waiting))
    back = lax.ppermute(here, LINE, ((1, 3), (2, 0)))
    return pl.pallas_call(
        assemble_kernel,
        in_specs=[pl.BlockSpec(memory_space=pl.ANY)] * 4,
        out_specs=pl.BlockSpec(memory_space=pl.ANY),
        out_shape=pltpu.HBM((2, *here.shape), here.dtype),
        scratch_shapes=[
            pltpu.VMEM((2, *here.shape), here.dtype),
            pltpu.SemaphoreType.DMA((2, 2)),
            pltpu.SemaphoreType.DMA((2, 2)),
        ],
        compiler_params=pltpu.CompilerParams(vmem_limit_bytes=48 * 1024 * 1024),
    )(here, beside, back, across).reshape(side, side, channels)


def layer_norm(values, gain, bias, axis):
    average = jnp.mean(values, axis=axis, keepdims=True)
    centred = values - average
    spread_sq = jnp.mean(centred * centred, axis=axis, keepdims=True)
    return centred * lax.rsqrt(spread_sq + 1e-05) * gain + bias


def triangle_update(
    pair_act,
    mask_float,
    layer_index,
    input_gain,
    input_bias,
    project_weight,
    gate_weight,
    output_gain,
    output_bias,
    output_weight,
    incoming,
):
    rows, cols = lax.axis_size("row"), lax.axis_size("col")
    peers = rows * cols
    rows_here, cols_here, channels_here = pair_act.shape
    width = output_weight.shape[1]
    own = width // peers
    pixels = rows_here * cols_here
    pair_float = pair_act.astype(jnp.float32).reshape(pixels, channels_here)
    normed = layer_norm(
        pair_float, input_gain[layer_index], input_bias[layer_index], -1
    ).astype(jnp.bfloat16)
    projected = lax.dot_general(
        project_weight[layer_index],
        normed,
        (((0,), (1,)), ((), ())),
        preferred_element_type=jnp.float32,
    ).reshape(4, peers, own, pixels)
    mask_row = mask_float.reshape(1, 1, pixels)
    left_proj = (jax.nn.sigmoid(projected[0]) * projected[1] * mask_row).astype(jnp.bfloat16)
    right_proj = (jax.nn.sigmoid(projected[2]) * projected[3] * mask_row).astype(jnp.bfloat16)
    both = jnp.concatenate([left_proj, right_proj], axis=1)
    both = lax.all_to_all(both, GRID, 0, 0)
    both = both.reshape(rows, cols, 2, own, rows_here, cols_here)
    both = both.transpose(2, 3, 0, 4, 1, 5).reshape(2, own, rows * rows_here, cols * cols_here)
    spec = "cki,ckj->cij" if incoming else "cik,cjk->cij"
    triangle = jnp.einsum(spec, both[0], both[1], preferred_element_type=jnp.float32)
    triangle = triangle.astype(jnp.bfloat16).reshape(own, rows, rows_here, cols, cols_here)
    triangle = triangle.transpose(1, 3, 0, 2, 4).reshape(peers, own, pixels)
    triangle = lax.all_to_all(triangle, GRID, 0, 0).reshape(width, pixels)
    normed_sum = layer_norm(
        triangle.astype(jnp.float32),
        output_gain[layer_index][:, None],
        output_bias[layer_index][:, None],
        0,
    ).astype(jnp.bfloat16)
    gate_value = jax.nn.sigmoid(
        jnp.dot(normed, gate_weight[layer_index], preferred_element_type=jnp.float32)
    )
    mapped = lax.dot_general(
        normed_sum,
        output_weight[layer_index],
        (((0,), (0,)), ((), ())),
        preferred_element_type=jnp.float32,
    )
    return (
        (pair_float + gate_value * mapped)
        .astype(jnp.bfloat16)
        .reshape(rows_here, cols_here, channels_here)
    )


def shards(pair_act, pair_mask, *params):
    mask_float = pair_mask.astype(jnp.float32)
    for index in range(2):
        pair_act = triangle_update(pair_act, mask_float, index, *params, index == 1)
    return pair_act


def solution(mesh):
    def updates(pair_act, pair_mask, *params):
        body, grid, cols = shards, mesh, "col"
        if fits(mesh, pair_act.shape[1], params[-1].shape[1]):
            sizes = mesh.devices.shape
            grid = jax.sharding.Mesh(
                mesh.devices.reshape(*sizes[:2], 2, sizes[2] // 2), ("groups", "row", "zh", "zl")
            )
            body, cols = by_kernels, ("zh", "zl")
        pixels = (("groups", "row"), cols)
        return jax.shard_map(
            body,
            mesh=grid,
            in_specs=(P(*pixels, None), P(*pixels)) + (P(),) * 7,
            out_specs=P(*pixels, None),
            check_vma=False,
        )(pair_act, pair_mask, *params)

    return updates
```

```python
import functools

import jax
import jax.numpy as jnp
from jax import lax
from jax.experimental import pallas as pl
from jax.experimental.pallas import tpu as pltpu
from jax.sharding import PartitionSpec as P

GRID = ("row", "col")
LANES = 128


IN_GAIN, IN_BIAS, OUT_GAIN, OUT_BIAS = range(4)


def channel_norm(values, gain, bias):
    average = jnp.mean(values, axis=0, keepdims=True)
    centred = values - average
    spread_sq = jnp.mean(centred * centred, axis=0, keepdims=True)
    return centred * lax.rsqrt(spread_sq + 1e-05) * gain + bias


def dot(left, right):
    return jnp.dot(left, right, preferred_element_type=jnp.float32)


def norm_of(values, small_ref, update, which):
    at = 4 * update + which
    return channel_norm(values, small_ref[:, at : at + 1], small_ref[:, at + 1 : at + 2])


def emit_projections(peers, update, zt, mask, small_ref, weight_ref, lr_ref):
    width = lr_ref.shape[0] // 2
    own = width // peers
    tile = zt.shape[1]
    normed = norm_of(zt, small_ref, update, IN_GAIN) * mask
    projected = dot(weight_ref[update, : 4 * width], normed.astype(jnp.bfloat16))
    left = (jnp.tanh(projected[:width]) + 1.0) * projected[width : 2 * width]
    right = (jnp.tanh(projected[2 * width : 3 * width]) + 1.0) * projected[3 * width :]
    both = jnp.concatenate(
        [left.reshape(peers, own, tile), right.reshape(peers, own, tile)], axis=1
    )
    lr_ref[...] = both.reshape(2 * width, tile).astype(jnp.bfloat16)


def pack_kernel(cuts, tile, z_ref, mask_ref, *refs):
    out_refs, (held_ref, z_sems, mask_sems, out_sems) = refs[:-4], refs[-4:]
    part_refs, (own_ref, next_ref) = out_refs[:-2], out_refs[-2:]
    upper = lax.axis_index("groups")
    home = upper == lax.axis_index("zh")
    per_strip = cuts[-1]
    rows = held_ref.shape[2]
    fetches = []
    for which in range(2):
        strip = lax.rem(upper + 1 - which, 2)
        for t in range(per_strip):
            at = pl.multiple_of((strip * per_strip + t) * tile, tile)
            fetches.append(
                pltpu.make_async_copy(
                    z_ref.at[pl.ds(at, tile)], held_ref.at[which, t, 0:tile], z_sems.at[which, t]
                )
            )
            fetches.append(
                pltpu.make_async_copy(
                    mask_ref.at[strip * per_strip + t], held_ref.at[which, t, tile:rows],
                    mask_sems.at[which, t],
                )
            )
    stores = [
        pltpu.make_async_copy(held_ref.at[0, begin:end], part_ref, out_sems.at[k])
        for k, (begin, end, part_ref) in enumerate(zip((0, *cuts), cuts, part_refs))
    ]
    stores += [
        pltpu.make_async_copy(held_ref.at[1], own_ref, out_sems.at[len(cuts)]),
        pltpu.make_async_copy(
            held_ref.at[1 - home.astype(jnp.int32)], next_ref, out_sems.at[len(cuts) + 1]
        ),
    ]
    for fetch in fetches:
        fetch.start()
    for fetch in fetches[: 2 * per_strip]:
        fetch.wait()
    for store in stores[: len(cuts)]:
        store.start()
    for fetch in fetches[2 * per_strip :]:
        fetch.wait()
    for store in stores[len(cuts) :]:
        store.start()
    for store in stores:
        store.wait()


def first_kernel(peers, parts, own_ref, *refs):
    far_refs, (small_ref, weight_ref), (lr_ref, zt_ref, mask_ref) = (
        refs[: len(parts)], refs[len(parts) : -3], refs[-3:],
    )
    home = lax.axis_index("groups") == lax.axis_index("zh")
    step = pl.program_id(0)
    tile = zt_ref.shape[1]

    def put(z_ref):
        zt_ref[...] = z_ref[0, :tile].astype(jnp.float32).T.astype(jnp.bfloat16)
        marks = z_ref[0, tile:].astype(jnp.float32)
        flat = jnp.concatenate([marks[k : k + 1] for k in range(tile // LANES)], axis=1)
        mask_ref[...] = jnp.broadcast_to(flat, mask_ref.shape).astype(jnp.bfloat16)

    pl.when(home)(lambda: put(own_ref))
    for (begin, end), far_ref in zip(parts, far_refs):
        here = jnp.logical_and(step >= begin, step < end)
        pl.when(jnp.logical_and(jnp.logical_not(home), here))(functools.partial(put, far_ref))
    zt = zt_ref[...].astype(jnp.float32)
    mask = mask_ref[...].astype(jnp.float32)[:1]
    emit_projections(peers, 0, zt, mask, small_ref, weight_ref, lr_ref)


def gate_kernel(update, zt_ref, small_ref, weight_ref, gate_ref):
    channels = gate_ref.shape[0]
    normed = norm_of(zt_ref[...].astype(jnp.float32), small_ref, update, IN_GAIN)
    at = weight_ref.shape[1] - 2 * channels
    gates = dot(weight_ref[update, at : at + channels], normed.astype(jnp.bfloat16))
    gate_ref[...] = (0.5 * jnp.tanh(gates) + 0.5).astype(jnp.bfloat16)


def updated(update, t_ref, zt_ref, gate_ref, small_ref, weight_ref):
    normed_sum = norm_of(t_ref[...].astype(jnp.float32), small_ref, update, OUT_GAIN)
    at = weight_ref.shape[1] - zt_ref.shape[0]
    mapped = dot(weight_ref[update, at:], normed_sum.astype(jnp.bfloat16))
    return zt_ref[...].astype(jnp.float32) + gate_ref[...].astype(jnp.float32) * mapped


def middle_kernel(
    peers, t_ref, zt_ref, gate_ref, mask_ref, small_ref, weight_ref, lr_ref, out_ref
):
    fresh = updated(0, t_ref, zt_ref, gate_ref, small_ref, weight_ref).astype(jnp.bfloat16)
    out_ref[...] = fresh
    mask = mask_ref[...].astype(jnp.float32)[:1]
    emit_projections(peers, 1, fresh.astype(jnp.float32), mask, small_ref, weight_ref, lr_ref)


def last_kernel(t_ref, zt_ref, gate_ref, small_ref, weight_ref, out_ref):
    fresh = updated(1, t_ref, zt_ref, gate_ref, small_ref, weight_ref)
    out_ref[...] = fresh.T.astype(jnp.bfloat16)


def assemble_kernel(here_ref, beside_ref, back_ref, across_ref, out_ref, held_ref, in_sems, out_sems):
    upper = lax.axis_index("groups")
    home = upper == lax.axis_index("zh")
    parts = in_sems.shape[1]
    size = here_ref.shape[0] // parts

    def move(*sources):
        pieces = [(which, k, slice(k * size, (k + 1) * size)) for k in range(parts) for which in range(2)]
        fetches = [
            pltpu.make_async_copy(
                sources[which].at[rows], held_ref.at[which, rows], in_sems.at[which, k]
            )
            for which, k, rows in pieces
        ]
        stores = [
            pltpu.make_async_copy(
                held_ref.at[which, rows], out_ref.at[lax.rem(upper + which, 2), rows],
                out_sems.at[which, k],
            )
            for which, k, rows in pieces
        ]
        for fetch in fetches:
            fetch.start()
        for fetch, store in zip(fetches, stores):
            fetch.wait()
            store.start()
        for store in stores:
            store.wait()

    pl.when(home)(lambda: move(here_ref, back_ref))
    pl.when(jnp.logical_not(home))(lambda: move(beside_ref, across_ref))


def triangle_kernel(blocks, side, own, incoming, made, x_ref, y_ref, left_ref, right_ref, rows_ref, tiles_ref):
    step = pl.program_id(0)
    zh = lax.axis_index("zh")
    pair = 2 * own
    span = 4 * side
    strip = side // 2
    half = blocks // 2
    pitch_rows = pair + 1
    lane = lax.broadcasted_iota(jnp.int32, (pair, LANES), 1)
    inside = lane < side

    wanted = range(blocks) if len(made) == 2 else range(made[0] * half, (made[0] + 1) * half)

    @pl.when(step < blocks)
    def _unpack():
        upper, row_pair = step // half, lax.rem(step, half)
        mirror = lax.rem(row_pair + zh, 2)
        for r in range(2):
            at = pl.multiple_of((row_pair * 2 + r) * side + upper * strip, 16)
            if incoming:
                at_right = at
            else:
                at_right = pl.multiple_of((mirror * 2 + r) * LANES + upper * strip, 16)
            for zl in range(half):
                for piece in range(2):
                    first = piece * strip * side
                    for group in range(strip // 4):
                        x = x_ref[
                            (r * half + zl) * pair : (r * half + zl + 1) * pair,
                            first + group * span : first + (group + 1) * span,
                        ].astype(jnp.float32)
                        a, b, c = x[:, :LANES], x[:, LANES : 2 * LANES], x[:, 2 * LANES :]
                        picked = (
                            a,
                            pltpu.roll(jnp.where(lane >= 96, a, b), 32, 1),
                            pltpu.roll(jnp.where(lane >= 64, b, c), 64, 1),
                            pltpu.roll(c, 96, 1),
                        )
                        for k, row in enumerate(picked):
                            rows_ref[pl.ds((group * 4 + k) * pitch_rows, pair), :] = jnp.where(
                                inside, row, 0.0
                            )
                    lanes = slice((piece * half + zl) * LANES, (piece * half + zl + 1) * LANES)
                    for ch in range(own):
                        left_ref[ch, pl.ds(at, strip), lanes] = rows_ref[
                            pl.ds(ch, strip, stride=pitch_rows), :
                        ].astype(jnp.bfloat16)
                        if incoming and piece not in made:
                            continue
                        right_ref[ch, pl.ds(at_right, strip), lanes] = rows_ref[
                            pl.ds(own + ch, strip, stride=pitch_rows), :
                        ].astype(jnp.bfloat16)

    @pl.when(step == blocks - 1)
    def _multiply():
        contract = ((0,), (0,)) if incoming else ((1,), (1,))
        for ch in range(own):
            right = right_ref[ch]
            if incoming:
                right = right[:, wanted[0] * LANES : (wanted[-1] + 1) * LANES]
            product = lax.dot_general(
                left_ref[ch], right, (contract, ((), ())), preferred_element_type=jnp.float32
            )
            for place in range(blocks):
                if incoming:
                    row, pitch = lax.rem(place // 2 + zh, 2) * 2 + place % 2, LANES
                else:
                    row, pitch = place, side
                for upper in range(2):
                    for col in range(len(wanted)):
                        tiles_ref[
                            col // half,
                            upper * blocks + row,
                            pl.ds((col % half) * own + ch, strip, stride=pitch_rows),
                            :,
                        ] = product[
                            place * pitch + upper * strip : place * pitch + (upper + 1) * strip,
                            col * LANES : (col + 1) * LANES,
                        ]

    @pl.when(step >= blocks)
    def _repack():
        for r in range(2):
            place = (step - blocks) * 2 + r
            for piece in range(len(made)):
                first = piece * strip * side
                for group in range(strip // 4):
                    p, q, t, s = (
                        tiles_ref[piece, place, pl.ds((group * 4 + k) * pitch_rows, pair), :]
                        for k in range(4)
                    )
                    q, t, s = pltpu.roll(q, 96, 1), pltpu.roll(t, 64, 1), pltpu.roll(s, 32, 1)
                    flat = jnp.concatenate(
                        [
                            jnp.where(inside, p, q),
                            jnp.where(lane < 64, q, t),
                            jnp.where(lane < 32, t, s),
                        ],
                        axis=1,
                    )
                    y_ref[
                        r * pair : (r + 1) * pair, first + group * span : first + (group + 1) * span
                    ] = flat.astype(jnp.bfloat16)


def fits(mesh, residues, width):
    rows, cols = mesh.shape["row"], mesh.shape["col"]
    return (
        mesh.shape["groups"] == 2
        and rows == 4
        and cols == 4
        and 4 * residues == 3 * LANES * cols
        and width == 8 * rows * cols
    )


def whole_spec(array):
    return pl.BlockSpec(array.shape, lambda i: (0,) * array.ndim)


def triangle_call(received, made, blocks, side, own, incoming):
    pair = 2 * own
    pixels = side * side
    padded = blocks * LANES
    strip = side // 2
    left_rows = blocks * side
    right_rows = left_rows if incoming else padded
    return pl.pallas_call(
        functools.partial(triangle_kernel, blocks, side, own, incoming, made),
        grid=(2 * blocks,),
        in_specs=[
            pl.BlockSpec((blocks * pair, pixels), lambda i: (jnp.minimum(i, blocks - 1), 0))
        ],
        out_specs=pl.BlockSpec(
            (2 * pair, pixels // 2 * len(made)), lambda i: (jnp.maximum(i - blocks, 0), 0)
        ),
        out_shape=pltpu.HBM((blocks * blocks * own, pixels // 2 * len(made)), jnp.bfloat16),
        scratch_shapes=[
            pltpu.VMEM((own, left_rows, padded), jnp.bfloat16),
            pltpu.VMEM((own, right_rows, padded), jnp.bfloat16),
            pltpu.VMEM((strip * (pair + 1), LANES), jnp.float32),
            pltpu.VMEM((len(made), 2 * blocks, strip * (pair + 1), LANES), jnp.float32),
        ],
        compiler_params=pltpu.CompilerParams(vmem_limit_bytes=48 * 1024 * 1024),
        cost_estimate=pl.CostEstimate(
            flops=own * (blocks * side) ** 3 * len(made),
            bytes_accessed=12 * blocks * blocks * pair * pixels // 2,
            transcendentals=0,
        ),
    )(received)


def pixel_call(body, tiled, fixed, outs, steps, tile, flops, start=0, pixels=None, kept=(), scratch=(), row_major_out=False):
    pixels = pixels or steps * tile

    def spec(channels, first, count, row_major):
        if row_major:
            return pl.BlockSpec(
                (tile, channels), lambda i: (jnp.clip(i + first, 0, count - 1), 0)
            )
        return pl.BlockSpec((channels, tile), lambda i: (0, jnp.clip(i + first, 0, count - 1)))

    def packed(a, first, count):
        return pl.BlockSpec(
            (1, *a.shape[1:]), lambda i: (jnp.clip(i + first, 0, count - 1), 0, 0)
        )

    in_specs = [
        packed(a, first, count) if a.ndim == 3 else spec(a.shape[0], first, count, False)
        for a, first, count in tiled
    ]
    in_specs += [whole_spec(a) for a in fixed]
    in_specs += [pl.BlockSpec(memory_space=pl.ANY)] * len(kept)
    n_in, n_kept = len(in_specs), len(kept)

    def kernel(*refs):
        body(*refs[: n_in - n_kept], *refs[n_in:])

    return pl.pallas_call(
        kernel,
        grid=(steps,),
        in_specs=in_specs,
        out_specs=[spec(ch, start, pixels // tile, row_major_out) for ch in outs],
        out_shape=[
            pltpu.HBM((pixels, ch) if row_major_out else (ch, pixels), jnp.bfloat16)
            for ch in outs
        ],
        input_output_aliases={n_in - n_kept + k: k for k in range(n_kept)},
        scratch_shapes=list(scratch),
        compiler_params=pltpu.CompilerParams(vmem_limit_bytes=48 * 1024 * 1024),
        cost_estimate=pl.CostEstimate(
            flops=flops, bytes_accessed=2 * steps * tile * (sum(outs) + 256), transcendentals=0
        ),
    )(*(a for a, *_ in tiled), *fixed, *kept)


LINE = ("groups", "zh")
CUBE = ("groups", "row", "zl")


def pack(pair_act, mask, cuts, tile):
    per_strip = cuts[-1]
    shape = (tile + mask.shape[1], pair_act.shape[1])
    outs = [end - begin for begin, end in zip((0, *cuts), cuts)] + [per_strip, per_strip]
    anywhere = pl.BlockSpec(memory_space=pltpu.HBM)
    return pl.pallas_call(
        functools.partial(pack_kernel, cuts, tile),
        in_specs=[anywhere] * 2,
        out_specs=[anywhere] * len(outs),
        out_shape=[pltpu.HBM((n, *shape), jnp.bfloat16) for n in outs],
        scratch_shapes=[
            pltpu.VMEM((2, per_strip, *shape), jnp.bfloat16),
            pltpu.SemaphoreType.DMA((2, per_strip)),
            pltpu.SemaphoreType.DMA((2, per_strip)),
            pltpu.SemaphoreType.DMA((len(outs),)),
        ],
        compiler_params=pltpu.CompilerParams(vmem_limit_bytes=48 * 1024 * 1024),
    )(pair_act, mask)


def by_kernels(
    pair_act,
    pair_mask,
    input_gain,
    input_bias,
    project_weight,
    gate_weight,
    output_gain,
    output_bias,
    output_weight,
):
    blocks = lax.axis_size("row")
    peers = blocks * blocks
    side, _, channels = pair_act.shape
    width = output_weight.shape[1]
    own = width // peers
    pixels = side * side
    strip = side // 2
    mult = 2 * channels

    tile = 9 * LANES
    per_piece = pixels // 2 // tile
    cuts = (1, per_piece - 1, per_piece)
    marks = pair_mask.astype(jnp.bfloat16).reshape(2 * per_piece, tile // LANES, LANES)
    marks = jnp.pad(marks, ((0, 0), (0, 16 - tile // LANES), (0, 0)))
    *z_parts, z_own, z_next = pack(pair_act.reshape(pixels, channels), marks, cuts, tile)
    z_far = []
    for part in z_parts[:-1]:
        over = lax.ppermute(part, LINE, ((1, 3), (2, 0)))
        z_far.append(lax.ppermute(over, LINE, ((0, 1), (3, 2))))
    z_near = lax.ppermute(z_next, LINE, ((1, 0), (2, 3), (0, 2), (3, 1)))
    z_far.append(lax.ppermute(z_parts[-1], LINE, ((1, 2), (2, 1))))
    small = jnp.stack([input_gain, input_bias, output_gain, output_bias], axis=1)
    small = small.reshape(-1, channels).T
    weights = jnp.concatenate(
        [project_weight * 0.5, gate_weight * 0.5, output_weight], axis=2
    ).transpose(0, 2, 1)
    fixed = (small, weights)

    def first(piece, ours, far, parts, kept):
        tiled = [(ours, 0, per_piece)]
        tiled += [(part, -begin, end - begin) for part, (begin, end) in zip(far, parts)]
        return pixel_call(
            functools.partial(first_kernel, peers, parts),
            tiled, fixed, (2 * width, channels, 16), per_piece, tile, pixels // 2 * mult * 4 * width,
            start=piece * per_piece, pixels=pixels, kept=kept,
        )

    begun = first(0, z_own, [z_near], [(0, per_piece)], ())
    sent, zt, mask = first(1, z_near, z_far, list(zip((0, *cuts), cuts)), begun)
    wide = 2 * tile
    steps = pixels // wide

    def gate_of(zt, u):
        return pixel_call(
            functools.partial(gate_kernel, u), [(zt, 0, steps)], fixed, (channels,),
            steps, wide, pixels * mult * channels,
        )[0]

    def exchange(array):
        there = lax.all_to_all(array.reshape(peers, -1, array.shape[1]), CUBE, 0, 0)
        return there.reshape(array.shape)

    gate = gate_of(zt, 0)
    triangle = exchange(triangle_call(exchange(sent), (0, 1), blocks, side, own, False))
    sent, zt = pixel_call(
        functools.partial(middle_kernel, peers),
        [(a, 0, steps // 2) for a in (triangle, zt, gate, mask)], fixed, (2 * width, channels),
        steps // 2, 2 * wide, pixels * mult * 5 * width,
    )
    gate = gate_of(zt, 1)
    received = exchange(sent)
    product = lambda piece: triangle_call(received, (piece,), blocks, side, own, True)

    def finish(piece, triangle):
        at = piece * steps // 2
        return pixel_call(
            last_kernel,
            [(triangle, 0, steps // 2), (zt, at, steps), (gate, at, steps)],
            fixed, (channels,), steps // 2, wide, pixels // 2 * mult * channels, row_major_out=True,
        )[0]

    there = finish(1, exchange(product(1)))
    beside, across = (
        lax.ppermute(there, LINE, pairs) for pairs in (((0, 1), (3, 2)), ((1, 2), (2, 1)))
    )
    there, waiting = lax.optimization_barrier((there, product(0)))
    here = finish(0, exchange(waiting))
    back = lax.ppermute(here, LINE, ((1, 3), (2, 0)))
    return pl.pallas_call(
        assemble_kernel,
        in_specs=[pl.BlockSpec(memory_space=pl.ANY)] * 4,
        out_specs=pl.BlockSpec(memory_space=pl.ANY),
        out_shape=pltpu.HBM((2, *here.shape), here.dtype),
        scratch_shapes=[
            pltpu.VMEM((2, *here.shape), here.dtype),
            pltpu.SemaphoreType.DMA((2, 2)),
            pltpu.SemaphoreType.DMA((2, 2)),
        ],
        compiler_params=pltpu.CompilerParams(vmem_limit_bytes=48 * 1024 * 1024),
    )(here, beside, back, across).reshape(side, side, channels)


def layer_norm(values, gain, bias, axis):
    average = jnp.mean(values, axis=axis, keepdims=True)
    centred = values - average
    spread_sq = jnp.mean(centred * centred, axis=axis, keepdims=True)
    return centred * lax.rsqrt(spread_sq + 1e-05) * gain + bias


def triangle_update(
    pair_act,
    mask_float,
    layer_index,
    input_gain,
    input_bias,
    project_weight,
    gate_weight,
    output_gain,
    output_bias,
    output_weight,
    incoming,
):
    rows, cols = lax.axis_size("row"), lax.axis_size("col")
    peers = rows * cols
    rows_here, cols_here, channels_here = pair_act.shape
    width = output_weight.shape[1]
    own = width // peers
    pixels = rows_here * cols_here
    pair_float = pair_act.astype(jnp.float32).reshape(pixels, channels_here)
    normed = layer_norm(
        pair_float, input_gain[layer_index], input_bias[layer_index], -1
    ).astype(jnp.bfloat16)
    projected = lax.dot_general(
        project_weight[layer_index],
        normed,
        (((0,), (1,)), ((), ())),
        preferred_element_type=jnp.float32,
    ).reshape(4, peers, own, pixels)
    mask_row = mask_float.reshape(1, 1, pixels)
    left_proj = (jax.nn.sigmoid(projected[0]) * projected[1] * mask_row).astype(jnp.bfloat16)
    right_proj = (jax.nn.sigmoid(projected[2]) * projected[3] * mask_row).astype(jnp.bfloat16)
    both = jnp.concatenate([left_proj, right_proj], axis=1)
    both = lax.all_to_all(both, GRID, 0, 0)
    both = both.reshape(rows, cols, 2, own, rows_here, cols_here)
    both = both.transpose(2, 3, 0, 4, 1, 5).reshape(2, own, rows * rows_here, cols * cols_here)
    spec = "cki,ckj->cij" if incoming else "cik,cjk->cij"
    triangle = jnp.einsum(spec, both[0], both[1], preferred_element_type=jnp.float32)
    triangle = triangle.astype(jnp.bfloat16).reshape(own, rows, rows_here, cols, cols_here)
    triangle = triangle.transpose(1, 3, 0, 2, 4).reshape(peers, own, pixels)
    triangle = lax.all_to_all(triangle, GRID, 0, 0).reshape(width, pixels)
    normed_sum = layer_norm(
        triangle.astype(jnp.float32),
        output_gain[layer_index][:, None],
        output_bias[layer_index][:, None],
        0,
    ).astype(jnp.bfloat16)
    gate_value = jax.nn.sigmoid(
        jnp.dot(normed, gate_weight[layer_index], preferred_element_type=jnp.float32)
    )
    mapped = lax.dot_general(
        normed_sum,
        output_weight[layer_index],
        (((0,), (0,)), ((), ())),
        preferred_element_type=jnp.float32,
    )
    return (
        (pair_float + gate_value * mapped)
        .astype(jnp.bfloat16)
        .reshape(rows_here, cols_here, channels_here)
    )


def shards(pair_act, pair_mask, *params):
    mask_float = pair_mask.astype(jnp.float32)
    for index in range(2):
        pair_act = triangle_update(pair_act, mask_float, index, *params, index == 1)
    return pair_act


def solution(mesh):
    def updates(pair_act, pair_mask, *params):
        body, grid, cols = shards, mesh, "col"
        if fits(mesh, pair_act.shape[1], params[-1].shape[1]):
            sizes = mesh.devices.shape
            grid = jax.sharding.Mesh(
                mesh.devices.reshape(*sizes[:2], 2, sizes[2] // 2), ("groups", "row", "zh", "zl")
            )
            body, cols = by_kernels, ("zh", "zl")
        pixels = (("groups", "row"), cols)
        return jax.shard_map(
            body,
            mesh=grid,
            in_specs=(P(*pixels, None), P(*pixels)) + (P(),) * 7,
            out_specs=P(*pixels, None),
            check_vma=False,
        )(pair_act, pair_mask, *params)

    return updates
```
